32 devices in a mesh: dp: 16 (over z, x, core), band: 2 (over y).
Axes of the slice: x: 2, y: 2, z: 4, core: 2. Of those that a mesh axis runs over, the one named last changes fastest.
Arguments:
- tokens: bfloat16 [16, 1024, 1152], P('dp', 'band'), may hold values from -6 to 6
- embedding: float32 [16, 1152], P('dp'), may hold values from -6 to 6
- heights: int32 [16], P('dp'), may hold values from 16 to 24, as said below
- widths: int32 [16], P('dp'), may hold values from 40 to 64, as said below
- cotangent: bfloat16 [16, 1024, 1152], P('dp', 'band'), may hold values from -6 to 6
- w_qkv: float32 [1152, 3456], P(('dp', 'band')), may hold values from -0.1875 to 0.1875
- w_proj: float32 [1152, 1152], P(('dp', 'band')), may hold values from -0.5 to 0.5
- w_fc1: float32 [1152, 4608], P(('dp', 'band')), may hold values from -1 to 1
- w_fc2: float32 [4608, 1152], P(('dp', 'band')), may hold values from -0.09375 to 0.09375
- w_ada: float32 [1152, 6912], P(('dp', 'band')), may hold values from -0.1875 to 0.1875
- biases: float32 [17280], P(('dp', 'band')), may hold values from -2 to 6
- m_qkv: float32 [1152, 3456], P(('dp', 'band')), may hold values from -3 to 3
- m_proj: float32 [1152, 1152], P(('dp', 'band')), may hold values from -3 to 3
- m_fc1: float32 [1152, 4608], P(('dp', 'band')), may hold values from -1 to 1
- m_fc2: float32 [4608, 1152], P(('dp', 'band')), may hold values from -3 to 3
- m_ada: float32 [1152, 6912], P(('dp', 'band')), may hold values from -3 to 3
- m_bias: float32 [17280], P(('dp', 'band')), may hold values from -3 to 3
- v_qkv: float32 [1152, 3456], P(('dp', 'band')), may hold values from 0.041831985 to 0.16732794
- v_proj: float32 [1152, 1152], P(('dp', 'band')), may hold values from 0.041831985 to 0.16732794
- v_fc1: float32 [1152, 4608], P(('dp', 'band')), may hold values from 0.0050198385 to 0.020079354
- v_fc2: float32 [4608, 1152], P(('dp', 'band')), may hold values from 0.041831985 to 0.16732794
- v_ada: float32 [1152, 6912], P(('dp', 'band')), may hold values from 0.041831985 to 0.16732794
- v_bias: float32 [17280], P(('dp', 'band')), may hold values from 0.041831985 to 0.16732794
Outputs:
- output: bfloat16 [16, 1024, 1152], P('dp', 'band')
- grad_tokens: bfloat16 [16, 1024, 1152], P('dp', 'band')
- grad_norm: float32 [], replicated
- new_qkv: float32 [1152, 3456], P(('dp', 'band'))
- new_proj: float32 [1152, 1152], P(('dp', 'band'))
- new_fc1: float32 [1152, 4608], P(('dp', 'band'))
- new_fc2: float32 [4608, 1152], P(('dp', 'band'))
- new_ada: float32 [1152, 6912], P(('dp', 'band'))
- new_bias: float32 [17280], P(('dp', 'band'))
- first_qkv: float32 [1152, 3456], P(('dp', 'band'))
- first_proj: float32 [1152, 1152], P(('dp', 'band'))
- first_fc1: float32 [1152, 4608], P(('dp', 'band'))
- first_fc2: float32 [4608, 1152], P(('dp', 'band'))
- first_ada: float32 [1152, 6912], P(('dp', 'band'))
- first_bias: float32 [17280], P(('dp', 'band'))
- second_qkv: float32 [1152, 3456], P(('dp', 'band'))
- second_proj: float32 [1152, 1152], P(('dp', 'band'))
- second_fc1: float32 [1152, 4608], P(('dp', 'band'))
- second_fc2: float32 [4608, 1152], P(('dp', 'band'))
- second_ada: float32 [1152, 6912], P(('dp', 'band'))
- second_bias: float32 [17280], P(('dp', 'band'))
The draws below stay inside these ranges and needn't reach their ends.
Inputs may be any that keep to these rules, and one draw needn't show every extreme that they name: `heights`: each image is 16 x 64 or 24 x 40 patches; its row count. `widths`: its column count, of the same shape as in heights.
All inputs are finite; a program needn't handle non-finite values.
Results may differ from the reference program's by a relative error of at most 0.019.
The reference program's roundings to bfloat16 on the way count: a program that leaves them out, or rounds other values in their place, can miss the bound.
Values may be sent and summed in bfloat16 or wider, within the bound.
No kernel may reach another device: no remote copies, remote signals or barrier semaphores. Data moves between devices by JAX's collectives and lax.ppermute only.
A program may use at most 384 MiB of HBM per device.

```python
import math
import jax
import jax.numpy as jnp
from jax import lax

D = 1152
HEADS = 16
HEAD_DIM = 72
FF = 4608
HA = 16
WA = 64
HB = 24
WB = 40
STEPS = 10
SEQ = 1024
IMAGES = 16
NBIAS = 17280
NPARAM = 23905152


def aspect_kinds(key):
    kinds = jax.random.randint(key, (IMAGES,), 0, 2)
    return kinds.at[0].set(0).at[1].set(1)


def draw_heights(key, part):
    kinds = aspect_kinds(key)
    return jnp.where(kinds == 0, HA, HB).astype(jnp.int32)


def draw_widths(key, part):
    kinds = aspect_kinds(key)
    return jnp.where(kinds == 0, WA, WB).astype(jnp.int32)


def draw_w_fc1(key, part):
    key = jax.random.fold_in(key, 13)
    common_key, noise_key = jax.random.split(key)
    common = jnp.clip(jax.random.normal(common_key, (FF,), jnp.float32), -4.0, 4.0)
    noise = jnp.clip(jax.random.normal(noise_key, (D, FF), jnp.float32), -4.0, 4.0)
    return (0.4 * common[None, :] + noise) * D ** (-0.5)


def draw_biases(key, part):
    key = jax.random.fold_in(key, 11)
    noise = jnp.clip(0.3 * jax.random.normal(key, (NBIAS,), jnp.float32), -1.5, 1.5)
    height_top = 2.0
    ramp = jnp.arange(D, dtype=jnp.float32) * (height_top / (D - 1))
    start = 5 * D + FF
    leading = jnp.zeros((start + D,), jnp.float32)
    between = jnp.zeros((2 * D,), jnp.float32)
    trailing = jnp.zeros((D,), jnp.float32)
    return noise + jnp.concatenate([leading, ramp, between, ramp, trailing])


def levels(own_key, extent, shards, smallest, top_value):
    gain, own = 1.0, jax.random.fold_in(own_key, 6)
    for position, parts in shards:
        steps = jnp.exp(jax.random.uniform(jax.random.fold_in(own, position), (parts,), jnp.float32, smallest / len(shards), top_value / len(shards)))
        gain = gain * jnp.repeat(steps, extent[position] // parts).reshape([-1 if axis == position else 1 for axis in range(len(extent))])
    return gain


def scatter_about(rng, shape, scale, limit, cuts=(), kind=jnp.bfloat16):
    values = scale * jax.random.normal(rng, shape, jnp.float32)
    if cuts:
        values = values * levels(rng, shape, cuts, -0.22, 0.18)
    return jnp.clip(values, -limit, limit).astype(kind)


def setup_inputs(seed: int = 0) -> dict:
    streams_of = jax.random.split(jax.random.key(seed), 24)
    tokens = scatter_about(streams_of[0], (IMAGES, SEQ, D), 1.0, 6.0, ((0, 16), (1, 2)))
    embedding = scatter_about(streams_of[1], (IMAGES, D), 1.0, 6.0, ((0, 16),), jnp.float32)
    heights = draw_heights(jax.random.fold_in(streams_of[23], 71), 0)
    widths = draw_widths(jax.random.fold_in(streams_of[23], 71), 0)
    cotangent = scatter_about(streams_of[4], (IMAGES, SEQ, D), 1.0, 6.0, ((0, 16), (1, 2)))
    w_qkv = scatter_about(streams_of[5], (D, 3 * D), D ** -0.5, 0.1875, ((0, 32),), jnp.float32)
    w_proj = scatter_about(streams_of[6], (D, D), (D // 8) ** -0.5, 0.5, ((0, 32),), jnp.float32)
    w_fc1 = draw_w_fc1(jax.random.fold_in(streams_of[23], 71), 0)
    w_fc2 = scatter_about(streams_of[8], (FF, D), FF ** -0.5, 0.09375, ((0, 32),), jnp.float32)
    w_ada = scatter_about(streams_of[9], (D, 6 * D), D ** -0.5, 0.1875, ((0, 32),), jnp.float32)
    biases = draw_biases(jax.random.fold_in(streams_of[23], 71), 0)
    m_qkv = scatter_about(streams_of[11], (D, 3 * D), (1000 * NPARAM ** -0.5), 3.0, ((0, 32),), jnp.float32)
    m_proj = scatter_about(streams_of[12], (D, D), (1000 * NPARAM ** -0.5), 3.0, ((0, 32),), jnp.float32)
    m_fc1 = scatter_about(streams_of[13], (D, FF), (350 * NPARAM ** -0.5), 1.0, ((0, 32),), jnp.float32)
    m_fc2 = scatter_about(streams_of[14], (FF, D), (1000 * NPARAM ** -0.5), 3.0, ((0, 32),), jnp.float32)
    m_ada = scatter_about(streams_of[15], (D, 6 * D), (1000 * NPARAM ** -0.5), 3.0, ((0, 32),), jnp.float32)
    m_bias = scatter_about(streams_of[16], (NBIAS,), (1000 * NPARAM ** -0.5), 3.0, ((0, 32),), jnp.float32)
    v_qkv = jnp.clip(jnp.exp(math.log(0.16732794) - 1.3862944 * jax.random.uniform(streams_of[17], (D, 3 * D), jnp.float32) ** levels(streams_of[17], (D, 3 * D), ((0, 32),), -0.2, 0.2)), 0.041831985, 0.16732794)
    v_proj = jnp.clip(jnp.exp(math.log(0.16732794) - 1.3862944 * jax.random.uniform(streams_of[18], (D, D), jnp.float32) ** levels(streams_of[18], (D, D), ((0, 32),), -0.2, 0.2)), 0.041831985, 0.16732794)
    v_fc1 = jnp.clip(jnp.exp(math.log(0.020079354) - 1.3862944 * jax.random.uniform(streams_of[19], (D, FF), jnp.float32) ** levels(streams_of[19], (D, FF), ((0, 32),), -0.2, 0.2)), 0.0050198385, 0.020079354)
    v_fc2 = jnp.clip(jnp.exp(math.log(0.16732794) - 1.3862944 * jax.random.uniform(streams_of[20], (FF, D), jnp.float32) ** levels(streams_of[20], (FF, D), ((0, 32),), -0.2, 0.2)), 0.041831985, 0.16732794)
    v_ada = jnp.clip(jnp.exp(math.log(0.16732794) - 1.3862944 * jax.random.uniform(streams_of[21], (D, 6 * D), jnp.float32) ** levels(streams_of[21], (D, 6 * D), ((0, 32),), -0.2, 0.2)), 0.041831985, 0.16732794)
    v_bias = jnp.clip(jnp.exp(math.log(0.16732794) - 1.3862944 * jax.random.uniform(streams_of[22], (NBIAS,), jnp.float32) ** levels(streams_of[22], (NBIAS,), ((0, 32),), -0.2, 0.2)), 0.041831985, 0.16732794)
    return {"tokens": tokens, "embedding": embedding, "heights": heights, "widths": widths, "cotangent": cotangent, "w_qkv": w_qkv, "w_proj": w_proj, "w_fc1": w_fc1, "w_fc2": w_fc2, "w_ada": w_ada, "biases": biases, "m_qkv": m_qkv, "m_proj": m_proj, "m_fc1": m_fc1, "m_fc2": m_fc2, "m_ada": m_ada, "m_bias": m_bias, "v_qkv": v_qkv, "v_proj": v_proj, "v_fc1": v_fc1, "v_fc2": v_fc2, "v_ada": v_ada, "v_bias": v_bias}


@jax.custom_vjp
def low(v):
    return lax.optimization_barrier(v.astype(jnp.bfloat16)).astype(jnp.float32)

@jax.custom_vjp
def low_back(v):
    return v

def low_keep(v):
    return (low(v), None)

def low_pass(kept, grad):
    return (grad,)

def back_keep(v):
    return (v, None)

def back_low(kept, grad):
    return (low(grad),)
low.defvjp(low_keep, low_pass)
low_back.defvjp(back_keep, back_low)
highest = lax.Precision.HIGHEST
clip_limit = 1000.0
learn_rate = 0.04
bias_rate = 0.25
beta_one = 0.5
beta_two = 0.5
weight_decay = 0.01

def matmul(left, right):
    return jnp.dot(left, right, precision=highest)

def layer_norm(values):
    centre = lax.optimization_barrier(jnp.mean(values, -1, keepdims=True))
    centered = values - centre
    spread = lax.optimization_barrier(jnp.mean(centered * centered, -1, keepdims=True))
    return centered * lax.rsqrt(spread + 1e-06)

def position_rows(slots, width):
    quarter = D // 4
    omega = 1.0 / 10000.0 ** (jnp.arange(quarter, dtype=jnp.float32) / quarter)
    rowpos = (slots // width).astype(jnp.float32)[..., None] * omega
    colpos = (slots % width).astype(jnp.float32)[..., None] * omega
    return jnp.concatenate([jnp.sin(rowpos), jnp.cos(rowpos), jnp.sin(colpos), jnp.cos(colpos)], -1)

def image_forward(params, x_in, cond, valid):
    w_qkv, w_proj, w_fc1, w_fc2, w_ada, biases = params
    bias_qkv = biases[:3 * D]
    bias_proj = biases[3 * D:4 * D]
    bias_fc1 = biases[4 * D:4 * D + FF]
    bias_fc2 = biases[4 * D + FF:5 * D + FF]
    bias_ada = biases[5 * D + FF:]
    modul = matmul(low(jax.nn.silu(cond))[None], low(w_ada))[0] + low(bias_ada)
    shift1, scale1, gate1, shift2, scale2, gate2 = [modul[j * D:(j + 1) * D] for j in range(6)]
    attn_in = low(layer_norm(x_in) * (1.0 + scale1) + shift1)
    qkv = low(low_back(matmul(attn_in, low(w_qkv)) + low(bias_qkv)))
    query = qkv[:, :D].reshape(SEQ, HEADS, HEAD_DIM)
    keys = qkv[:, D:2 * D].reshape(SEQ, HEADS, HEAD_DIM)
    values = qkv[:, 2 * D:].reshape(SEQ, HEADS, HEAD_DIM)
    scores = low_back(jnp.einsum('qhd,khd->hqk', query, keys, precision=highest) * HEAD_DIM ** (-0.5))
    scores = jnp.where(valid[None, None, :], scores, -1e+30)
    top = lax.optimization_barrier(jnp.max(scores, -1, keepdims=True))
    expo = jnp.exp(scores - top)
    probs = low(expo / lax.optimization_barrier(jnp.sum(expo, -1, keepdims=True)))
    mixed = jnp.einsum('hqk,khd->qhd', probs, values, precision=highest).reshape(SEQ, D)
    mixed = low(low_back(mixed))
    attn = low_back(matmul(mixed, low(w_proj)) + low(bias_proj))
    x_mid = x_in + gate1 * attn
    mlp_in = low(layer_norm(x_mid) * (1.0 + scale2) + shift2)
    hidden_pre = low_back(matmul(mlp_in, low(w_fc1)) + low(bias_fc1))
    hidden = low(jax.nn.gelu(hidden_pre, approximate=True))
    branch = low_back(matmul(hidden, low(w_fc2)) + low(bias_fc2))
    return x_mid + gate2 * branch

def adam_step(weight, first, second, grad, factor, rate):
    clipped = grad * factor
    first = beta_one * first + (1.0 - beta_one) * clipped
    second = beta_two * second + (1.0 - beta_two) * clipped * clipped
    first_hat = first / (1.0 - beta_one ** STEPS)
    second_hat = second / (1.0 - beta_two ** STEPS)
    update = first_hat / (jnp.sqrt(second_hat) + 1e-08) + weight_decay * weight
    return (weight - rate * update, first, second)

def reference(tokens, embedding, heights, widths, cotangent, w_qkv, w_proj, w_fc1, w_fc2, w_ada, biases, m_qkv, m_proj, m_fc1, m_fc2, m_ada, m_bias, v_qkv, v_proj, v_fc1, v_fc2, v_ada, v_bias):
    params = (w_qkv, w_proj, w_fc1, w_fc2, w_ada, biases)
    slots = jnp.arange(SEQ, dtype=jnp.int32)

    def per_image(carry, item):
        token_img, cond, height, width, cot_img = item
        valid = slots < height * width
        x_in = token_img.astype(jnp.float32) + position_rows(slots, width)

        def forward(par, xin):
            return image_forward(par, xin, cond, valid)
        result, pullback = jax.vjp(forward, params, x_in)
        grad_par, grad_x = pullback(cot_img.astype(jnp.float32) * valid[:, None].astype(jnp.float32))
        carry = jax.tree.map(lambda total, piece: total + piece, carry, grad_par)
        return (carry, (result.astype(jnp.bfloat16), grad_x.astype(jnp.bfloat16)))
    start = jax.tree.map(jnp.zeros_like, params)
    grads, (output, grad_tokens) = lax.scan(per_image, start, (tokens, embedding, heights, widths, cotangent))
    squares = sum((jnp.sum(piece * piece) for piece in grads))
    grad_norm = jnp.sqrt(squares)
    factor = jnp.minimum(1.0, clip_limit / grad_norm)
    firsts = (m_qkv, m_proj, m_fc1, m_fc2, m_ada, m_bias)
    seconds = (v_qkv, v_proj, v_fc1, v_fc2, v_ada, v_bias)
    rates = (learn_rate, learn_rate, learn_rate, learn_rate, learn_rate, bias_rate)
    results = [adam_step(params[j], firsts[j], seconds[j], grads[j], factor, rates[j]) for j in range(6)]
    new_w = [item[0] for item in results]
    new_m = [item[1] for item in results]
    new_v = [item[2] for item in results]
    return (output, grad_tokens, grad_norm, new_w[0], new_w[1], new_w[2], new_w[3], new_w[4], new_w[5], new_m[0], new_m[1], new_m[2], new_m[3], new_m[4], new_m[5], new_v[0], new_v[1], new_v[2], new_v[3], new_v[4], new_v[5])
```

```python
import functools
import math

import jax
import jax.numpy as jnp
from jax import lax
from jax.experimental import pallas as pl
from jax.experimental.pallas import tpu as pltpu
from jax.sharding import PartitionSpec as P

D = 1152
HEADS = 16
HEAD_DIM = 72
FF = 4608
STEPS = 10
OWN_HEADS = HEADS // 2
OWN_FF = FF // 2
AXES = ("dp", "band")

clip_limit = 1000.0
learn_rate = 0.04
bias_rate = 0.25
beta_one = 0.5
beta_two = 0.5
weight_decay = 0.01

bf16 = jnp.bfloat16
f32 = jnp.float32
VMEM_LIMIT = 56 * 1024 * 1024
SCALE = HEAD_DIM ** (-0.5)
SCALE2 = SCALE * math.log2(math.e)


def normalize(values):
    centre = jnp.mean(values, -1, keepdims=True)
    centered = values - centre
    spread = lax.rsqrt(jnp.mean(centered * centered, -1, keepdims=True) + 1e-06)
    return (centered * spread, spread)


def norm_back(normed, spread, grad):
    return spread * (
        grad
        - jnp.mean(grad, -1, keepdims=True)
        - normed * jnp.mean(grad * normed, -1, keepdims=True)
    )


def gelu_tanh(values):
    return jax.nn.gelu(values, approximate=True)


def position_rows(slots, width):
    quarter = D // 4
    omega = 1.0 / 10000.0 ** (jnp.arange(quarter, dtype=f32) / quarter)
    rowpos = (slots // width).astype(f32)[..., None] * omega
    colpos = (slots % width).astype(f32)[..., None] * omega
    return jnp.concatenate([jnp.sin(rowpos), jnp.cos(rowpos), jnp.sin(colpos), jnp.cos(colpos)], -1)


def adam_step(weight, first, second, grad, factor, rate):
    clipped = grad * factor
    first = beta_one * first + (1.0 - beta_one) * clipped
    second = beta_two * second + (1.0 - beta_two) * clipped * clipped
    first_hat = first / (1.0 - beta_one**STEPS)
    second_hat = second / (1.0 - beta_two**STEPS)
    update = first_hat / (jnp.sqrt(second_hat) + 1e-08) + weight_decay * weight
    return (weight - rate * update, first, second)


def dot(left, right, over):
    return lax.dot_general(left, right, (over, ((), ())), preferred_element_type=f32)


def attend_kernel(mask_ref, qkv_ref, mixed_ref, logsum_ref, score_ref):
    seq = qkv_ref.shape[-1]
    half = seq // 2
    step = 512
    keys = qkv_ref[1, 0].T
    values = qkv_ref[2, 0]
    for start in range(0, seq, step):
        query = qkv_ref[0, 0, :, start : start + step]
        score_ref[...] = dot(keys, query, ((1,), (0,)))
        score_ref[half - 64 : half, :] += mask_ref[0]
        score_ref[seq - 64 :, :] += mask_ref[1]
        scores = score_ref[...]
        top = jnp.max(scores, 0, keepdims=True)
        expo = jnp.exp2((scores - top) * SCALE2)
        total = jnp.sum(expo, 0, keepdims=True)
        probs = (expo * (1.0 / total)).astype(bf16)
        mixed = dot(values, probs, ((1,), (0,)))
        mixed_ref[0, :, start : start + step] = mixed.astype(bf16)
        logsum_ref[0, :, start : start + step] = top * SCALE2 + jnp.log2(total)


def attend(qkv, mask):
    heads, seq = qkv.shape[1], qkv.shape[3]
    pairs = heads * seq * seq
    return pl.pallas_call(
        attend_kernel,
        grid=(heads,),
        in_specs=[
            pl.BlockSpec(memory_space=pltpu.SMEM),
            pl.BlockSpec((3, 1, HEAD_DIM, seq), lambda h: (0, h, 0, 0)),
        ],
        out_specs=[
            pl.BlockSpec((1, HEAD_DIM, seq), lambda h: (h, 0, 0)),
            pl.BlockSpec((1, 1, seq), lambda h: (h, 0, 0)),
        ],
        out_shape=[
            jax.ShapeDtypeStruct((heads, HEAD_DIM, seq), bf16),
            jax.ShapeDtypeStruct((heads, 1, seq), f32),
        ],
        scratch_shapes=[pltpu.VMEM((seq, 512), f32)],
        compiler_params=pltpu.CompilerParams(vmem_limit_bytes=VMEM_LIMIT),
        cost_estimate=pl.CostEstimate(
            flops=4 * pairs * 256, bytes_accessed=8 * heads * seq * HEAD_DIM, transcendentals=pairs
        ),
        name="attend",
    )(mask, qkv)


def attend_back_kernel(mask_ref, qkv_ref, logsum_ref, dmix_ref, out_ref, score_ref, dk_ref, dv_ref):
    seq = qkv_ref.shape[-1]
    half = seq // 2
    step = 512
    keys_t = qkv_ref[1, 0]
    keys = keys_t.T
    values = qkv_ref[2, 0].T
    for start in range(0, seq, step):
        query = qkv_ref[0, 0, :, start : start + step]
        dmix = dmix_ref[0, :, start : start + step]
        score_ref[...] = dot(keys, query, ((1,), (0,)))
        score_ref[half - 64 : half, :] += mask_ref[0]
        score_ref[seq - 64 :, :] += mask_ref[1]
        probs = jnp.exp2(score_ref[...] * SCALE2 - logsum_ref[0, :, start : start + step])
        dprobs = dot(values, dmix, ((1,), (0,)))
        prod = probs * dprobs
        delta = jnp.sum(prod, 0, keepdims=True)
        dscore = (prod - probs * delta).astype(bf16)
        probs_low = probs.astype(bf16)
        out_ref[0, 0, :, start : start + step] = (
            dot(keys_t, dscore, ((1,), (0,))) * SCALE
        ).astype(bf16)
        dk = dot(query, dscore, ((1,), (1,)))
        dv = dot(dmix, probs_low, ((1,), (1,)))
        if start == 0:
            dk_ref[...] = dk
            dv_ref[...] = dv
        else:
            dk_ref[...] += dk
            dv_ref[...] += dv
    out_ref[1, 0] = (dk_ref[...] * SCALE).astype(bf16)
    out_ref[2, 0] = dv_ref[...].astype(bf16)


def attend_back(qkv, logsum, dmix, mask):
    heads, seq = qkv.shape[1], qkv.shape[3]
    pairs = heads * seq * seq
    block = pl.BlockSpec((3, 1, HEAD_DIM, seq), lambda h: (0, h, 0, 0))
    return pl.pallas_call(
        attend_back_kernel,
        grid=(heads,),
        in_specs=[
            pl.BlockSpec(memory_space=pltpu.SMEM),
            block,
            pl.BlockSpec((1, 1, seq), lambda h: (h, 0, 0)),
            pl.BlockSpec((1, HEAD_DIM, seq), lambda h: (h, 0, 0)),
        ],
        out_specs=block,
        out_shape=jax.ShapeDtypeStruct(qkv.shape, bf16),
        scratch_shapes=[
            pltpu.VMEM((seq, 512), f32),
            pltpu.VMEM((HEAD_DIM, seq), f32),
            pltpu.VMEM((HEAD_DIM, seq), f32),
        ],
        compiler_params=pltpu.CompilerParams(vmem_limit_bytes=VMEM_LIMIT),
        cost_estimate=pl.CostEstimate(
            flops=10 * pairs * 256, bytes_accessed=14 * heads * seq * HEAD_DIM, transcendentals=pairs
        ),
        name="attend_back",
    )(mask, qkv, logsum, dmix)


def place_kernel(plan, count, where_ref, *refs):
    pieces, out_ref, sem = refs[:count], refs[count], refs[count + 1]
    zi, xi, yi = where_ref[0], where_ref[1], where_ref[2]
    copies = []
    for number, (piece, index, dz, dx, dy) in enumerate(plan):
        source = pieces[piece]
        for i in index:
            source = source.at[i]
        target = out_ref.at[zi ^ dz, xi ^ dx, yi ^ dy]
        copies.append(pltpu.make_async_copy(source, target, sem.at[number]))
    for copy in copies:
        copy.start()
    for copy in copies:
        copy.wait()


def place(where, pieces, plan, nz):
    rows, columns = pieces[0].shape[-2:]
    return pl.pallas_call(
        functools.partial(place_kernel, tuple(plan), len(pieces)),
        in_specs=[pl.BlockSpec(memory_space=pltpu.SMEM)]
        + [pl.BlockSpec(memory_space=pl.ANY)] * len(pieces),
        out_specs=pl.BlockSpec(memory_space=pltpu.VMEM),
        out_shape=jax.ShapeDtypeStruct((nz, 2, 2, rows, columns), pieces[0].dtype),
        scratch_shapes=[pltpu.SemaphoreType.DMA((len(plan),))],
        compiler_params=pltpu.CompilerParams(vmem_limit_bytes=VMEM_LIMIT),
        cost_estimate=pl.CostEstimate(
            flops=0, bytes_accessed=16 * nz * rows * columns, transcendentals=0
        ),
        name="place",
    )(where, *pieces)


class Group:
    def __init__(self, n):
        self.n = n
        self.nz = n // 8
        self.me = lax.axis_index(AXES).astype(jnp.int32)
        self.y = self.me & 1
        self.c = (self.me >> 1) & 1
        self.x = (self.me >> 2) & 1
        self.z = self.me >> 3
        self.where = jnp.stack([self.z, self.x, self.y])

    def xor(self, value, mask):
        return lax.ppermute(value, AXES, [(i, i ^ mask) for i in range(self.n)])

    def core(self, value):
        return self.xor(value, 2)

    def turn(self, value):
        return lax.ppermute(
            value,
            AXES,
            [(i, (i & ~3) | ((i & 1) << 1) | ((i >> 1) & 1)) for i in range(self.n)],
        )

    def turn_other(self, value):
        return lax.ppermute(
            value,
            AXES,
            [(i, (i & ~3) | ((1 - (i & 1)) << 1) | ((i >> 1) & 1)) for i in range(self.n)],
        )

    def turn_other_back(self, value):
        return lax.ppermute(
            value,
            AXES,
            [(i, (i & ~3) | ((i & 1) << 1) | (1 - ((i >> 1) & 1))) for i in range(self.n)],
        )

    def to_block(self, parts):
        mine = lax.dynamic_index_in_dim(parts, self.y, 0, False)
        other = lax.dynamic_index_in_dim(parts, 1 - self.y, 0, False)
        got_a, got_b = self.turn(mine), self.turn_other(other)
        straight = self.c == 0
        return jnp.concatenate(
            [jnp.where(straight, got_a, got_b), jnp.where(straight, got_b, got_a)], 0
        )

    def from_block(self, block):
        rows = block.shape[0] // 2
        pieces = block.reshape(2, rows, block.shape[1])
        got_a = self.turn(lax.dynamic_index_in_dim(pieces, self.c, 0, False))
        got_b = self.turn_other_back(lax.dynamic_index_in_dim(pieces, 1 - self.c, 0, False))
        straight = self.y == 0
        return jnp.stack(
            [jnp.where(straight, got_a, got_b), jnp.where(straight, got_b, got_a)], 0
        )

    def gather(self, block):
        nz, half = self.nz, self.nz // 2
        pieces = [block] + [self.xor(block, d << 3) for d in range(1, nz)]
        low, high = jnp.stack(pieces[:half]), jnp.stack(pieces[half:])
        low_y = self.xor(low, 1)
        high_x = self.xor(high, 4)
        low_x = self.xor(jnp.stack([low, low_y]), 4)
        high_y = self.xor(jnp.stack([high, high_x]), 1)
        plan = []
        for k in range(half):
            plan.append((0, (k,), k, 0, 0))
            plan.append((1, (k,), half + k, 0, 0))
            plan.append((2, (k,), k, 0, 1))
            plan.append((3, (k,), half + k, 1, 0))
            for other in range(2):
                plan.append((4, (other, k), k, 1, other))
                plan.append((5, (other, k), half + k, other, 1))
        return place(self.where, [low, high, low_y, high_x, low_x, high_y], plan, nz)

    def scatter(self, grads):
        nz, half = self.nz, self.nz // 2
        low, high = grads[:half], grads[half:]

        def pick(value, index, axis):
            return lax.dynamic_index_in_dim(value, index, axis, False)

        got_x = self.xor(pick(low, 1 - self.x, 1), 4)
        got_y = self.xor(pick(high, 1 - self.y, 2), 1)
        sum_x = pick(low, self.x, 1).astype(f32) + got_x.astype(f32)
        sum_y = pick(high, self.y, 2).astype(f32) + got_y.astype(f32)
        got_xy = self.xor(pick(sum_x, 1 - self.y, 1).astype(bf16), 1)
        got_yx = self.xor(pick(sum_y, 1 - self.x, 1).astype(bf16), 4)
        own_low = pick(sum_x, self.y, 1) + got_xy.astype(f32)
        own_high = pick(sum_y, self.x, 1) + got_yx.astype(f32)
        own = jnp.concatenate([own_low, own_high], 0)
        total = pick(own, self.z, 0)
        low_own = own.astype(bf16)
        for d in range(1, nz):
            total = total + self.xor(pick(low_own, self.z ^ d, 0), d << 3).astype(f32)
        return total

    def all_sum(self, value):
        mask = 2
        while mask:
            value = value + self.xor(value, mask)
            mask = {2: 1, 1: 4}.get(mask, mask * 2)
            if mask >= self.n:
                mask = 0
        return value


def per_device(
    tokens,
    embedding,
    heights,
    widths,
    cotangent,
    w_qkv,
    w_proj,
    w_fc1,
    w_fc2,
    w_ada,
    biases,
    m_qkv,
    m_proj,
    m_fc1,
    m_fc2,
    m_ada,
    m_bias,
    v_qkv,
    v_proj,
    v_fc1,
    v_fc2,
    v_ada,
    v_bias,
):
    rows = tokens.shape[1]
    n = lax.axis_size("dp") * lax.axis_size("band")
    own_rows = w_qkv.shape[0]
    g = Group(n)
    nz = g.nz
    groups = n // 4
    pair = 2 * own_rows
    ff_pair = 2 * w_fc2.shape[0]
    bias_rows = biases.shape[0]

    qkv_parts = (
        w_qkv.astype(bf16)
        .reshape(own_rows, 3, OWN_HEADS, 2, HEAD_DIM)
        .transpose(3, 0, 1, 2, 4)
        .reshape(2, own_rows, 3 * OWN_HEADS * HEAD_DIM)
    )
    qkv_w = g.gather(g.to_block(qkv_parts)).reshape(D, 3 * OWN_HEADS * HEAD_DIM)
    tokens_here = g.turn(tokens[0])
    cond_row = jax.nn.silu(embedding[0]).astype(bf16)
    small = jnp.concatenate(
        [
            cond_row,
            biases.astype(bf16),
            heights.astype(bf16),
            widths.astype(bf16),
        ]
    )
    small_size = -(-small.shape[0] // 128) * 128
    small = jnp.pad(small, (0, small_size - small.shape[0]))[None]
    quad = jnp.stack([small, g.xor(small, 1), g.xor(small, 2), g.xor(small, 3)])
    eight = jnp.concatenate([quad, g.xor(quad, 4)], 0)
    every = jnp.concatenate([eight] + [g.xor(eight, d << 3) for d in range(1, nz)], 0)
    every = every.reshape(n, small_size)
    spread = (jnp.arange(n)[:, None] == (jnp.arange(n)[None, :] ^ g.me)).astype(bf16)
    natural = dot(spread, every, ((1,), (0,)))
    bias_full = natural[:, D : D + bias_rows].reshape(-1)
    bias_qkv = bias_full[: 3 * D]
    bias_proj = bias_full[3 * D : 4 * D]
    bias_fc1 = bias_full[4 * D : 4 * D + FF]
    bias_fc2 = bias_full[4 * D + FF : 5 * D + FF]
    bias_ada = bias_full[5 * D + FF :]
    image_row = lax.dynamic_index_in_dim(natural, (g.me & ~3) | (g.y << 1), 0, False)
    height = image_row[D + bias_rows].astype(jnp.int32)
    width = image_row[D + bias_rows + 1].astype(jnp.int32)
    conds = every[:, :D].reshape(nz, 2, 2, 2, D)[:, :, :, 0]
    conds = jnp.where(g.c == g.y, conds, conds[:, :, ::-1])
    conds_own = lax.dynamic_slice_in_dim(
        conds.reshape(groups * 2, D), g.me * own_rows, own_rows, 1
    )
    mod_part = dot(conds_own, w_ada.astype(bf16), ((1,), (0,))).reshape(nz, 2, 2, 6 * D)
    mod_x = mod_part[:, 0] + g.xor(mod_part[:, 1], 4)
    mod_y = mod_x[:, 0] + g.xor(mod_x[:, 1], 1)
    mod_z = mod_y[0:1]
    for d in range(1, nz):
        mod_z = mod_z + g.xor(mod_y[d : d + 1], d << 3)
    modul = mod_z + g.core(mod_z) + bias_ada
    shift1, scale1, gate1, shift2, scale2, gate2 = [
        modul[:, j * D : (j + 1) * D] for j in range(6)
    ]

    proj_own = g.gather(w_proj.astype(bf16))
    heads_match = pair % HEAD_DIM == 0
    if heads_match:
        proj_w = proj_own.reshape(OWN_HEADS * HEAD_DIM, D)
    else:
        mine = proj_own.reshape(groups, pair, D)
        theirs = g.core(mine)
        first = g.c == 0
        whole = jnp.stack(
            [jnp.where(first, mine, theirs), jnp.where(first, theirs, mine)], 1
        ).reshape(OWN_HEADS, 2, HEAD_DIM, D)
        proj_w = lax.dynamic_index_in_dim(whole, g.c, 1, False).reshape(OWN_HEADS * HEAD_DIM, D)
    fc1_parts = (
        w_fc1.astype(bf16)
        .reshape(own_rows, groups, 2, ff_pair)
        .transpose(2, 0, 1, 3)
        .reshape(2, own_rows, OWN_FF)
    )
    fc1_w = g.gather(g.to_block(fc1_parts)).reshape(D, OWN_FF)
    fc2_w = g.gather(w_fc2.astype(bf16)).reshape(OWN_FF, D)
    cotangent_here = g.turn(cotangent[0])

    slots = g.c * rows + jnp.arange(rows, dtype=jnp.int32)
    count = height * width
    valid_rows = (slots < count).astype(f32)[:, None]
    seq = 2 * rows
    cut = jnp.where(count < seq, -1e30, 0.0).astype(f32)
    mask = jnp.stack([jnp.where(g.c == 1, cut, 0.0), jnp.where(g.c == 0, cut, 0.0)])
    x_in = tokens_here.astype(f32) + position_rows(slots, width)
    normed1, spread1 = normalize(x_in)
    attn_in = (normed1 * (1.0 + scale1) + shift1).astype(bf16)
    attn_all = jnp.concatenate([attn_in, g.core(attn_in)], 0)
    own_bias_qkv = lax.dynamic_index_in_dim(
        bias_qkv.reshape(3 * OWN_HEADS, 2, HEAD_DIM), g.c, 1, False
    ).reshape(-1, 1)
    qkv = (dot(qkv_w, attn_all, ((0,), (1,))) + own_bias_qkv).astype(bf16)
    qkv = qkv.reshape(3, OWN_HEADS, HEAD_DIM, seq)
    mixed, logsum = attend(qkv, mask)
    mixed = mixed.reshape(OWN_HEADS * HEAD_DIM, seq)
    attn_sib = dot(mixed[:, rows:], proj_w, ((0,), (0,)))
    attn = dot(mixed[:, :rows], proj_w, ((0,), (0,))) + g.core(attn_sib) + bias_proj
    x_mid = x_in + gate1 * attn
    normed2, spread2 = normalize(x_mid)
    mlp_in = (normed2 * (1.0 + scale2) + shift2).astype(bf16)
    mlp_all = jnp.concatenate([mlp_in, g.core(mlp_in)], 0)
    own_bias_fc1 = lax.dynamic_index_in_dim(
        bias_fc1.reshape(groups, 2, ff_pair), g.c, 1, False
    ).reshape(-1)
    hidden_pre = dot(mlp_all, fc1_w, ((1,), (0,))) + own_bias_fc1
    hidden = gelu_tanh(hidden_pre).astype(bf16)
    d_out = cotangent_here.astype(f32) * valid_rows
    d_branch = (gate2 * d_out).astype(bf16)
    branch_all = jnp.concatenate([d_branch, g.core(d_branch)], 0)
    g_fc2 = dot(hidden, branch_all, ((0,), (0,))).astype(bf16)
    red_fc2 = g.scatter(g_fc2.reshape(nz, 2, 2, -1, D))
    branch_sib = dot(hidden[rows:], fc2_w, ((1,), (0,)))
    branch = dot(hidden[:rows], fc2_w, ((1,), (0,))) + g.core(branch_sib) + bias_fc2
    output = g.turn((x_mid + gate2 * branch).astype(bf16))[None]
    d_gate2 = jnp.sum(d_out * branch, 0)
    gb_fc2 = jnp.sum(d_branch.astype(f32), 0)
    d_hidden = dot(branch_all, fc2_w, ((1,), (1,)))
    gelu_value, gelu_pull = jax.vjp(gelu_tanh, hidden_pre)
    d_pre = gelu_pull(d_hidden)[0].astype(bf16)
    g_fc1 = dot(mlp_all, d_pre, ((0,), (0,))).astype(bf16)
    red_fc1 = g.scatter(g_fc1.reshape(nz, 2, 2, -1, OWN_FF))
    gb_fc1 = jnp.sum(d_pre.astype(f32), 0)
    d_mlp_sib = dot(d_pre[rows:], fc1_w, ((1,), (1,)))
    d_mlp_in = dot(d_pre[:rows], fc1_w, ((1,), (1,))) + g.core(d_mlp_sib)
    d_scale2 = jnp.sum(d_mlp_in * normed2, 0)
    d_shift2 = jnp.sum(d_mlp_in, 0)
    d_mid = d_out + norm_back(normed2, spread2, d_mlp_in * (1.0 + scale2))
    d_attn = (gate1 * d_mid).astype(bf16)
    d_gate1 = jnp.sum(d_mid * attn, 0)
    gb_proj = jnp.sum(d_attn.astype(f32), 0)
    d_attn_all = jnp.concatenate([d_attn, g.core(d_attn)], 0)
    d_mixed = dot(proj_w, d_attn_all, ((1,), (1,))).astype(bf16)
    g_proj = dot(mixed, d_attn_all, ((1,), (0,))).astype(bf16)
    if heads_match:
        g_proj = g_proj.reshape(nz, 2, 2, -1, D)
    else:
        own = (jnp.arange(2) == g.c)[None, :, None, None]
        whole = jnp.where(own, g_proj.reshape(OWN_HEADS, 1, HEAD_DIM, D), 0).reshape(
            groups, 2, pair, D
        )
        theirs = g.core(lax.dynamic_index_in_dim(whole, 1 - g.c, 1, False))
        mine = lax.dynamic_index_in_dim(whole, g.c, 1, False)
        g_proj = (mine.astype(f32) + theirs.astype(f32)).astype(bf16).reshape(nz, 2, 2, -1, D)
    red_proj = g.scatter(g_proj)
    d_qkv = attend_back(qkv, logsum, d_mixed.reshape(OWN_HEADS, HEAD_DIM, seq), mask)
    d_qkv = d_qkv.reshape(3 * OWN_HEADS * HEAD_DIM, seq)
    g_qkv = dot(attn_all, d_qkv, ((0,), (1,))).astype(bf16)
    red_qkv = g.scatter(g_qkv.reshape(nz, 2, 2, -1, 3 * OWN_HEADS * HEAD_DIM))
    gb_qkv = jnp.sum(d_qkv.astype(f32), 1)
    d_attn_sib = dot(d_qkv[:, rows:], qkv_w, ((0,), (1,)))
    d_attn_in = dot(d_qkv[:, :rows], qkv_w, ((0,), (1,))) + g.core(d_attn_sib)
    d_scale1 = jnp.sum(d_attn_in * normed1, 0)
    d_shift1 = jnp.sum(d_attn_in, 0)
    grad_tokens = (d_mid + norm_back(normed1, spread1, d_attn_in * (1.0 + scale1))).astype(bf16)
    grad_tokens = g.turn(grad_tokens)[None]

    d_modul = jnp.concatenate([d_shift1, d_scale1, d_gate1, d_shift2, d_scale2, d_gate2])
    own = (jnp.arange(2) == g.c)[None, :, None]
    gb_qkv = jnp.where(own, gb_qkv.reshape(3 * OWN_HEADS, 1, HEAD_DIM), 0.0).reshape(-1)
    gb_fc1 = jnp.where(own, gb_fc1.reshape(groups, 1, ff_pair), 0.0).reshape(-1)
    vector = jnp.concatenate([gb_qkv, gb_proj, gb_fc1, gb_fc2, d_modul])[None]
    vector = vector + g.core(vector)
    plain = vector.shape[1] - 6 * D
    sums, mods = vector[:, :plain], vector[:, plain:]
    others = [g.xor(vector, d << 3) for d in range(1, nz)]
    for item in others:
        sums = sums + item[:, :plain]
    mods = jnp.concatenate([mods] + [item[:, plain:] for item in others], 0)[:, None]
    for mask_bit in (1, 4):
        packed = jnp.concatenate([sums.reshape(-1), mods.reshape(-1)])[None]
        packed = g.xor(packed, mask_bit)[0]
        sums = sums + packed[:plain]
        mods = jnp.stack([mods, packed[plain:].reshape(mods.shape)], 1)
    mods = mods.reshape(groups * 2, 6 * D)
    red_ada = lax.dot_general(
        conds_own.astype(f32),
        mods,
        (((0,), (0,)), ((), ())),
        precision=lax.Precision.HIGHEST,
        preferred_element_type=f32,
    )
    g_bias = jnp.concatenate([sums[0], jnp.sum(mods, 0)])
    red_bias = lax.dynamic_slice_in_dim(g_bias, g.me * bias_rows, bias_rows)

    red_qkv = (
        g.from_block(red_qkv)
        .reshape(2, own_rows, 3, OWN_HEADS, HEAD_DIM)
        .transpose(1, 2, 3, 0, 4)
        .reshape(own_rows, 3 * D)
    )
    red_fc1 = (
        g.from_block(red_fc1)
        .reshape(2, own_rows, groups, ff_pair)
        .transpose(1, 2, 0, 3)
        .reshape(own_rows, FF)
    )
    reduced = (red_qkv, red_proj, red_fc1, red_fc2, red_ada, red_bias)
    squares = sum((jnp.sum(piece * piece) for piece in reduced))
    squares = g.all_sum(jnp.broadcast_to(squares, (1, 128)))[0, 0]
    grad_norm = jnp.sqrt(squares)
    factor = jnp.minimum(1.0, clip_limit / grad_norm)
    params = (w_qkv, w_proj, w_fc1, w_fc2, w_ada, biases)
    firsts = (m_qkv, m_proj, m_fc1, m_fc2, m_ada, m_bias)
    seconds = (v_qkv, v_proj, v_fc1, v_fc2, v_ada, v_bias)
    rates = (learn_rate, learn_rate, learn_rate, learn_rate, learn_rate, bias_rate)
    results = [
        adam_step(params[j], firsts[j], seconds[j], reduced[j], factor, rates[j]) for j in range(6)
    ]
    return (
        output,
        grad_tokens,
        grad_norm,
        *[item[0] for item in results],
        *[item[1] for item in results],
        *[item[2] for item in results],
    )


def solution(mesh):
    state = (P(AXES, None),) * 5 + (P(AXES),)
    return jax.shard_map(
        per_device,
        mesh=mesh,
        in_specs=(
            P("dp", "band", None),
            P("dp", None),
            P("dp"),
            P("dp"),
            P("dp", "band", None),
            *state,
            *state,
            *state,
        ),
        out_specs=(
            P("dp", "band", None),
            P("dp", "band", None),
            P(),
            *state,
            *state,
            *state,
        ),
        check_vma=False,
    )
```

```python
import functools
import math

import jax
import jax.numpy as jnp
from jax import lax
from jax.experimental import pallas as pl
from jax.experimental.pallas import tpu as pltpu
from jax.sharding import PartitionSpec as P

D = 1152
HEADS = 16
HEAD_DIM = 72
FF = 4608
STEPS = 10
OWN_HEADS = HEADS // 2
OWN_FF = FF // 2
QKV = 3 * OWN_HEADS * HEAD_DIM
HALF = OWN_HEADS // 2
AXES = ("z", "x", "core", "y")

clip_limit = 1000.0
learn_rate = 0.04
bias_rate = 0.25
beta_one = 0.5
beta_two = 0.5
weight_decay = 0.01

bf16 = jnp.bfloat16
f32 = jnp.float32
VMEM_LIMIT = 56 * 1024 * 1024
LIGHT = pl.CostEstimate(flops=1, bytes_accessed=1, transcendentals=0)
SCALE = HEAD_DIM ** (-0.5)
SCALE2 = SCALE * math.log2(math.e)


def normalize(values):
    centre = jnp.mean(values, -1, keepdims=True)
    centered = values - centre
    spread = lax.rsqrt(jnp.mean(centered * centered, -1, keepdims=True) + 1e-06)
    return (centered * spread, spread)


def norm_back(normed, spread, grad):
    return spread * (
        grad
        - jnp.mean(grad, -1, keepdims=True)
        - normed * jnp.mean(grad * normed, -1, keepdims=True)
    )


def gelu_tanh(values):
    return jax.nn.gelu(values, approximate=True)


def position_rows(slots, width):
    quarter = D // 4
    omega = 1.0 / 10000.0 ** (jnp.arange(quarter, dtype=f32) / quarter)
    rowpos = (slots // width).astype(f32)[..., None] * omega
    colpos = (slots % width).astype(f32)[..., None] * omega
    return jnp.concatenate([jnp.sin(rowpos), jnp.cos(rowpos), jnp.sin(colpos), jnp.cos(colpos)], -1)


def adam_step(weight, first, second, grad, factor, rate):
    clipped = grad * factor
    first = beta_one * first + (1.0 - beta_one) * clipped
    second = beta_two * second + (1.0 - beta_two) * clipped * clipped
    first_hat = first / (1.0 - beta_one**STEPS)
    second_hat = second / (1.0 - beta_two**STEPS)
    update = first_hat / (jnp.sqrt(second_hat) + 1e-08) + weight_decay * weight
    return (weight - rate * update, first, second)


def dot(left, right, over):
    return lax.dot_general(left, right, (over, ((), ())), preferred_element_type=f32)


def attend_kernel(deps, mask_ref, qkv_ref, *refs):
    mixed_ref, logsum_ref, score_ref = refs[deps:]
    seq = qkv_ref.shape[-1]
    half = seq // 2
    step = 512
    keys = qkv_ref[0, 1, 0].T
    values = qkv_ref[0, 2, 0]
    for start in range(0, seq, step):
        query = qkv_ref[0, 0, 0, :, start : start + step]
        score_ref[...] = dot(keys, query, ((1,), (0,)))
        score_ref[half - 64 : half, :] += mask_ref[0]
        score_ref[seq - 64 :, :] += mask_ref[1]
        scores = score_ref[...]
        top = jnp.max(scores, 0, keepdims=True)
        expo = jnp.exp2((scores - top) * SCALE2)
        total = jnp.sum(expo, 0, keepdims=True)
        probs = (expo * (1.0 / total)).astype(bf16)
        mixed = dot(values, probs, ((1,), (0,)))
        mixed_ref[0, :, start : start + step] = mixed.astype(bf16)
        logsum_ref[0, :, start : start + step] = top * SCALE2 + jnp.log2(total)


def attend(part, qkv, mask, earlier=(), deps=()):
    heads, seq = qkv.shape[2], qkv.shape[4]
    pairs = heads * seq * seq
    anywhere = pl.BlockSpec(memory_space=pl.ANY)
    return pl.pallas_call(
        functools.partial(attend_kernel, len(earlier) + len(deps)),
        grid=(heads,),
        in_specs=[
            pl.BlockSpec(memory_space=pltpu.SMEM),
            pl.BlockSpec((1, 3, 1, HEAD_DIM, seq), lambda h: (part, 0, h, 0, 0)),
        ]
        + [anywhere] * (len(earlier) + len(deps)),
        out_specs=[
            pl.BlockSpec((1, HEAD_DIM, seq), lambda h: (part * heads + h, 0, 0)),
            pl.BlockSpec((1, 1, seq), lambda h: (part * heads + h, 0, 0)),
        ],
        out_shape=[
            jax.ShapeDtypeStruct((2 * heads, HEAD_DIM, seq), bf16),
            jax.ShapeDtypeStruct((2 * heads, 1, seq), f32),
        ],
        input_output_aliases={2 + i: i for i in range(len(earlier))},
        scratch_shapes=[pltpu.VMEM((seq, 512), f32)],
        compiler_params=pltpu.CompilerParams(vmem_limit_bytes=VMEM_LIMIT),
        cost_estimate=LIGHT,
        name="attend",
    )(mask, qkv, *earlier, *deps)


def attend_back_kernel(deps, mask_ref, qkv_ref, logsum_ref, dmix_ref, *refs):
    out_ref, score_ref, dk_ref, dv_ref = refs[deps:]
    seq = qkv_ref.shape[-1]
    half = seq // 2
    step = 512
    keys_t = qkv_ref[0, 1, 0]
    keys = keys_t.T
    values = qkv_ref[0, 2, 0].T
    for start in range(0, seq, step):
        query = qkv_ref[0, 0, 0, :, start : start + step]
        dmix = dmix_ref[0, :, start : start + step]
        score_ref[...] = dot(keys, query, ((1,), (0,)))
        score_ref[half - 64 : half, :] += mask_ref[0]
        score_ref[seq - 64 :, :] += mask_ref[1]
        probs = jnp.exp2(score_ref[...] * SCALE2 - logsum_ref[0, :, start : start + step])
        dprobs = dot(values, dmix, ((1,), (0,)))
        prod = probs * dprobs
        delta = jnp.sum(prod, 0, keepdims=True)
        dscore = (prod - probs * delta).astype(bf16)
        probs_low = probs.astype(bf16)
        out_ref[0, 0, 0, :, start : start + step] = (
            dot(keys_t, dscore, ((1,), (0,))) * SCALE
        ).astype(bf16)
        dk = dot(query, dscore, ((1,), (1,)))
        dv = dot(dmix, probs_low, ((1,), (1,)))
        if start == 0:
            dk_ref[...] = dk
            dv_ref[...] = dv
        else:
            dk_ref[...] += dk
            dv_ref[...] += dv
    out_ref[0, 1, 0] = (dk_ref[...] * SCALE).astype(bf16)
    out_ref[0, 2, 0] = dv_ref[...].astype(bf16)


def attend_back(part, qkv, logsum, dmix, mask, earlier=(), deps=()):
    heads, seq = qkv.shape[2], qkv.shape[4]
    pairs = heads * seq * seq
    block = pl.BlockSpec((1, 3, 1, HEAD_DIM, seq), lambda h: (part, 0, h, 0, 0))
    anywhere = pl.BlockSpec(memory_space=pl.ANY)
    return pl.pallas_call(
        functools.partial(attend_back_kernel, len(earlier) + len(deps)),
        grid=(heads,),
        in_specs=[
            pl.BlockSpec(memory_space=pltpu.SMEM),
            block,
            pl.BlockSpec((1, 1, seq), lambda h: (part * heads + h, 0, 0)),
            pl.BlockSpec((1, HEAD_DIM, seq), lambda h: (part * heads + h, 0, 0)),
        ]
        + [anywhere] * (len(earlier) + len(deps)),
        out_specs=block,
        out_shape=jax.ShapeDtypeStruct(qkv.shape, bf16),
        input_output_aliases={4 + i: i for i in range(len(earlier))},
        scratch_shapes=[
            pltpu.VMEM((seq, 512), f32),
            pltpu.VMEM((HEAD_DIM, seq), f32),
            pltpu.VMEM((HEAD_DIM, seq), f32),
        ],
        compiler_params=pltpu.CompilerParams(vmem_limit_bytes=VMEM_LIMIT),
        cost_estimate=LIGHT,
        name="attend_back",
    )(mask, qkv, logsum, dmix, *earlier, *deps)


def move_kernel(plans, count, deps, where_ref, *refs):
    pieces = refs[:count]
    outs = refs[count + deps : count + deps + len(plans)]
    sem = refs[-1]
    zi, xi, yi = where_ref[0], where_ref[1], where_ref[2]

    def locate(ref, index):
        for item in index:
            if isinstance(item, tuple):
                item = {"z": zi, "x": xi, "y": yi}[item[0]] ^ item[1]
            ref = ref.at[item]
        return ref

    copies = []
    for out, plan in zip(outs, plans):
        for piece, source, target in plan:
            copies.append(
                pltpu.make_async_copy(
                    locate(pieces[piece], source), locate(out, target), sem.at[len(copies)]
                )
            )
    for copy in copies:
        copy.start()
    for copy in copies:
        copy.wait()


def move(where, pieces, shapes, plans, deps=(), name="move"):
    total = sum(len(plan) for plan in plans)
    anywhere = pl.BlockSpec(memory_space=pl.ANY)
    return pl.pallas_call(
        functools.partial(move_kernel, plans, len(pieces), len(deps)),
        in_specs=[pl.BlockSpec(memory_space=pltpu.SMEM)] + [anywhere] * (len(pieces) + len(deps)),
        out_specs=[pl.BlockSpec(memory_space=pltpu.VMEM)] * len(plans),
        out_shape=[jax.ShapeDtypeStruct(shape, pieces[0].dtype) for shape in shapes],
        scratch_shapes=[pltpu.SemaphoreType.DMA((total,))],
        compiler_params=pltpu.CompilerParams(vmem_limit_bytes=VMEM_LIMIT),
        cost_estimate=LIGHT,
        name=name,
    )(where, *pieces, *deps)


def add_near_kernel(half, where_ref, grads, more, got_x, got_y, *refs):
    send_y, send_x, own, parts, gx, gy, sem = refs[-7:]
    zi, xi, yi = where_ref[0], where_ref[1], where_ref[2]
    lows, highs = pl.ds(0, half), pl.ds(half, half)
    sources = [
        ((lows, xi, 1 - yi), got_x.at[:, 1 - yi], gx.at[0]),
        ((highs, 1 - xi, yi), got_y.at[:, 1 - xi], gy.at[0]),
        ((lows, xi, yi), got_x.at[:, yi], gx.at[1]),
        ((highs, xi, yi), got_y.at[:, xi], gy.at[1]),
    ]
    copies = []
    for number, (place, got_from, got_to) in enumerate(sources):
        pairs = [
            (grads.at[place], parts.at[number, :, pl.ds(0, 3)]),
            (more.at[place], parts.at[number, :, 3]),
            (got_from, got_to),
        ]
        copies.append(
            [
                pltpu.make_async_copy(source, target, sem.at[3 * number + i])
                for i, (source, target) in enumerate(pairs)
            ]
        )
    for group in copies:
        for copy in group:
            copy.start()
    for number in range(4):
        for copy in copies[number]:
            copy.wait()
        got = (gx, gy, gx, gy)[number]
        for k in range(half):
            for i in range(4):
                total = parts[number, k, i].astype(f32) + got[number // 2, k, i].astype(f32)
                if number == 0:
                    send_y[k, i] = total.astype(bf16)
                elif number == 1:
                    send_x[k, i] = total.astype(bf16)
                else:
                    own[(number - 2) * half + k, i] = total


def add_near(where, grads, more, got_x, got_y, deps=()):
    nz, rows, columns = grads.shape[0], *grads.shape[-2:]
    half = nz // 2
    anywhere = pl.BlockSpec(memory_space=pl.ANY)
    inside = pl.BlockSpec(memory_space=pltpu.VMEM)
    return pl.pallas_call(
        functools.partial(add_near_kernel, half),
        in_specs=[pl.BlockSpec(memory_space=pltpu.SMEM)] + [anywhere] * (4 + len(deps)),
        out_specs=[inside] * 3,
        out_shape=[
            jax.ShapeDtypeStruct((half, 4, rows, columns), bf16),
            jax.ShapeDtypeStruct((half, 4, rows, columns), bf16),
            jax.ShapeDtypeStruct((nz, 4, rows, columns), f32),
        ],
        scratch_shapes=[
            pltpu.VMEM((4, half, 4, rows, columns), bf16),
            pltpu.VMEM((2, half, 4, rows, columns), bf16),
            pltpu.VMEM((2, half, 4, rows, columns), bf16),
            pltpu.SemaphoreType.DMA((12,)),
        ],
        compiler_params=pltpu.CompilerParams(vmem_limit_bytes=VMEM_LIMIT),
        cost_estimate=LIGHT,
        name="add_near",
    )(where, grads, more, got_x, got_y, *deps)


def add_far_kernel(nz, where_ref, own_ref, got_y, got_x, *refs):
    sends, mine = refs[-2:]
    zi = where_ref[0]
    half = nz // 2
    for k in range(nz):
        got = got_y[k] if k < half else got_x[k - half]
        total = own_ref[k] + got.astype(f32)
        distance = zi ^ k

        @pl.when(distance == 0)
        def _():
            mine[...] = total

        @pl.when(distance > 0)
        def _():
            sends[jnp.maximum(distance - 1, 0)] = total.astype(bf16)


def add_far(where, own, got_y, got_x, deps=()):
    nz = own.shape[0]
    inside = pl.BlockSpec(memory_space=pltpu.VMEM)
    return pl.pallas_call(
        functools.partial(add_far_kernel, nz),
        in_specs=[pl.BlockSpec(memory_space=pltpu.SMEM)]
        + [inside] * 3
        + [pl.BlockSpec(memory_space=pl.ANY)] * len(deps),
        out_specs=[inside] * 2,
        out_shape=[
            jax.ShapeDtypeStruct((nz - 1, *own.shape[1:]), bf16),
            jax.ShapeDtypeStruct(own.shape[1:], f32),
        ],
        compiler_params=pltpu.CompilerParams(vmem_limit_bytes=VMEM_LIMIT),
        cost_estimate=LIGHT,
        name="add_far",
    )(where, own, got_y, got_x, *deps)


def multiply_kernel(left_ref, right_ref, *refs):
    refs[-1][...] = dot(left_ref[...], right_ref[...], ((1,), (0,)))


def multiply(left, right, deps=()):
    rows, inner = left.shape
    columns = right.shape[1]
    step = 256
    return pl.pallas_call(
        multiply_kernel,
        grid=(rows // step,),
        in_specs=[
            pl.BlockSpec((step, inner), lambda i: (i, 0)),
            pl.BlockSpec((inner, columns), lambda i: (0, 0)),
        ]
        + [pl.BlockSpec(memory_space=pl.ANY)] * len(deps),
        out_specs=pl.BlockSpec((step, columns), lambda i: (i, 0)),
        out_shape=jax.ShapeDtypeStruct((rows, columns), f32),
        compiler_params=pltpu.CompilerParams(vmem_limit_bytes=VMEM_LIMIT),
        cost_estimate=LIGHT,
        name="multiply",
    )(left, right, *deps)


def weight_grad_kernel(left_ref, right_ref, out_ref):
    out_ref[...] = dot(left_ref[...].T, right_ref[...], ((1,), (1,))).astype(bf16)


def weight_grad(left, right):
    tokens, rows = left.shape
    columns = right.shape[0]
    step = 384
    return pl.pallas_call(
        weight_grad_kernel,
        grid=(rows // step,),
        in_specs=[
            pl.BlockSpec((tokens, step), lambda i: (0, i)),
            pl.BlockSpec((columns, tokens), lambda i: (0, 0)),
        ],
        out_specs=pl.BlockSpec((step, columns), lambda i: (i, 0)),
        out_shape=jax.ShapeDtypeStruct((rows, columns), bf16),
        compiler_params=pltpu.CompilerParams(vmem_limit_bytes=VMEM_LIMIT),
        cost_estimate=LIGHT,
        name="weight_grad",
    )(left, right)


def weight_grad_turned_kernel(left_ref, right_ref, out_ref, turned_ref):
    z = pl.program_id(0)
    rows = out_ref.shape[2]

    @pl.when(z == 0)
    def _():
        turned_ref[...] = left_ref[...].T.reshape(turned_ref.shape)

    total = dot(turned_ref[z], right_ref[...], ((1,), (0,))).astype(bf16)
    for x in range(2):
        for y in range(2):
            first = (2 * x + y) * rows
            out_ref[2 * x + y, 0] = total[first : first + rows]


def weight_grad_turned(left, right, nz):
    tokens, width = left.shape
    columns = right.shape[1]
    rows = width // (4 * nz)
    return pl.pallas_call(
        weight_grad_turned_kernel,
        grid=(nz,),
        in_specs=[
            pl.BlockSpec((tokens, width), lambda z: (0, 0)),
            pl.BlockSpec((tokens, columns), lambda z: (0, 0)),
        ],
        out_specs=pl.BlockSpec((4, 1, rows, columns), lambda z: (0, z, 0, 0)),
        out_shape=jax.ShapeDtypeStruct((4, nz, rows, columns), bf16),
        scratch_shapes=[pltpu.VMEM((nz, 4 * rows, tokens), bf16)],
        compiler_params=pltpu.CompilerParams(vmem_limit_bytes=VMEM_LIMIT),
        cost_estimate=LIGHT,
        name="weight_grad_turned",
    )(left, right)


def input_grad_kernel(left_ref, right_ref, *refs):
    refs[-1][...] = dot(left_ref[...].T, right_ref[...], ((1,), (1,)))


def input_grad(left, right, deps=()):
    inner, tokens = left.shape
    columns = right.shape[0]
    step = 256
    return pl.pallas_call(
        input_grad_kernel,
        grid=(tokens // step,),
        in_specs=[
            pl.BlockSpec((inner, step), lambda i: (0, i)),
            pl.BlockSpec((columns, inner), lambda i: (0, 0)),
        ]
        + [pl.BlockSpec(memory_space=pl.ANY)] * len(deps),
        out_specs=pl.BlockSpec((step, columns), lambda i: (i, 0)),
        out_shape=jax.ShapeDtypeStruct((tokens, columns), f32),
        compiler_params=pltpu.CompilerParams(vmem_limit_bytes=VMEM_LIMIT),
        cost_estimate=LIGHT,
        name="input_grad",
    )(left, right, *deps)


def after_kernel(value_ref, *refs):
    refs[-1][...] = value_ref[...]


def after(value, *deps):
    flat = value.reshape(-1, value.shape[-1])
    return pl.pallas_call(
        after_kernel,
        in_specs=[pl.BlockSpec(memory_space=pltpu.VMEM)]
        + [pl.BlockSpec(memory_space=pl.ANY)] * len(deps),
        out_specs=pl.BlockSpec(memory_space=pltpu.VMEM),
        out_shape=jax.ShapeDtypeStruct(flat.shape, flat.dtype),
        compiler_params=pltpu.CompilerParams(vmem_limit_bytes=VMEM_LIMIT),
        cost_estimate=LIGHT,
        name="after",
    )(flat, *deps).reshape(value.shape)


class Group:
    def __init__(self, n):
        self.n = n
        self.nz = n // 8
        self.me = lax.axis_index(AXES).astype(jnp.int32)
        self.y = self.me & 1
        self.c = (self.me >> 1) & 1
        self.x = (self.me >> 2) & 1
        self.z = self.me >> 3
        self.where = jnp.stack([self.z, self.x, self.y])

    def xor(self, value, mask):
        return lax.ppermute(value, AXES, [(i, i ^ mask) for i in range(self.n)])

    def core(self, value):
        return self.xor(value, 2)

    def turn(self, value):
        got = lax.ppermute(
            value,
            AXES,
            [(i, i ^ 3) for i in range(self.n) if (i & 3) in (1, 2)],
        )
        return jnp.where(self.c == self.y, value, got)

    def turn_other(self, value):
        return lax.ppermute(
            value,
            AXES,
            [(i, (i & ~3) | ((1 - (i & 1)) << 1) | ((i >> 1) & 1)) for i in range(self.n)],
        )

    def turn_other_back(self, value):
        return lax.ppermute(
            value,
            AXES,
            [(i, (i & ~3) | ((i & 1) << 1) | (1 - ((i >> 1) & 1))) for i in range(self.n)],
        )

    def to_block(self, parts):
        mine = lax.dynamic_index_in_dim(parts, self.y, 0, False)
        other = lax.dynamic_index_in_dim(parts, 1 - self.y, 0, False)
        got_a, got_b = self.turn(mine), self.turn_other(other)
        straight = self.c == 0
        return jnp.concatenate(
            [jnp.where(straight, got_a, got_b), jnp.where(straight, got_b, got_a)], 0
        )

    def from_block(self, block):
        rows = block.shape[0] // 2
        pieces = block.reshape(2, rows, block.shape[1])
        got_a = self.turn(lax.dynamic_index_in_dim(pieces, self.c, 0, False))
        got_b = self.turn_other_back(lax.dynamic_index_in_dim(pieces, 1 - self.c, 0, False))
        straight = self.y == 0
        return jnp.stack(
            [jnp.where(straight, got_a, got_b), jnp.where(straight, got_b, got_a)], 0
        )

    def gather_z(self, block):
        return [block] + [self.xor(block, d << 3) for d in range(1, self.nz)]

    def gather_near(self, pieces, deps=()):
        half = self.nz // 2
        plans = [
            [(k, (), (k,)) for k in range(half)],
            [(half + k, (), (k,)) for k in range(half)],
        ]
        shape = (half, *pieces[0].shape)
        low, high = move(self.where, pieces, [shape] * 2, plans, deps, "stack_z")
        return low, high, self.xor(low, 1), self.xor(high, 4)

    def gather_far(self, near, deps=()):
        half = self.nz // 2
        low, high, low_y, high_x = near
        plans = [[(0, (), (0,)), (2, (), (1,))], [(1, (), (0,)), (3, (), (1,))]]
        shape = (2, *low.shape)
        low_2, high_2 = move(self.where, near, [shape] * 2, plans, deps, "stack_near")
        return low_2, high_2, self.xor(low_2, 4), self.xor(high_2, 1)

    def gather_end(self, far, deps=(), cuts=((),), shapes=None, order="zxy"):
        nz, half = self.nz, self.nz // 2
        plans = []
        for cut in cuts:
            plan = []
            for k in range(half):
                for other in range(2):
                    for piece, target in (
                        (0, (("z", k), ("x", 0), ("y", other))),
                        (1, (("z", half + k), ("x", other), ("y", 0))),
                        (2, (("z", k), ("x", 1), ("y", other))),
                        (3, (("z", half + k), ("x", other), ("y", 1))),
                    ):
                        target = tuple(dict((t[0], t) for t in target)[axis] for axis in order)
                        plan.append((piece, (other, k, *cut), target))
            plans.append(plan)
        lead = tuple({"z": nz}.get(axis, 2) for axis in order)
        shapes = [(*lead, *shape) for shape in shapes or [far[0].shape[2:]]]
        return move(self.where, far, shapes, plans, deps, "place")

    def scatter_z(self, blocks, deps=()):
        nz = self.nz
        plans = [[(0, (("z", d),), ())] for d in range(nz)]
        parts = move(self.where, [blocks], [blocks.shape[1:]] * nz, plans, deps, "split_z")
        return parts, [self.xor(parts[d], d << 3) for d in range(1, nz)]

    def sum_z(self, state):
        parts, got = state
        return sum((item.astype(f32) for item in got), parts[0].astype(f32))

    def scatter_start(self, grads, deps=()):
        half = self.nz // 2
        plans = [[], []]
        for k in range(half):
            for other in range(2):
                for piece, cut in ((0, pl.ds(0, 3)), (1, 3)):
                    plans[0].append((piece, (k, ("x", 1), other), (k, other, cut)))
                    plans[1].append((piece, (half + k, other, ("y", 1)), (k, other, cut)))
        shape = (half, 2, 4, *grads[1].shape[3:])
        to_x, to_y = move(self.where, grads, [shape] * 2, plans, deps, "split")
        return grads, self.xor(to_x, 4), self.xor(to_y, 1), to_x

    def scatter_near(self, state, deps=()):
        grads, got_x, got_y = state[:3]
        send_y, send_x, own = add_near(self.where, *grads, got_x, got_y, deps)
        return own, self.xor(send_y, 1), self.xor(send_x, 4)

    def scatter_far(self, state, deps=()):
        sends, mine = add_far(self.where, *state, deps)
        return mine, [self.xor(sends[d - 1], d << 3) for d in range(1, self.nz)]

    def scatter_end(self, state):
        mine, got = state
        return sum((item.astype(f32) for item in got), mine)

    def all_sum(self, value):
        value = value + self.core(value)
        value = value + self.xor(value, 1)
        value = value + self.xor(value, 4)
        return sum((self.xor(value, d << 3) for d in range(1, self.nz)), value)


def per_device(
    tokens,
    embedding,
    heights,
    widths,
    cotangent,
    w_qkv,
    w_proj,
    w_fc1,
    w_fc2,
    w_ada,
    biases,
    m_qkv,
    m_proj,
    m_fc1,
    m_fc2,
    m_ada,
    m_bias,
    v_qkv,
    v_proj,
    v_fc1,
    v_fc2,
    v_ada,
    v_bias,
):
    rows = tokens.shape[1]
    n = math.prod(lax.axis_size(axis) for axis in AXES)
    own_rows = w_qkv.shape[0]
    g = Group(n)
    nz = g.nz
    groups = n // 4
    pair = 2 * own_rows
    ff_rows = w_fc2.shape[0]
    bias_rows = biases.shape[0]

    qkv_parts = (
        w_qkv.astype(bf16)
        .reshape(own_rows, 3, 2, HALF, 2, HEAD_DIM)
        .transpose(4, 0, 2, 1, 3, 5)
        .reshape(2, own_rows, QKV)
    )
    third = own_rows * D // QKV
    qp_block = jnp.concatenate(
        [g.to_block(qkv_parts), w_proj.astype(bf16).reshape(third, QKV)], 0
    ).reshape(4, third, QKV)
    qp_z = g.gather_z(qp_block)
    qp_near = g.gather_near(qp_z)
    fc1_parts = (
        w_fc1.astype(bf16)
        .reshape(own_rows, nz, 2, 2, 2, ff_rows)
        .transpose(3, 0, 2, 4, 1, 5)
        .reshape(2, own_rows, OWN_FF)
    )
    fc1_block = g.to_block(after(fc1_parts, qp_block))
    fc1_z = g.gather_z(after(fc1_block, qp_near[0]))
    qp_far = g.gather_far(qp_near, [fc1_z[0]])
    fc1_near = g.gather_near(fc1_z, qp_far[2:])
    qkv_w = g.gather_end(qp_far, (), ((pl.ds(0, 3),),), ((3, third, QKV),))[0]
    qkv_w = qkv_w.reshape(D, QKV)
    fc2_w = lax.all_gather(
        after(w_fc2.astype(bf16), qkv_w), ("x", "y", "z"), axis=0, tiled=True
    )
    tokens_here = g.turn(after(tokens[0], qp_block))
    cond_row = jax.nn.silu(embedding[0]).astype(bf16)
    small = jnp.concatenate(
        [
            cond_row,
            biases.astype(bf16),
            heights.astype(bf16),
            widths.astype(bf16),
        ]
    )
    small_size = -(-small.shape[0] // 128) * 128
    small = jnp.pad(small, (0, small_size - small.shape[0]))[None]
    line = jnp.stack([small] + [g.xor(small, d << 3) for d in range(1, nz)])
    near = jnp.stack([line, g.xor(line, 4)], 1)
    every = jnp.stack([near] + [g.xor(near, low) for low in range(1, 4)], 2)
    every = every.reshape(n, small_size)
    spread = (jnp.arange(n)[:, None] == (jnp.arange(n)[None, :] ^ g.me)).astype(bf16)
    natural = dot(spread, every, ((1,), (0,)))
    bias_full = natural[:, D : D + bias_rows].reshape(-1)
    bias_qkv = bias_full[: 3 * D]
    bias_proj = bias_full[3 * D : 4 * D]
    bias_fc1 = bias_full[4 * D : 4 * D + FF]
    bias_fc2 = bias_full[4 * D + FF : 5 * D + FF]
    bias_ada = bias_full[5 * D + FF :]
    image_row = lax.dynamic_index_in_dim(natural, (g.me & ~3) | (g.y << 1), 0, True)
    image_row = after(image_row, qp_near[0])[0]
    height = image_row[D + bias_rows].astype(jnp.int32)
    width = image_row[D + bias_rows + 1].astype(jnp.int32)
    conds = every[:, :D].reshape(nz, 2, 2, 2, D)[:, :, :, 0]
    conds = jnp.where(g.c == g.y, conds, conds[:, :, ::-1])
    conds_own = lax.dynamic_slice_in_dim(
        conds.reshape(groups * 2, D), g.me * own_rows, own_rows, 1
    )
    mod_part = dot(conds_own, w_ada.astype(bf16), ((1,), (0,))).reshape(nz, 2, 2, 6 * D)
    mod_x = mod_part[:, 0] + g.xor(mod_part[:, 1], 4)
    mod_y = mod_x[:, 0] + g.xor(mod_x[:, 1], 1)
    mod_z = mod_y[0:1]
    for d in range(1, nz):
        mod_z = mod_z + g.xor(mod_y[d : d + 1], d << 3)
    modul = mod_z + g.core(mod_z) + bias_ada
    shift1, scale1, gate1, shift2, scale2, gate2 = [
        modul[:, j * D : (j + 1) * D] for j in range(6)
    ]

    cotangent_here = g.turn(after(cotangent[0], qkv_w))

    slots = g.c * rows + jnp.arange(rows, dtype=jnp.int32)
    count = height * width
    valid_rows = (slots < count).astype(f32)[:, None]
    seq = 2 * rows
    cut = jnp.where(count < seq, -1e30, 0.0).astype(f32)
    mask = jnp.stack([jnp.where(g.c == 1, cut, 0.0), jnp.where(g.c == 0, cut, 0.0)])
    x_in = tokens_here.astype(f32) + position_rows(slots, width)
    normed1, spread1 = normalize(x_in)
    attn_in = (normed1 * (1.0 + scale1) + shift1).astype(bf16)
    attn_all = jnp.concatenate([attn_in, g.core(attn_in)], 0)
    own_bias_qkv = lax.dynamic_index_in_dim(
        bias_qkv.reshape(3, 2, HALF, 2, HEAD_DIM), g.c, 3, False
    ).swapaxes(0, 1).reshape(-1, 1)
    qkv = (dot(qkv_w, attn_all, ((0,), (1,))) + own_bias_qkv).astype(bf16)
    qkv = qkv.reshape(2, 3, HALF, HEAD_DIM, seq)
    first = attend(0, qkv, mask, (), fc1_near[:2])
    fc1_far = g.gather_far(fc1_near, first[1:])
    proj_own = g.gather_end(qp_far, first[1:], ((3,),), ((third, QKV),))[0].reshape(-1, D)
    heads_match = pair % HEAD_DIM == 0
    if heads_match:
        proj_w = proj_own
    else:
        mine = proj_own.reshape(groups, pair, D)
        theirs = g.core(mine)
        own_first = g.c == 0
        whole = jnp.stack(
            [jnp.where(own_first, mine, theirs), jnp.where(own_first, theirs, mine)], 1
        ).reshape(OWN_HEADS, 2, HEAD_DIM, D)
        proj_w = lax.dynamic_index_in_dim(whole, g.c, 1, False).reshape(OWN_HEADS * HEAD_DIM, D)
    mixed, logsum = attend(1, qkv, mask, first, fc1_far[:2])
    fc1_w = g.gather_end(fc1_far)[0].reshape(D, OWN_FF)
    mixed = mixed.reshape(OWN_HEADS * HEAD_DIM, seq)
    attn_sib = dot(mixed[:, rows:], proj_w, ((0,), (0,)))
    attn = dot(mixed[:, :rows], proj_w, ((0,), (0,))) + g.core(attn_sib) + bias_proj
    x_mid = x_in + gate1 * attn
    normed2, spread2 = normalize(x_mid)
    mlp_in = (normed2 * (1.0 + scale2) + shift2).astype(bf16)
    mlp_all = jnp.concatenate([mlp_in, g.core(mlp_in)], 0)
    own_bias_fc1 = lax.dynamic_index_in_dim(
        bias_fc1.reshape(nz, 2, 2, 2, ff_rows), g.c, 2, False
    ).transpose(1, 2, 0, 3).reshape(-1)
    hidden_pre = dot(mlp_all, fc1_w, ((1,), (0,))) + own_bias_fc1
    hidden = gelu_tanh(hidden_pre).astype(bf16)
    d_out = cotangent_here.astype(f32) * valid_rows
    d_branch = (gate2 * d_out).astype(bf16)
    branch_all = jnp.concatenate([d_branch, g.core(d_branch)], 0)
    g_fc2 = dot(hidden, branch_all, ((0,), (0,))).astype(bf16)
    red_fc2 = lax.psum_scatter(g_fc2, ("x", "y"), scatter_dimension=0, tiled=True)
    gb_fc2 = jnp.sum(d_branch.astype(f32), 0)
    d_hidden = dot(branch_all, fc2_w, ((1,), (1,)))
    gelu_value, gelu_pull = jax.vjp(gelu_tanh, hidden_pre)
    d_pre = gelu_pull(d_hidden)[0].astype(bf16)
    g_fc1 = weight_grad_turned(mlp_all, d_pre, nz).reshape(D, OWN_FF)
    red_fc1 = lax.psum_scatter(g_fc1, ("x", "y"), scatter_dimension=0, tiled=True)
    gb_fc1 = jnp.sum(d_pre.astype(f32), 0)
    d_mlp_sib = dot(d_pre[rows:], fc1_w, ((1,), (1,)))
    d_mlp_in = dot(d_pre[:rows], fc1_w, ((1,), (1,))) + g.core(d_mlp_sib)
    d_scale2 = jnp.sum(d_mlp_in * normed2, 0)
    d_shift2 = jnp.sum(d_mlp_in, 0)
    d_mid = d_out + norm_back(normed2, spread2, d_mlp_in * (1.0 + scale2))
    d_attn = (gate1 * d_mid).astype(bf16)
    d_gate1 = jnp.sum(d_mid * attn, 0)
    gb_proj = jnp.sum(d_attn.astype(f32), 0)
    d_attn_all = jnp.concatenate([d_attn, g.core(d_attn)], 0)
    d_mixed = dot(proj_w, d_attn_all, ((1,), (1,))).astype(bf16)
    g_proj = dot(mixed, d_attn_all, ((1,), (0,))).astype(bf16)
    if heads_match:
        g_proj = g_proj.reshape(nz, 2, 2, third, QKV)
    else:
        own = (jnp.arange(2) == g.c)[None, :, None, None]
        whole = jnp.where(own, g_proj.reshape(OWN_HEADS, 1, HEAD_DIM, D), 0).reshape(
            groups, 2, pair, D
        )
        theirs = g.core(lax.dynamic_index_in_dim(whole, 1 - g.c, 1, False))
        mine = lax.dynamic_index_in_dim(whole, g.c, 1, False)
        g_proj = (mine.astype(f32) + theirs.astype(f32)).astype(bf16).reshape(nz, 2, 2, third, QKV)
    d_mixed = d_mixed.reshape(OWN_HEADS, HEAD_DIM, seq)
    d_qkv = attend_back(0, qkv, logsum, d_mixed, mask, (), [g_proj])
    fc2_state = g.scatter_z(red_fc2.reshape(nz, -1, D))
    d_qkv = attend_back(1, qkv, logsum, d_mixed, mask, [d_qkv], fc2_state[0][:1])
    d_qkv = d_qkv.reshape(QKV, seq)
    g_qkv = weight_grad(attn_all, d_qkv)
    qkv_state = g.scatter_start([g_qkv.reshape(nz, 2, 2, 3, third, QKV), g_proj])
    branch_all = multiply(hidden, fc2_w, [qkv_state[3]])
    branch = branch_all[:rows] + g.core(branch_all[rows:]) + bias_fc2
    output = (x_mid + gate2 * branch).astype(bf16)
    d_gate2 = jnp.sum(d_out * branch, 0)
    gb_qkv = jnp.sum(d_qkv.astype(f32), 1)
    d_attn_both = input_grad(d_qkv, qkv_w, [branch_all])
    d_attn_in = d_attn_both[:rows] + g.core(d_attn_both[rows:])
    d_scale1 = jnp.sum(d_attn_in * normed1, 0)
    d_shift1 = jnp.sum(d_attn_in, 0)
    grad_tokens = (d_mid + norm_back(normed1, spread1, d_attn_in * (1.0 + scale1))).astype(bf16)

    d_modul = jnp.concatenate([d_shift1, d_scale1, d_gate1, d_shift2, d_scale2, d_gate2])
    own = (jnp.arange(2) == g.c)[None, :, None]
    gb_qkv = gb_qkv.reshape(2, 3, HALF, HEAD_DIM).swapaxes(0, 1)
    gb_qkv = jnp.where(own, gb_qkv.reshape(3 * OWN_HEADS, 1, HEAD_DIM), 0.0).reshape(-1)
    gb_fc1 = gb_fc1.reshape(2, 2, nz, ff_rows).transpose(2, 0, 1, 3)
    gb_fc1 = jnp.where(
        own, gb_fc1.reshape(groups, 1, 2 * ff_rows), 0.0
    ).reshape(-1)
    vector = jnp.concatenate([gb_qkv, gb_proj, gb_fc1, gb_fc2, d_modul])[None]
    fc1_state = g.scatter_z(red_fc1.reshape(nz, -1, OWN_FF), [vector, output, grad_tokens])
    qkv_state = g.scatter_near(qkv_state, fc1_state[0][:1])
    vector = after(vector, qkv_state[0])
    vector = vector + g.core(vector)
    plain = vector.shape[1] - 6 * D
    sums, mods = vector[:, :plain], vector[:, plain:]
    others = [g.xor(vector, d << 3) for d in range(1, nz)]
    for item in others:
        sums = sums + item[:, :plain]
    mods = jnp.concatenate([mods] + [item[:, plain:] for item in others], 0)[:, None]
    qkv_state = g.scatter_far(qkv_state, [sums, mods])
    sums = after(sums, qkv_state[0])
    for mask_bit in (1, 4):
        packed = jnp.concatenate([sums.reshape(-1), mods.reshape(-1)])[None]
        packed = g.xor(packed, mask_bit)[0]
        sums = sums + packed[:plain]
        mods = jnp.stack([mods, packed[plain:].reshape(mods.shape)], 1)
    mods = mods.reshape(groups * 2, 6 * D)
    red_ada = lax.dot_general(
        conds_own.astype(f32),
        mods,
        (((0,), (0,)), ((), ())),
        precision=lax.Precision.HIGHEST,
        preferred_element_type=f32,
    )
    g_bias = jnp.concatenate([sums[0], jnp.sum(mods, 0)])
    red_bias = lax.dynamic_slice_in_dim(g_bias, g.me * bias_rows, bias_rows)

    red_fc2 = g.sum_z(fc2_state)
    red_fc1 = after(g.sum_z(fc1_state), sums)
    red_qp = g.scatter_end(qkv_state)
    red_qkv = red_qp[:3].reshape(2 * own_rows, QKV)
    red_proj = red_qp[3].reshape(own_rows, D)
    output, grad_tokens = g.turn(after(output, sums))[None], g.turn(after(grad_tokens, sums))[None]
    red_qkv = (
        g.from_block(red_qkv)
        .reshape(2, own_rows, 2, 3, HALF, HEAD_DIM)
        .transpose(1, 3, 2, 4, 0, 5)
        .reshape(own_rows, 3 * D)
    )
    red_fc1 = (
        g.from_block(red_fc1)
        .reshape(2, own_rows, 2, 2, nz, ff_rows)
        .transpose(1, 4, 2, 0, 3, 5)
        .reshape(own_rows, FF)
    )
    reduced = (red_qkv, red_proj, red_fc1, red_fc2, red_ada, red_bias)
    squares = sum((jnp.sum(piece * piece) for piece in reduced))
    squares = g.all_sum(jnp.broadcast_to(squares, (1, 128)))[0, 0]
    grad_norm = jnp.sqrt(squares)
    factor = jnp.minimum(1.0, clip_limit / grad_norm)
    params = (w_qkv, w_proj, w_fc1, w_fc2, w_ada, biases)
    firsts = (m_qkv, m_proj, m_fc1, m_fc2, m_ada, m_bias)
    seconds = (v_qkv, v_proj, v_fc1, v_fc2, v_ada, v_bias)
    rates = (learn_rate, learn_rate, learn_rate, learn_rate, learn_rate, bias_rate)
    results = [
        adam_step(params[j], firsts[j], seconds[j], reduced[j], factor, rates[j]) for j in range(6)
    ]
    return (
        output,
        grad_tokens,
        grad_norm,
        *[item[0] for item in results],
        *[item[1] for item in results],
        *[item[2] for item in results],
    )


def solution(mesh):
    count = mesh.devices.size
    fine = jax.sharding.Mesh(mesh.devices.reshape(count // 8, 2, 2, 2), AXES)
    image = ("z", "x", "core")
    patches = P(image, "y", None)
    state = (P(AXES, None),) * 5 + (P(AXES),)
    return jax.shard_map(
        per_device,
        mesh=fine,
        in_specs=(patches, P(image, None), P(image), P(image), patches, *state, *state, *state),
        out_specs=(patches, patches, P(), *state, *state, *state),
        check_vma=False,
    )
```

```python
import functools
import math

import jax
import jax.numpy as jnp
from jax import lax
from jax.experimental import pallas as pl
from jax.experimental.pallas import tpu as pltpu
from jax.sharding import PartitionSpec as P

D = 1152
HEADS = 16
HEAD_DIM = 72
FF = 4608
STEPS = 10
OWN_HEADS = HEADS // 2
OWN_FF = FF // 2
QKV = 3 * OWN_HEADS * HEAD_DIM
HALF = OWN_HEADS // 2
AXES = ("z", "x", "core", "y")

clip_limit = 1000.0
learn_rate = 0.04
bias_rate = 0.25
beta_one = 0.5
beta_two = 0.5
weight_decay = 0.01

bf16 = jnp.bfloat16
f32 = jnp.float32
VMEM_LIMIT = 56 * 1024 * 1024
PACE = 0.05 * 3.3e6


def cost(microseconds):
    return pl.CostEstimate(
        flops=1, bytes_accessed=int(microseconds * PACE), transcendentals=0
    )


SCALE = HEAD_DIM ** (-0.5)
SCALE2 = SCALE * math.log2(math.e)


def normalize(values):
    centre = jnp.mean(values, -1, keepdims=True)
    centered = values - centre
    spread = lax.rsqrt(jnp.mean(centered * centered, -1, keepdims=True) + 1e-06)
    return (centered * spread, spread)


def norm_back(normed, spread, grad):
    return spread * (
        grad
        - jnp.mean(grad, -1, keepdims=True)
        - normed * jnp.mean(grad * normed, -1, keepdims=True)
    )


def gelu_tanh(values):
    return jax.nn.gelu(values, approximate=True)


def position_rows(slots, width):
    quarter = D // 4
    omega = 1.0 / 10000.0 ** (jnp.arange(quarter, dtype=f32) / quarter)
    rowpos = (slots // width).astype(f32)[..., None] * omega
    colpos = (slots % width).astype(f32)[..., None] * omega
    return jnp.concatenate([jnp.sin(rowpos), jnp.cos(rowpos), jnp.sin(colpos), jnp.cos(colpos)], -1)


def adam_step(weight, first, second, grad, factor, rate):
    clipped = grad * factor
    first = beta_one * first + (1.0 - beta_one) * clipped
    second = beta_two * second + (1.0 - beta_two) * clipped * clipped
    first_hat = first / (1.0 - beta_one**STEPS)
    second_hat = second / (1.0 - beta_two**STEPS)
    update = first_hat / (jnp.sqrt(second_hat) + 1e-08) + weight_decay * weight
    return (weight - rate * update, first, second)


def dot(left, right, over):
    return lax.dot_general(left, right, (over, ((), ())), preferred_element_type=f32)


def attend_kernel(deps, mask_ref, qkv_ref, *refs):
    mixed_ref, logsum_ref, score_ref = refs[deps:]
    seq = qkv_ref.shape[-1]
    half = seq // 2
    step = 512
    keys = qkv_ref[0, 1, 0].T
    values = qkv_ref[0, 2, 0]
    for start in range(0, seq, step):
        query = qkv_ref[0, 0, 0, :, start : start + step]
        score_ref[...] = dot(keys, query, ((1,), (0,)))
        score_ref[half - 64 : half, :] += mask_ref[0]
        score_ref[seq - 64 :, :] += mask_ref[1]
        scores = score_ref[...]
        top = jnp.max(scores, 0, keepdims=True)
        expo = jnp.exp2((scores - top) * SCALE2)
        total = jnp.sum(expo, 0, keepdims=True)
        probs = (expo * (1.0 / total)).astype(bf16)
        mixed = dot(values, probs, ((1,), (0,)))
        mixed_ref[0, :, start : start + step] = mixed.astype(bf16)
        logsum_ref[0, :, start : start + step] = top * SCALE2 + jnp.log2(total)


def attend(part, qkv, mask, earlier=(), deps=()):
    heads, seq = qkv.shape[2], qkv.shape[4]
    pairs = heads * seq * seq
    anywhere = pl.BlockSpec(memory_space=pl.ANY)
    return pl.pallas_call(
        functools.partial(attend_kernel, len(earlier) + len(deps)),
        grid=(heads,),
        in_specs=[
            pl.BlockSpec(memory_space=pltpu.SMEM),
            pl.BlockSpec((1, 3, 1, HEAD_DIM, seq), lambda h: (part, 0, h, 0, 0)),
        ]
        + [anywhere] * (len(earlier) + len(deps)),
        out_specs=[
            pl.BlockSpec((1, HEAD_DIM, seq), lambda h: (part * heads + h, 0, 0)),
            pl.BlockSpec((1, 1, seq), lambda h: (part * heads + h, 0, 0)),
        ],
        out_shape=[
            jax.ShapeDtypeStruct((2 * heads, HEAD_DIM, seq), bf16),
            jax.ShapeDtypeStruct((2 * heads, 1, seq), f32),
        ],
        input_output_aliases={2 + i: i for i in range(len(earlier))},
        scratch_shapes=[pltpu.VMEM((seq, 512), f32)],
        compiler_params=pltpu.CompilerParams(vmem_limit_bytes=VMEM_LIMIT),
        cost_estimate=cost(9.8),
        name="attend",
    )(mask, qkv, *earlier, *deps)


def attend_back_kernel(deps, mask_ref, qkv_ref, logsum_ref, dmix_ref, *refs):
    out_ref, score_ref, dk_ref, dv_ref = refs[deps:]
    seq = qkv_ref.shape[-1]
    half = seq // 2
    step = 512
    keys_t = qkv_ref[0, 1, 0]
    keys = keys_t.T
    values = qkv_ref[0, 2, 0].T
    for start in range(0, seq, step):
        query = qkv_ref[0, 0, 0, :, start : start + step]
        dmix = dmix_ref[0, :, start : start + step]
        score_ref[...] = dot(keys, query, ((1,), (0,)))
        score_ref[half - 64 : half, :] += mask_ref[0]
        score_ref[seq - 64 :, :] += mask_ref[1]
        probs = jnp.exp2(score_ref[...] * SCALE2 - logsum_ref[0, :, start : start + step])
        dprobs = dot(values, dmix, ((1,), (0,)))
        prod = probs * dprobs
        delta = jnp.sum(prod, 0, keepdims=True)
        dscore = (prod - probs * delta).astype(bf16)
        probs_low = probs.astype(bf16)
        out_ref[0, 0, 0, :, start : start + step] = (
            dot(keys_t, dscore, ((1,), (0,))) * SCALE
        ).astype(bf16)
        dk = dot(query, dscore, ((1,), (1,)))
        dv = dot(dmix, probs_low, ((1,), (1,)))
        if start == 0:
            dk_ref[...] = dk
            dv_ref[...] = dv
        else:
            dk_ref[...] += dk
            dv_ref[...] += dv
    out_ref[0, 1, 0] = (dk_ref[...] * SCALE).astype(bf16)
    out_ref[0, 2, 0] = dv_ref[...].astype(bf16)


def attend_back(part, qkv, logsum, dmix, mask, earlier=(), deps=()):
    heads, seq = qkv.shape[2], qkv.shape[4]
    pairs = heads * seq * seq
    block = pl.BlockSpec((1, 3, 1, HEAD_DIM, seq), lambda h: (part, 0, h, 0, 0))
    anywhere = pl.BlockSpec(memory_space=pl.ANY)
    return pl.pallas_call(
        functools.partial(attend_back_kernel, len(earlier) + len(deps)),
        grid=(heads,),
        in_specs=[
            pl.BlockSpec(memory_space=pltpu.SMEM),
            block,
            pl.BlockSpec((1, 1, seq), lambda h: (part * heads + h, 0, 0)),
            pl.BlockSpec((1, HEAD_DIM, seq), lambda h: (part * heads + h, 0, 0)),
        ]
        + [anywhere] * (len(earlier) + len(deps)),
        out_specs=block,
        out_shape=jax.ShapeDtypeStruct(qkv.shape, bf16),
        input_output_aliases={4 + i: i for i in range(len(earlier))},
        scratch_shapes=[
            pltpu.VMEM((seq, 512), f32),
            pltpu.VMEM((HEAD_DIM, seq), f32),
            pltpu.VMEM((HEAD_DIM, seq), f32),
        ],
        compiler_params=pltpu.CompilerParams(vmem_limit_bytes=VMEM_LIMIT),
        cost_estimate=cost(16.6),
        name="attend_back",
    )(mask, qkv, logsum, dmix, *earlier, *deps)


def move_kernel(plans, count, deps, where_ref, *refs):
    pieces = refs[:count]
    outs = refs[count + deps : count + deps + len(plans)]
    sem = refs[-1]
    zi, xi, yi = where_ref[0], where_ref[1], where_ref[2]

    def locate(ref, index):
        place = tuple(
            {"z": zi, "x": xi, "y": yi}[item[0]] ^ item[1] if isinstance(item, tuple) else item
            for item in index
        )
        return ref.at[place] if place else ref

    copies = []
    for out, plan in zip(outs, plans):
        for piece, source, target in plan:
            copies.append(
                pltpu.make_async_copy(
                    locate(pieces[piece], source), locate(out, target), sem.at[len(copies)]
                )
            )
    for copy in copies:
        copy.start()
    for copy in copies:
        copy.wait()


def move(where, pieces, shapes, plans, deps=(), name="move"):
    total = sum(len(plan) for plan in plans)
    anywhere = pl.BlockSpec(memory_space=pl.ANY)
    return pl.pallas_call(
        functools.partial(move_kernel, plans, len(pieces), len(deps)),
        in_specs=[pl.BlockSpec(memory_space=pltpu.SMEM)] + [anywhere] * (len(pieces) + len(deps)),
        out_specs=[pl.BlockSpec(memory_space=pltpu.VMEM)] * len(plans),
        out_shape=[jax.ShapeDtypeStruct(shape, pieces[0].dtype) for shape in shapes],
        scratch_shapes=[pltpu.SemaphoreType.DMA((total,))],
        compiler_params=pltpu.CompilerParams(vmem_limit_bytes=VMEM_LIMIT),
        cost_estimate=cost(4.0),
        name=name,
    )(where, *pieces, *deps)


def add_near_kernel(half, where_ref, grads, more, got_x, got_y, *refs):
    send_y, send_x, own, parts, gx, gy, sem = refs[-7:]
    zi, xi, yi = where_ref[0], where_ref[1], where_ref[2]
    lows, highs = pl.ds(0, half), pl.ds(half, half)
    sources = [
        ((lows, xi, 1 - yi), got_x.at[:, 1 - yi], gx.at[0]),
        ((highs, 1 - xi, yi), got_y.at[:, 1 - xi], gy.at[0]),
        ((lows, xi, yi), got_x.at[:, yi], gx.at[1]),
        ((highs, xi, yi), got_y.at[:, xi], gy.at[1]),
    ]
    copies = []
    for number, (place, got_from, got_to) in enumerate(sources):
        pairs = [
            (grads.at[place], parts.at[number, :, pl.ds(0, 3)]),
            (more.at[place], parts.at[number, :, 3]),
            (got_from, got_to),
        ]
        copies.append(
            [
                pltpu.make_async_copy(source, target, sem.at[3 * number + i])
                for i, (source, target) in enumerate(pairs)
            ]
        )
    for group in copies:
        for copy in group:
            copy.start()
    for number in range(4):
        for copy in copies[number]:
            copy.wait()
        got = (gx, gy, gx, gy)[number]
        for k in range(half):
            for i in range(4):
                total = parts[number, k, i].astype(f32) + got[number // 2, k, i].astype(f32)
                if number == 0:
                    send_y[k, i] = total.astype(bf16)
                elif number == 1:
                    send_x[k, i] = total.astype(bf16)
                else:
                    own[(number - 2) * half + k, i] = total


def add_near(where, grads, more, got_x, got_y, deps=()):
    nz, rows, columns = grads.shape[0], *grads.shape[-2:]
    half = nz // 2
    anywhere = pl.BlockSpec(memory_space=pl.ANY)
    inside = pl.BlockSpec(memory_space=pltpu.VMEM)
    return pl.pallas_call(
        functools.partial(add_near_kernel, half),
        in_specs=[pl.BlockSpec(memory_space=pltpu.SMEM)] + [anywhere] * (4 + len(deps)),
        out_specs=[inside] * 3,
        out_shape=[
            jax.ShapeDtypeStruct((half, 4, rows, columns), bf16),
            jax.ShapeDtypeStruct((half, 4, rows, columns), bf16),
            jax.ShapeDtypeStruct((nz, 4, rows, columns), f32),
        ],
        scratch_shapes=[
            pltpu.VMEM((4, half, 4, rows, columns), bf16),
            pltpu.VMEM((2, half, 4, rows, columns), bf16),
            pltpu.VMEM((2, half, 4, rows, columns), bf16),
            pltpu.SemaphoreType.DMA((12,)),
        ],
        compiler_params=pltpu.CompilerParams(vmem_limit_bytes=VMEM_LIMIT),
        cost_estimate=cost(5.4),
        name="add_near",
    )(where, grads, more, got_x, got_y, *deps)


def add_far_kernel(nz, where_ref, own_ref, got_y, got_x, *refs):
    sends, mine = refs[-2:]
    zi = where_ref[0]
    half = nz // 2
    for k in range(nz):
        got = got_y[k] if k < half else got_x[k - half]
        total = own_ref[k] + got.astype(f32)
        distance = zi ^ k

        @pl.when(distance == 0)
        def _():
            mine[...] = total

        @pl.when(distance > 0)
        def _():
            sends[jnp.maximum(distance - 1, 0)] = total.astype(bf16)


def add_far(where, own, got_y, got_x, deps=()):
    nz = own.shape[0]
    inside = pl.BlockSpec(memory_space=pltpu.VMEM)
    return pl.pallas_call(
        functools.partial(add_far_kernel, nz),
        in_specs=[pl.BlockSpec(memory_space=pltpu.SMEM)]
        + [inside] * 3
        + [pl.BlockSpec(memory_space=pl.ANY)] * len(deps),
        out_specs=[inside] * 2,
        out_shape=[
            jax.ShapeDtypeStruct((nz - 1, *own.shape[1:]), bf16),
            jax.ShapeDtypeStruct(own.shape[1:], f32),
        ],
        compiler_params=pltpu.CompilerParams(vmem_limit_bytes=VMEM_LIMIT),
        cost_estimate=cost(3.8),
        name="add_far",
    )(where, own, got_y, got_x, *deps)


def run(us, kernel, grid, ins, outs, args, name, scratch=(), deps=()):
    return pl.pallas_call(
        functools.partial(kernel, len(ins), len(deps)),
        grid=grid,
        in_specs=list(ins) + [pl.BlockSpec(memory_space=pl.ANY)] * len(deps),
        out_specs=[spec for spec, _ in outs],
        out_shape=[shape for _, shape in outs],
        scratch_shapes=list(scratch),
        compiler_params=pltpu.CompilerParams(vmem_limit_bytes=VMEM_LIMIT),
        cost_estimate=cost(us),
        name=name,
    )(*args, *deps)


def split_refs(count, deps, refs):
    return refs[:count], refs[count + deps :]


def fixed(*shape):
    return pl.BlockSpec(shape, lambda i: (0,) * len(shape))


def down(*shape):
    return pl.BlockSpec(shape, lambda i: (i,) + (0,) * (len(shape) - 1))


def across(*shape):
    return pl.BlockSpec(shape, lambda i: (0,) * (len(shape) - 1) + (i,))


def array(dtype, *shape):
    return jax.ShapeDtypeStruct(shape, dtype)


def qkv_kernel(count, deps, *refs):
    (w_ref, mine_ref, other_ref, bias_ref), (out_ref, turned_ref) = split_refs(count, deps, refs)
    step = pl.program_id(0)

    @pl.when(step == 0)
    def _():
        turned_ref[...] = w_ref[...].T

    @pl.when(step < 2)
    def _():
        total = dot(turned_ref[...], mine_ref[...], ((1,), (1,))) + bias_ref[...]
        out_ref[...] = total.astype(bf16)

    @pl.when(step >= 2)
    def _():
        total = dot(turned_ref[...], other_ref[...], ((1,), (1,))) + bias_ref[...]
        out_ref[...] = total.astype(bf16)


def project_qkv(weight, mine, other, bias, deps=()):
    rows, width = mine.shape
    columns = weight.shape[1]
    step = rows // 2
    return run(
        10.4,
        qkv_kernel,
        (4,),
        [
            fixed(width, columns),
            pl.BlockSpec((step, width), lambda i: (jnp.minimum(i, 1), 0)),
            pl.BlockSpec((step, width), lambda i: (jnp.maximum(i - 2, 0), 0)),
            fixed(columns, 1),
        ],
        [(across(columns, step), array(bf16, columns, 2 * rows))],
        (weight, mine, other, bias),
        "project_qkv",
        [pltpu.VMEM((columns, width), bf16)],
        deps,
    )[0]


def multiply_kernel(turn_left, over, count, deps, *refs):
    (left_ref, right_ref), (out_ref,) = split_refs(count, deps, refs)
    left = left_ref[...].T if turn_left else left_ref[...]
    out_ref[...] = dot(left, right_ref[...], ((1,), (over,)))


def multiply(left, right, part, turn_left=False, over=0, deps=()):
    tokens = left.shape[1] if turn_left else left.shape[0]
    inner = left.shape[0] if turn_left else left.shape[1]
    columns = right.shape[1 - over]
    step = tokens // 2
    if turn_left:
        left_spec = pl.BlockSpec((inner, step), lambda i: (0, i + part))
    else:
        left_spec = pl.BlockSpec((step, inner), lambda i: (i + part, 0))
    return run(
        inner * columns / 3.4e5,
        functools.partial(multiply_kernel, turn_left, over),
        (1,),
        [left_spec, fixed(*right.shape)],
        [(down(step, columns), array(f32, tokens // 2, columns))],
        (left, right),
        "multiply",
        (),
        deps,
    )[0]


def fc1_kernel(count, deps, *refs):
    (mine_ref, other_ref, w_ref, bias_ref), (slope_ref, hidden_ref) = split_refs(count, deps, refs)
    rows = mine_ref.shape[0]
    factor = math.sqrt(2.0 / math.pi)
    for part, ref in enumerate((mine_ref, other_ref)):
        pre = dot(ref[...], w_ref[...], ((1,), (0,))) + bias_ref[...]
        square = pre * pre
        bent = jnp.tanh(pre * (factor + (factor * 0.044715) * square))
        share = 0.5 + 0.5 * bent
        slope = share + (0.5 * pre) * (1.0 - bent * bent) * (
            factor + (3.0 * 0.044715 * factor) * square
        )
        slope_ref[part * rows : (part + 1) * rows] = slope
        hidden_ref[part * rows : (part + 1) * rows] = (pre * share).astype(bf16)


def fc1(mine, other, weight, bias, deps=()):
    rows, width = mine.shape
    columns = weight.shape[1]
    step = 384
    return run(
        16.0,
        fc1_kernel,
        (columns // step,),
        [fixed(rows, width)] * 2 + [across(width, step), across(1, step)],
        [
            (across(2 * rows, step), array(f32, 2 * rows, columns)),
            (across(2 * rows, step), array(bf16, 2 * rows, columns)),
        ],
        (mine, other, weight, bias),
        "fc1",
        (),
        deps,
    )


def fc2_back_kernel(count, deps, *refs):
    (mine_ref, other_ref, w_ref, slope_ref), (out_ref, sums_ref) = split_refs(count, deps, refs)
    rows = mine_ref.shape[0]
    total = 0.0
    for part, ref in enumerate((mine_ref, other_ref)):
        d_hidden = dot(ref[...], w_ref[...], ((1,), (1,)))
        d_pre = (d_hidden * slope_ref[part * rows : (part + 1) * rows]).astype(bf16)
        out_ref[part * rows : (part + 1) * rows] = d_pre
        total = total + jnp.sum(d_pre.astype(f32), 0, keepdims=True)
    sums_ref[...] = total


def fc2_back(mine, other, weight, slope, deps=()):
    rows, width = mine.shape
    columns = weight.shape[0]
    step = 384
    return run(
        13.9,
        fc2_back_kernel,
        (columns // step,),
        [fixed(rows, width)] * 2 + [down(step, width), across(2 * rows, step)],
        [
            (across(2 * rows, step), array(bf16, 2 * rows, columns)),
            (across(1, step), array(f32, 1, columns)),
        ],
        (mine, other, weight, slope),
        "fc2_back",
        (),
        deps,
    )


def fc2_grad_kernel(count, deps, *refs):
    (hidden_ref, mine_ref, other_ref), (out_ref,) = split_refs(count, deps, refs)
    rows = mine_ref.shape[0]
    turned = hidden_ref[...].T
    total = dot(turned[:, :rows], mine_ref[...], ((1,), (0,)))
    total = total + dot(turned[:, rows:], other_ref[...], ((1,), (0,)))
    out_ref[...] = total.astype(bf16)


def fc2_grad(hidden, mine, other, deps=()):
    tokens, columns = hidden.shape
    rows, width = mine.shape
    step = 384
    return run(
        10.7,
        fc2_grad_kernel,
        (columns // step,),
        [across(tokens, step)] + [fixed(rows, width)] * 2,
        [(down(step, width), array(bf16, columns, width))],
        (hidden, mine, other),
        "fc2_grad",
        (),
        deps,
    )[0]


def fc1_grad_kernel(count, deps, *refs):
    (mine_ref, other_ref, right_ref), (out_ref, turned_ref) = split_refs(count, deps, refs)
    z = pl.program_id(0)
    rows = out_ref.shape[2]
    half = mine_ref.shape[0]

    @pl.when(z == 0)
    def _():
        shape = (*turned_ref.shape[:2], half)
        turned_ref[:, :, :half] = mine_ref[...].T.reshape(shape)
        turned_ref[:, :, half:] = other_ref[...].T.reshape(shape)

    total = dot(turned_ref[z], right_ref[...], ((1,), (0,))).astype(bf16)
    for k in range(4):
        out_ref[k, 0] = total[k * rows : (k + 1) * rows]


def fc1_grad(mine, other, right, nz, deps=()):
    half, width = mine.shape
    tokens, columns = right.shape
    rows = width // (4 * nz)
    return run(
        11.4,
        fc1_grad_kernel,
        (nz,),
        [fixed(half, width)] * 2 + [fixed(tokens, columns)],
        [
            (
                pl.BlockSpec((4, 1, rows, columns), lambda z: (0, z, 0, 0)),
                array(bf16, 4, nz, rows, columns),
            )
        ],
        (mine, other, right),
        "fc1_grad",
        [pltpu.VMEM((nz, 4 * rows, tokens), bf16)],
        deps,
    )[0]


def qkv_grad_kernel(count, deps, *refs):
    (mine_ref, other_ref, right_ref), (out_ref,) = split_refs(count, deps, refs)
    half = mine_ref.shape[0]
    total = dot(mine_ref[...].T, right_ref[:, :half], ((1,), (1,)))
    total = total + dot(other_ref[...].T, right_ref[:, half:], ((1,), (1,)))
    out_ref[...] = total.astype(bf16)


def qkv_grad(mine, other, right, deps=()):
    half, width = mine.shape
    columns, tokens = right.shape
    step = 384
    return run(
        8.5,
        qkv_grad_kernel,
        (width // step,),
        [across(half, step)] * 2 + [fixed(columns, tokens)],
        [(down(step, columns), array(bf16, width, columns))],
        (mine, other, right),
        "qkv_grad",
        (),
        deps,
    )[0]


def proj_back_kernel(count, deps, *refs):
    (w_ref, mixed_ref, mine_ref, other_ref), (back_ref, grad_ref) = split_refs(count, deps, refs)
    half = mine_ref.shape[0]
    back_ref[:, :half] = dot(w_ref[...], mine_ref[...], ((1,), (1,))).astype(bf16)
    back_ref[:, half:] = dot(w_ref[...], other_ref[...], ((1,), (1,))).astype(bf16)
    total = dot(mixed_ref[:, :half], mine_ref[...], ((1,), (0,)))
    total = total + dot(mixed_ref[:, half:], other_ref[...], ((1,), (0,)))
    grad_ref[...] = total.astype(bf16)


def proj_back(weight, mixed, mine, other, deps=()):
    inner, tokens = mixed.shape
    half, width = mine.shape
    step = inner // 2
    return run(
        6.4,
        proj_back_kernel,
        (2,),
        [down(step, width), down(step, tokens)] + [fixed(half, width)] * 2,
        [
            (down(step, tokens), array(bf16, inner, tokens)),
            (down(step, width), array(bf16, inner, width)),
        ],
        (weight, mixed, mine, other),
        "proj_back",
        (),
        deps,
    )


def lane_sums_kernel(count, deps, *refs):
    (value_ref,), (out_ref,) = split_refs(count, deps, refs)
    out_ref[...] = jnp.sum(value_ref[...].astype(f32), 1, keepdims=True)


def lane_sums(value, deps=()):
    rows, width = value.shape
    return run(
        3.4,
        lane_sums_kernel,
        (1,),
        [fixed(rows, width)],
        [(fixed(rows, 1), array(f32, rows, 1))],
        (value,),
        "lane_sums",
        (),
        deps,
    )[0]


def sum_blocks_kernel(count, deps, *refs):
    ins, (out_ref,) = split_refs(count, deps, refs)
    out_ref[...] = sum((ref[...].astype(f32) for ref in ins[1:]), ins[0][...].astype(f32))


def sum_blocks(mine, got, deps=()):
    shape = mine.shape
    return run(
        3.0,
        sum_blocks_kernel,
        (1,),
        [fixed(*shape)] * (1 + len(got)),
        [(fixed(*shape), array(f32, *shape))],
        (mine, *got),
        "sum_blocks",
        (),
        deps,
    )[0]


ROWS = 128


def middle_kernel(count, deps, *refs):
    (vec_ref, mine_ref, got_ref, x_ref), (attn_ref, mid_ref, mlp_ref) = split_refs(
        count, deps, refs
    )
    attn = mine_ref[...] + got_ref[...] + vec_ref[6:7]
    mid = x_ref[...] + vec_ref[2:3] * attn
    normed, _ = normalize(mid)
    attn_ref[...] = attn
    mid_ref[...] = mid
    mlp_ref[...] = (normed * (1.0 + vec_ref[4:5]) + vec_ref[3:4]).astype(bf16)


def middle(vec, mine, got, x_in, deps=()):
    rows, width = mine.shape
    block = down(ROWS, width)
    return run(
        6.2,
        middle_kernel,
        (rows // ROWS,),
        [fixed(8, width)] + [block] * 3,
        [
            (block, array(f32, rows, width)),
            (block, array(f32, rows, width)),
            (block, array(bf16, rows, width)),
        ],
        (vec, mine, got, x_in),
        "middle",
        (),
        deps,
    )


def add_sums(sums_ref, values):
    @pl.when(pl.program_id(0) == 0)
    def _():
        sums_ref[...] = jnp.zeros_like(sums_ref)

    for number, value in enumerate(values):
        sums_ref[number : number + 1] += jnp.sum(value, 0, keepdims=True)


def valid_cotangent(valid_ref, cot_ref):
    row = pl.program_id(0) * ROWS + lax.broadcasted_iota(jnp.int32, (ROWS, 1), 0)
    return jnp.where(row < valid_ref[0], cot_ref[...].astype(f32), 0.0)


def middle_back_kernel(count, deps, *refs):
    (valid_ref, vec_ref, mine_ref, got_ref, cot_ref, mid_ref, attn_ref), (
        d_mid_ref,
        d_attn_ref,
        sums_ref,
    ) = split_refs(count, deps, refs)
    d_mlp = mine_ref[...] + got_ref[...]
    normed, spread = normalize(mid_ref[...])
    d_mid = valid_cotangent(valid_ref, cot_ref) + norm_back(
        normed, spread, d_mlp * (1.0 + vec_ref[4:5])
    )
    d_attn = (vec_ref[2:3] * d_mid).astype(bf16)
    d_mid_ref[...] = d_mid
    d_attn_ref[...] = d_attn
    add_sums(sums_ref, (d_mlp, d_mlp * normed, d_mid * attn_ref[...], d_attn.astype(f32)))


def middle_back(valid, vec, mine, got, cot, mid, attn, deps=()):
    rows, width = mine.shape
    block = down(ROWS, width)
    return run(
        7.5,
        middle_back_kernel,
        (rows // ROWS,),
        [pl.BlockSpec(memory_space=pltpu.SMEM), fixed(8, width)] + [block] * 5,
        [
            (block, array(f32, rows, width)),
            (block, array(bf16, rows, width)),
            (fixed(8, width), array(f32, 8, width)),
        ],
        (valid, vec, mine, got, cot, mid, attn),
        "middle_back",
        (),
        deps,
    )


def finish_first_kernel(count, deps, *refs):
    (vec_ref, mine_ref, got_ref, d_mid_ref, x_ref), (grad_ref, sums_ref) = split_refs(
        count, deps, refs
    )
    d_attn_in = mine_ref[...] + got_ref[...]
    normed, spread = normalize(x_ref[...])
    grad_ref[...] = (
        d_mid_ref[...] + norm_back(normed, spread, d_attn_in * (1.0 + vec_ref[1:2]))
    ).astype(bf16)
    add_sums(sums_ref, (d_attn_in, d_attn_in * normed))


def finish_first(vec, mine, got, d_mid, x_in, deps=()):
    rows, width = mine.shape
    block = down(ROWS, width)
    return run(
        6.2,
        finish_first_kernel,
        (rows // ROWS,),
        [fixed(8, width)] + [block] * 4,
        [
            (block, array(bf16, rows, width)),
            (fixed(8, width), array(f32, 8, width)),
        ],
        (vec, mine, got, d_mid, x_in),
        "finish_first",
        (),
        deps,
    )


def finish_last_kernel(count, deps, *refs):
    (valid_ref, vec_ref, mine_ref, got_ref, cot_ref, mid_ref), (out_ref, sums_ref) = split_refs(
        count, deps, refs
    )
    branch = mine_ref[...] + got_ref[...] + vec_ref[7:8]
    out_ref[...] = (mid_ref[...] + vec_ref[5:6] * branch).astype(bf16)
    add_sums(sums_ref, (valid_cotangent(valid_ref, cot_ref) * branch,))


def finish_last(valid, vec, mine, got, cot, mid, deps=()):
    rows, width = mine.shape
    block = down(ROWS, width)
    return run(
        5.3,
        finish_last_kernel,
        (rows // ROWS,),
        [pl.BlockSpec(memory_space=pltpu.SMEM), fixed(8, width)] + [block] * 4,
        [
            (block, array(bf16, rows, width)),
            (fixed(8, width), array(f32, 8, width)),
        ],
        (valid, vec, mine, got, cot, mid),
        "finish_last",
        (),
        deps,
    )


def adam_kernel(layout, rate, scalar_ref, *refs):
    grads, (w_ref, m_ref, v_ref), (new_w, new_m, new_v) = refs[:-6], refs[-6:-3], refs[-3:]
    factor = scalar_ref[0]
    column = 0
    if layout is None:
        pieces = [(0, 0, w_ref.shape[1])]
    else:
        pieces = layout
    swap = scalar_ref[1] > 0.5
    for part, first, width in pieces:
        if layout is None:
            grad = grads[0][...].astype(f32)
        else:
            here = slice(first, first + width)
            grad = jnp.where(
                swap, grads[1 - part][:, here].astype(f32), grads[part][:, here].astype(f32)
            )
        place = (slice(None), slice(column, column + width))
        weight, moment, second = adam_step(
            w_ref[place], m_ref[place], v_ref[place], grad, factor, rate
        )
        new_w[place], new_m[place], new_v[place] = weight, moment, second
        column += width


def adam(weight, first, second, grads, scalars, rate, layout=None):
    inside = pl.BlockSpec(memory_space=pltpu.VMEM)
    shape = jax.ShapeDtypeStruct(weight.shape, f32)
    return pl.pallas_call(
        functools.partial(adam_kernel, layout, rate),
        in_specs=[pl.BlockSpec(memory_space=pltpu.SMEM)] + [inside] * (len(grads) + 3),
        out_specs=[inside] * 3,
        out_shape=[shape] * 3,
        compiler_params=pltpu.CompilerParams(vmem_limit_bytes=VMEM_LIMIT),
        cost_estimate=cost(4.0),
        name="adam",
    )(scalars, *grads, weight, first, second)


def after_kernel(value_ref, *refs):
    refs[-1][...] = value_ref[...]


def after(value, *deps):
    flat = value.reshape(-1, value.shape[-1])
    return pl.pallas_call(
        after_kernel,
        in_specs=[pl.BlockSpec(memory_space=pltpu.VMEM)]
        + [pl.BlockSpec(memory_space=pl.ANY)] * len(deps),
        out_specs=pl.BlockSpec(memory_space=pltpu.VMEM),
        out_shape=jax.ShapeDtypeStruct(flat.shape, flat.dtype),
        compiler_params=pltpu.CompilerParams(vmem_limit_bytes=VMEM_LIMIT),
        cost_estimate=cost(1.5),
        name="after",
    )(flat, *deps).reshape(value.shape)


class Group:
    def __init__(self, n):
        self.n = n
        self.nz = n // 8
        self.me = lax.axis_index(AXES).astype(jnp.int32)
        self.y = self.me & 1
        self.c = (self.me >> 1) & 1
        self.x = (self.me >> 2) & 1
        self.z = self.me >> 3
        self.where = jnp.stack([self.z, self.x, self.y])

    def xor(self, value, mask):
        return lax.ppermute(value, AXES, [(i, i ^ mask) for i in range(self.n)])

    def core(self, value):
        return self.xor(value, 2)

    def turn(self, value):
        got = lax.ppermute(
            value,
            AXES,
            [(i, i ^ 3) for i in range(self.n) if (i & 3) in (1, 2)],
        )
        return jnp.where(self.c == self.y, value, got)

    def turn_other(self, value):
        return lax.ppermute(
            value,
            AXES,
            [(i, (i & ~3) | ((1 - (i & 1)) << 1) | ((i >> 1) & 1)) for i in range(self.n)],
        )

    def turn_other_back(self, value):
        return lax.ppermute(
            value,
            AXES,
            [(i, (i & ~3) | ((i & 1) << 1) | (1 - ((i >> 1) & 1))) for i in range(self.n)],
        )

    def to_block(self, parts):
        mine = lax.dynamic_index_in_dim(parts, self.y, 0, False)
        other = lax.dynamic_index_in_dim(parts, 1 - self.y, 0, False)
        got_a, got_b = self.turn(mine), self.turn_other(other)
        straight = self.c == 0
        return jnp.concatenate(
            [jnp.where(straight, got_a, got_b), jnp.where(straight, got_b, got_a)], 0
        )

    def from_block(self, block):
        rows = block.shape[0] // 2
        pieces = block.reshape(2, rows, block.shape[1])
        got_a = self.turn(lax.dynamic_index_in_dim(pieces, self.c, 0, False))
        got_b = self.turn_other_back(lax.dynamic_index_in_dim(pieces, 1 - self.c, 0, False))
        return got_a, got_b

    def gather_z(self, block):
        return [block] + [self.xor(block, d << 3) for d in range(1, self.nz)]

    def gather_near(self, pieces, deps=()):
        half = self.nz // 2
        plans = [
            [(k, (), (k,)) for k in range(half)],
            [(half + k, (), (k,)) for k in range(half)],
        ]
        shape = (half, *pieces[0].shape)
        low, high = move(self.where, pieces, [shape] * 2, plans, deps, "stack_z")
        return low, high, self.xor(low, 1), self.xor(high, 4)

    def gather_far(self, near, deps=()):
        half = self.nz // 2
        low, high, low_y, high_x = near
        plans = [[(0, (), (0,)), (2, (), (1,))], [(1, (), (0,)), (3, (), (1,))]]
        shape = (2, *low.shape)
        low_2, high_2 = move(self.where, near, [shape] * 2, plans, deps, "stack_near")
        return low_2, high_2, self.xor(low_2, 4), self.xor(high_2, 1)

    def gather_end(self, far, deps=(), cuts=((),), shapes=None, order="zxy"):
        nz, half = self.nz, self.nz // 2
        plans = []
        for cut in cuts:
            plan = []
            for k in range(half):
                for other in range(2):
                    for piece, target in (
                        (0, (("z", k), ("x", 0), ("y", other))),
                        (1, (("z", half + k), ("x", other), ("y", 0))),
                        (2, (("z", k), ("x", 1), ("y", other))),
                        (3, (("z", half + k), ("x", other), ("y", 1))),
                    ):
                        target = tuple(dict((t[0], t) for t in target)[axis] for axis in order)
                        plan.append((piece, (other, k, *cut), target))
            plans.append(plan)
        lead = tuple({"z": nz}.get(axis, 2) for axis in order)
        shapes = [(*lead, *shape) for shape in shapes or [far[0].shape[2:]]]
        return move(self.where, far, shapes, plans, deps, "place")

    def scatter_z(self, blocks, deps=()):
        nz = self.nz
        plans = [[(0, (("z", d),), ())] for d in range(nz)]
        parts = move(self.where, [blocks], [blocks.shape[1:]] * nz, plans, deps, "split_z")
        return parts, [self.xor(parts[d], d << 3) for d in range(1, nz)]

    def sum_z(self, state):
        parts, got = state
        return sum((item.astype(f32) for item in got), parts[0].astype(f32))

    def scatter_start(self, grads, deps=()):
        half = self.nz // 2
        plans = [[], []]
        for k in range(half):
            for other in range(2):
                for piece, cut in ((0, pl.ds(0, 3)), (1, 3)):
                    plans[0].append((piece, (k, ("x", 1), other), (k, other, cut)))
                    plans[1].append((piece, (half + k, other, ("y", 1)), (k, other, cut)))
        shape = (half, 2, 4, *grads[1].shape[3:])
        to_x, to_y = move(self.where, grads, [shape] * 2, plans, deps, "split")
        return grads, self.xor(to_x, 4), self.xor(to_y, 1), to_x

    def scatter_near(self, state, deps=()):
        grads, got_x, got_y = state[:3]
        send_y, send_x, own = add_near(self.where, *grads, got_x, got_y, deps)
        return own, self.xor(send_y, 1), self.xor(send_x, 4)

    def scatter_far(self, state, deps=()):
        sends, mine = add_far(self.where, *state, deps)
        return mine, [self.xor(sends[d - 1], d << 3) for d in range(1, self.nz)]

    def scatter_end(self, state):
        mine, got = state
        return sum((item.astype(f32) for item in got), mine)

    def all_sum(self, value):
        value = value + self.core(value)
        value = value + self.xor(value, 1)
        value = value + self.xor(value, 4)
        return sum((self.xor(value, d << 3) for d in range(1, self.nz)), value)


def per_device(
    tokens,
    embedding,
    heights,
    widths,
    cotangent,
    w_qkv,
    w_proj,
    w_fc1,
    w_fc2,
    w_ada,
    biases,
    m_qkv,
    m_proj,
    m_fc1,
    m_fc2,
    m_ada,
    m_bias,
    v_qkv,
    v_proj,
    v_fc1,
    v_fc2,
    v_ada,
    v_bias,
):
    rows = tokens.shape[1]
    n = math.prod(lax.axis_size(axis) for axis in AXES)
    own_rows = w_qkv.shape[0]
    g = Group(n)
    nz = g.nz
    groups = n // 4
    pair = 2 * own_rows
    ff_rows = w_fc2.shape[0]
    bias_rows = biases.shape[0]

    qkv_parts = (
        w_qkv.astype(bf16)
        .reshape(own_rows, 3, 2, HALF, 2, HEAD_DIM)
        .transpose(4, 0, 2, 1, 3, 5)
        .reshape(2, own_rows, QKV)
    )
    third = own_rows * D // QKV
    qp_block = jnp.concatenate(
        [g.to_block(qkv_parts), w_proj.astype(bf16).reshape(third, QKV)], 0
    ).reshape(4, third, QKV)
    qp_z = g.gather_z(qp_block)
    tokens_here = g.turn(after(tokens[0], qp_block))
    cotangent_here = g.turn(after(cotangent[0], tokens_here))
    cond_row = jax.nn.silu(embedding[0]).astype(bf16).reshape(groups * 2, 2, own_rows)
    cond_row = lax.dynamic_index_in_dim(cond_row, g.y, 1, False)
    small = jnp.concatenate([biases.astype(bf16), heights.astype(bf16), widths.astype(bf16)])
    small = jnp.concatenate(
        [cond_row, jnp.broadcast_to(small[None], (groups * 2, bias_rows + 2))], 1
    )
    small = jnp.pad(small, ((0, 0), (0, -small.shape[1] % 128)))
    small = lax.all_to_all(small, ("z", "x", "core"), 0, 0, tiled=True)
    conds_own = small[:, :own_rows]
    small_other = g.xor(small, 1)
    low = g.y == 0
    natural = jnp.stack(
        [jnp.where(low, small, small_other), jnp.where(low, small_other, small)], 1
    ).reshape(n, -1)[:, own_rows:].astype(f32)
    mod_part = dot(conds_own, w_ada.astype(bf16), ((1,), (0,)))
    mod_sum = jnp.sum(
        lax.all_to_all(mod_part, ("z", "x", "y"), 0, 0, tiled=True), 0, keepdims=True
    )
    mod_sum = mod_sum + g.core(mod_sum)
    qp_near = g.gather_near(qp_z, [tokens_here, mod_sum])
    fc1_parts = (
        w_fc1.astype(bf16)
        .reshape(own_rows, nz, 2, 2, 2, ff_rows)
        .transpose(3, 0, 2, 4, 1, 5)
        .reshape(2, own_rows, OWN_FF)
    )
    fc1_block = g.to_block(after(fc1_parts, qp_block))
    ff_block = jnp.concatenate(
        [
            fc1_block.reshape(2 * own_rows, 2, D).swapaxes(0, 1).reshape(-1, D),
            w_fc2.astype(bf16),
        ]
    )
    ff_all = lax.all_gather(after(ff_block, qp_near[0]), ("x", "y", "z"), axis=0, tiled=True)
    ff_all = ff_all.reshape(2, 2, nz, 4, 2 * own_rows, D)
    qp_far = g.gather_far(qp_near)
    bias_full = natural[:, :bias_rows].reshape(-1)
    bias_qkv = bias_full[: 3 * D]
    bias_proj = bias_full[3 * D : 4 * D]
    bias_fc1 = bias_full[4 * D : 4 * D + FF]
    bias_fc2 = bias_full[4 * D + FF : 5 * D + FF]
    bias_ada = bias_full[5 * D + FF :]
    image_row = lax.dynamic_index_in_dim(natural, (g.me & ~3) | (g.y << 1), 0, True)
    image_row = after(image_row, qp_far[0])[0]
    height = image_row[bias_rows].astype(jnp.int32)
    width = image_row[bias_rows + 1].astype(jnp.int32)
    modul = mod_sum + bias_ada
    shift1, scale1, gate1, shift2, scale2, gate2 = [
        modul[:, j * D : (j + 1) * D] for j in range(6)
    ]

    vec = jnp.concatenate([modul.reshape(6, D), bias_proj[None], bias_fc2[None]])

    slots = g.c * rows + jnp.arange(rows, dtype=jnp.int32)
    count = height * width
    valid_rows = (slots < count).astype(f32)[:, None]
    seq = 2 * rows
    cut = jnp.where(count < seq, -1e30, 0.0).astype(f32)
    mask = jnp.stack([jnp.where(g.c == 1, cut, 0.0), jnp.where(g.c == 0, cut, 0.0)])
    valid = jnp.clip(count - g.c * rows, 0, rows).astype(jnp.int32)[None]
    x_in = tokens_here.astype(f32) + position_rows(slots, width)
    normed1, spread1 = normalize(x_in)
    attn_in = (normed1 * (1.0 + scale1) + shift1).astype(bf16)
    d_out = cotangent_here.astype(f32) * valid_rows
    d_branch = (gate2 * d_out).astype(bf16)
    gb_fc2 = jnp.sum(d_branch.astype(f32), 0, keepdims=True)
    attn_sib = g.core(attn_in)
    qkv_w = g.gather_end(qp_far, [attn_in], ((pl.ds(0, 3),),), ((3, third, QKV),))[0]
    qkv_w = qkv_w.reshape(D, QKV)
    own_bias_qkv = lax.dynamic_index_in_dim(
        bias_qkv.reshape(3, 2, HALF, 2, HEAD_DIM), g.c, 3, False
    ).swapaxes(0, 1).reshape(-1, 1)
    qkv = project_qkv(qkv_w, attn_in, attn_sib, own_bias_qkv)
    qkv = qkv.reshape(2, 3, HALF, HEAD_DIM, seq)
    first = attend(0, qkv, mask)
    proj_own = g.gather_end(qp_far, first[1:], ((3,),), ((third, QKV),))[0].reshape(-1, D)
    heads_match = pair % HEAD_DIM == 0
    if heads_match:
        proj_w = proj_own
    else:
        mine = proj_own.reshape(groups, pair, D)
        theirs = g.core(mine)
        own_first = g.c == 0
        whole = jnp.stack(
            [jnp.where(own_first, mine, theirs), jnp.where(own_first, theirs, mine)], 1
        ).reshape(OWN_HEADS, 2, HEAD_DIM, D)
        proj_w = lax.dynamic_index_in_dim(whole, g.c, 1, False).reshape(OWN_HEADS * HEAD_DIM, D)
    mixed, logsum = attend(1, qkv, mask, first, [proj_w])
    mixed = mixed.reshape(OWN_HEADS * HEAD_DIM, seq)
    attn_got = g.core(dot(mixed[:, rows:], proj_w, ((0,), (0,))))
    attn_mine = dot(mixed[:, :rows], proj_w, ((0,), (0,)))
    attn, x_mid, mlp_in = middle(vec, attn_mine, attn_got, x_in)
    mlp_got = g.core(mlp_in)
    own_bias_fc1 = lax.dynamic_index_in_dim(
        bias_fc1.reshape(nz, 2, 2, 2, ff_rows), g.c, 2, False
    ).transpose(1, 2, 0, 3).reshape(-1)
    plan = [
        (0, (x, y, z, h), (z, x, y, slice(None), pl.ds(h * D, D)))
        for x in range(2)
        for y in range(2)
        for z in range(nz)
        for h in range(2)
    ]
    fc1_w = move(
        g.where, [ff_all], [(nz, 2, 2, 2 * own_rows, OWN_FF)], [plan], [mlp_in], "place_fc1"
    )[0].reshape(D, OWN_FF)
    slope, hidden = fc1(mlp_in, mlp_got, fc1_w, own_bias_fc1[None])
    branch_got = g.core(d_branch)
    g_fc2 = fc2_grad(hidden, d_branch, branch_got)
    red_fc2 = lax.psum_scatter(g_fc2, ("x", "y"), scatter_dimension=0, tiled=True)
    plan = [
        (0, (x, y, z, pl.ds(2, 2)), (x, y, z)) for x in range(2) for y in range(2) for z in range(nz)
    ]
    fc2_w = move(
        g.where, [ff_all], [(2, 2, nz, 2, 2 * own_rows, D)], [plan], [g_fc2], "place_fc2"
    )[0].reshape(OWN_FF, D)
    d_pre, gb_fc1 = fc2_back(d_branch, branch_got, fc2_w, slope, [g_fc2])
    d_mlp_got = g.core(dot(d_pre[rows:], fc1_w, ((1,), (1,))))
    d_mlp_mine = dot(d_pre[:rows], fc1_w, ((1,), (1,)))
    g_fc1 = fc1_grad(mlp_in, mlp_got, d_pre, nz, [d_mlp_mine]).reshape(D, OWN_FF)
    red_fc1 = lax.psum_scatter(g_fc1, ("x", "y"), scatter_dimension=0, tiled=True)
    d_mid, d_attn, middle_sums = middle_back(
        valid, vec, d_mlp_mine, d_mlp_got, cotangent_here, x_mid, attn
    )
    d_attn_got = g.core(d_attn)
    d_mixed, g_proj = proj_back(proj_w, mixed, d_attn, d_attn_got)
    if heads_match:
        g_proj = g_proj.reshape(nz, 2, 2, third, QKV)
    else:
        own = (jnp.arange(2) == g.c)[None, :, None, None]
        whole = jnp.where(own, g_proj.reshape(OWN_HEADS, 1, HEAD_DIM, D), 0).reshape(
            groups, 2, pair, D
        )
        theirs = g.core(lax.dynamic_index_in_dim(whole, 1 - g.c, 1, False))
        mine = lax.dynamic_index_in_dim(whole, g.c, 1, False)
        g_proj = (mine.astype(f32) + theirs.astype(f32)).astype(bf16).reshape(nz, 2, 2, third, QKV)
    d_mixed = d_mixed.reshape(OWN_HEADS, HEAD_DIM, seq)
    d_qkv = attend_back(0, qkv, logsum, d_mixed, mask, (), [g_proj])
    fc2_state = g.scatter_z(red_fc2.reshape(nz, -1, D), [d_qkv])
    d_qkv = attend_back(1, qkv, logsum, d_mixed, mask, [d_qkv], [fc2_state[0][0]])
    d_qkv = d_qkv.reshape(QKV, seq)
    red_fc1 = lax.psum_scatter(after(red_fc1, d_qkv), "z", scatter_dimension=0, tiled=True)
    g_qkv = qkv_grad(attn_in, attn_sib, d_qkv)
    red_fc2 = sum_blocks(fc2_state[0][0], fc2_state[1], [g_qkv])
    qkv_state = g.scatter_start([g_qkv.reshape(nz, 2, 2, 3, third, QKV), g_proj], [red_fc2])
    d_attn_in = multiply(d_qkv, qkv_w, 1, True, 1, [qkv_state[3]])
    d_attn_in_got = g.core(d_attn_in)
    d_attn_in = multiply(d_qkv, qkv_w, 0, True, 1, [d_attn_in])
    gb_qkv = lane_sums(d_qkv, [d_attn_in])
    grad_tokens, first_sums = finish_first(
        vec, d_attn_in, d_attn_in_got, d_mid, x_in, [gb_qkv, red_fc1]
    )
    qkv_state = g.scatter_near(qkv_state, [first_sums])
    branch = multiply(hidden, fc2_w, 1, deps=[qkv_state[0]])
    branch_got = g.core(branch)
    branch = multiply(hidden, fc2_w, 0, deps=[branch])
    qkv_state = g.scatter_far(qkv_state, [branch])
    output, last_sums = finish_last(
        valid, vec, branch, branch_got, cotangent_here, x_mid, [qkv_state[0]]
    )
    red_qp = sum_blocks(qkv_state[0], qkv_state[1], [last_sums])
    fc1_parts = g.from_block(after(red_fc1, red_qp))

    own = (jnp.arange(2) == g.c)[None, :, None]
    gb_qkv = gb_qkv.reshape(2, 3, HALF, HEAD_DIM).swapaxes(0, 1)
    gb_qkv = jnp.where(own, gb_qkv.reshape(3 * OWN_HEADS, 1, HEAD_DIM), 0.0).reshape(3, D)
    gb_fc1 = gb_fc1.reshape(2, 2, nz, ff_rows).transpose(2, 0, 1, 3)
    gb_fc1 = jnp.where(own, gb_fc1.reshape(groups, 1, 2 * ff_rows), 0.0).reshape(-1, D)
    vector = jnp.concatenate(
        [
            gb_qkv,
            middle_sums[3:4],
            gb_fc1,
            gb_fc2,
            first_sums[:2],
            middle_sums[2:3],
            middle_sums[:2],
            last_sums[:1],
        ]
    )
    vector = after(vector, red_qp)
    vector = vector + g.core(vector)
    plain = vector.shape[0] - 6
    others = [g.xor(vector, d << 3) for d in range(1, nz)]
    sums = sum((item[:plain] for item in others), vector[:plain])
    mods = jnp.stack([vector[plain:]] + [item[plain:] for item in others])[:, None]
    for bit in (1, 4):
        packed = jnp.concatenate([sums, mods.reshape(-1, D)])
        packed = g.xor(packed, bit)
        sums = sums + packed[:plain]
        mods = jnp.stack([mods, packed[plain:].reshape(mods.shape)], 1)
    mods = mods.reshape(groups * 2, 6 * D)
    place_of = (g.z * 2 + g.x) * 2 + g.y
    order = jnp.arange(groups * 2)[None, :] == (jnp.arange(groups * 2)[:, None] ^ place_of)
    conds_own = dot(order.astype(bf16), conds_own, ((1,), (0,)))
    red_ada = lax.dot_general(
        conds_own.astype(f32),
        mods,
        (((0,), (0,)), ((), ())),
        precision=lax.Precision.HIGHEST,
        preferred_element_type=f32,
    )
    g_bias = jnp.concatenate([sums.reshape(-1), jnp.sum(mods, 0)])
    red_bias = lax.dynamic_slice_in_dim(g_bias, g.me * bias_rows, bias_rows)

    red_qkv = red_qp[:3].reshape(2 * own_rows, QKV)
    red_proj = red_qp[3].reshape(own_rows, D)
    output = g.turn(after(output, sums))[None]
    grad_tokens = g.turn(after(grad_tokens, sums))[None]
    squares = sum(
        (
            jnp.sum(jnp.square(piece.astype(f32)))
            for piece in (red_qp, red_fc1, red_fc2, red_ada, red_bias)
        )
    )
    squares = g.all_sum(jnp.broadcast_to(squares, (1, 128)))[0, 0]
    red_qkv = g.from_block(red_qkv)
    grad_norm = jnp.sqrt(squares)
    factor = jnp.minimum(1.0, clip_limit / grad_norm)
    scalars = jnp.stack([factor, g.y.astype(f32)])
    piece = HALF * HEAD_DIM
    qkv_layout = [
        (c, (hh * 3 + kind) * piece + head * HEAD_DIM, HEAD_DIM)
        for kind in range(3)
        for hh in range(2)
        for head in range(HALF)
        for c in range(2)
    ]
    fc1_layout = [
        (c, ((x * 2 + y) * nz + z) * ff_rows, ff_rows)
        for z in range(nz)
        for x in range(2)
        for c in range(2)
        for y in range(2)
    ]
    results = [
        adam(w_qkv, m_qkv, v_qkv, red_qkv, scalars, learn_rate, qkv_layout),
        adam(w_proj, m_proj, v_proj, [red_proj], scalars, learn_rate),
        adam(w_fc1, m_fc1, v_fc1, fc1_parts, scalars, learn_rate, fc1_layout),
        adam(w_fc2, m_fc2, v_fc2, [red_fc2], scalars, learn_rate),
        adam(w_ada, m_ada, v_ada, [red_ada], scalars, learn_rate),
        adam_step(biases, m_bias, v_bias, red_bias, factor, bias_rate),
    ]
    return (
        output,
        grad_tokens,
        grad_norm,
        *[item[0] for item in results],
        *[item[1] for item in results],
        *[item[2] for item in results],
    )


def solution(mesh):
    count = mesh.devices.size
    fine = jax.sharding.Mesh(mesh.devices.reshape(count // 8, 2, 2, 2), AXES)
    image = ("z", "x", "core")
    patches = P(image, "y", None)
    state = (P(AXES, None),) * 5 + (P(AXES),)
    return jax.shard_map(
        per_device,
        mesh=fine,
        in_specs=(patches, P(image, None), P(image), P(image), patches, *state, *state, *state),
        out_specs=(patches, patches, P(), *state, *state, *state),
        check_vma=False,
    )
```

```python
import functools
import math

import jax
import jax.numpy as jnp
from jax import lax
from jax.experimental import pallas as pl
from jax.experimental.pallas import tpu as pltpu
from jax.sharding import PartitionSpec as P

D = 1152
HEADS = 16
HEAD_DIM = 72
FF = 4608
STEPS = 10
OWN_HEADS = HEADS // 2
OWN_FF = FF // 2
QKV = 3 * OWN_HEADS * HEAD_DIM
HALF = OWN_HEADS // 2
AXES = ("z", "x", "core", "y")

clip_limit = 1000.0
learn_rate = 0.04
bias_rate = 0.25
beta_one = 0.5
beta_two = 0.5
weight_decay = 0.01

bf16 = jnp.bfloat16
f32 = jnp.float32
VMEM_LIMIT = 56 * 1024 * 1024
PACE = 0.05 * 3.3e6


def cost(microseconds):
    return pl.CostEstimate(
        flops=1, bytes_accessed=int(microseconds * PACE), transcendentals=0
    )


SCALE = HEAD_DIM ** (-0.5)
SCALE2 = SCALE * math.log2(math.e)


def normalize(values):
    centre = jnp.mean(values, -1, keepdims=True)
    centered = values - centre
    spread = lax.rsqrt(jnp.mean(centered * centered, -1, keepdims=True) + 1e-06)
    return (centered * spread, spread)


def norm_back(normed, spread, grad):
    return spread * (
        grad
        - jnp.mean(grad, -1, keepdims=True)
        - normed * jnp.mean(grad * normed, -1, keepdims=True)
    )


def gelu_tanh(values):
    return jax.nn.gelu(values, approximate=True)


def position_rows(slots, width):
    quarter = D // 4
    omega = 1.0 / 10000.0 ** (jnp.arange(quarter, dtype=f32) / quarter)
    rowpos = (slots // width).astype(f32)[..., None] * omega
    colpos = (slots % width).astype(f32)[..., None] * omega
    return jnp.concatenate([jnp.sin(rowpos), jnp.cos(rowpos), jnp.sin(colpos), jnp.cos(colpos)], -1)


def adam_step(weight, first, second, grad, factor, rate):
    clipped = grad * factor
    first = beta_one * first + (1.0 - beta_one) * clipped
    second = beta_two * second + (1.0 - beta_two) * clipped * clipped
    first_hat = first / (1.0 - beta_one**STEPS)
    second_hat = second / (1.0 - beta_two**STEPS)
    update = first_hat / (jnp.sqrt(second_hat) + 1e-08) + weight_decay * weight
    return (weight - rate * update, first, second)


def dot(left, right, over):
    return lax.dot_general(left, right, (over, ((), ())), preferred_element_type=f32)


def attend_kernel(deps, mask_ref, qkv_ref, *refs):
    mixed_ref, logsum_ref, score_ref = refs[deps:]
    seq = qkv_ref.shape[-1]
    half = seq // 2
    step = 512
    keys = qkv_ref[0, 1, 0].T
    values = qkv_ref[0, 2, 0]
    for start in range(0, seq, step):
        query = qkv_ref[0, 0, 0, :, start : start + step]
        score_ref[...] = dot(keys, query, ((1,), (0,)))
        score_ref[half - 64 : half, :] += mask_ref[0]
        score_ref[seq - 64 :, :] += mask_ref[1]
        scores = score_ref[...]
        top = jnp.max(scores, 0, keepdims=True)
        expo = jnp.exp2((scores - top) * SCALE2)
        total = jnp.sum(expo, 0, keepdims=True)
        probs = (expo * (1.0 / total)).astype(bf16)
        mixed = dot(values, probs, ((1,), (0,)))
        mixed_ref[0, :, start : start + step] = mixed.astype(bf16)
        logsum_ref[0, :, start : start + step] = top * SCALE2 + jnp.log2(total)


def attend(part, qkv, mask, earlier=(), deps=()):
    heads, seq = qkv.shape[2], qkv.shape[4]
    pairs = heads * seq * seq
    anywhere = pl.BlockSpec(memory_space=pl.ANY)
    return pl.pallas_call(
        functools.partial(attend_kernel, len(earlier) + len(deps)),
        grid=(heads,),
        in_specs=[
            pl.BlockSpec(memory_space=pltpu.SMEM),
            pl.BlockSpec((1, 3, 1, HEAD_DIM, seq), lambda h: (part, 0, h, 0, 0)),
        ]
        + [anywhere] * (len(earlier) + len(deps)),
        out_specs=[
            pl.BlockSpec((1, HEAD_DIM, seq), lambda h: (part * heads + h, 0, 0)),
            pl.BlockSpec((1, 1, seq), lambda h: (part * heads + h, 0, 0)),
        ],
        out_shape=[
            jax.ShapeDtypeStruct((2 * heads, HEAD_DIM, seq), bf16),
            jax.ShapeDtypeStruct((2 * heads, 1, seq), f32),
        ],
        input_output_aliases={2 + i: i for i in range(len(earlier))},
        scratch_shapes=[pltpu.VMEM((seq, 512), f32)],
        compiler_params=pltpu.CompilerParams(vmem_limit_bytes=VMEM_LIMIT),
        cost_estimate=cost(9.8),
        name="attend",
    )(mask, qkv, *earlier, *deps)


def attend_back_kernel(deps, mask_ref, qkv_ref, logsum_ref, dmix_ref, *refs):
    out_ref, score_ref, dk_ref, dv_ref = refs[deps:]
    seq = qkv_ref.shape[-1]
    half = seq // 2
    step = 512
    keys_t = qkv_ref[0, 1, 0]
    keys = keys_t.T
    values = qkv_ref[0, 2, 0].T
    for start in range(0, seq, step):
        query = qkv_ref[0, 0, 0, :, start : start + step]
        dmix = dmix_ref[0, :, start : start + step]
        score_ref[...] = dot(keys, query, ((1,), (0,)))
        score_ref[half - 64 : half, :] += mask_ref[0]
        score_ref[seq - 64 :, :] += mask_ref[1]
        probs = jnp.exp2(score_ref[...] * SCALE2 - logsum_ref[0, :, start : start + step])
        dprobs = dot(values, dmix, ((1,), (0,)))
        prod = probs * dprobs
        delta = jnp.sum(prod, 0, keepdims=True)
        dscore = (prod - probs * delta).astype(bf16)
        probs_low = probs.astype(bf16)
        out_ref[0, 0, 0, :, start : start + step] = (
            dot(keys_t, dscore, ((1,), (0,))) * SCALE
        ).astype(bf16)
        dk = dot(query, dscore, ((1,), (1,)))
        dv = dot(dmix, probs_low, ((1,), (1,)))
        if start == 0:
            dk_ref[...] = dk
            dv_ref[...] = dv
        else:
            dk_ref[...] += dk
            dv_ref[...] += dv
    out_ref[0, 1, 0] = (dk_ref[...] * SCALE).astype(bf16)
    out_ref[0, 2, 0] = dv_ref[...].astype(bf16)


def attend_back(part, qkv, logsum, dmix, mask, earlier=(), deps=()):
    heads, seq = qkv.shape[2], qkv.shape[4]
    pairs = heads * seq * seq
    block = pl.BlockSpec((1, 3, 1, HEAD_DIM, seq), lambda h: (part, 0, h, 0, 0))
    anywhere = pl.BlockSpec(memory_space=pl.ANY)
    return pl.pallas_call(
        functools.partial(attend_back_kernel, len(earlier) + len(deps)),
        grid=(heads,),
        in_specs=[
            pl.BlockSpec(memory_space=pltpu.SMEM),
            block,
            pl.BlockSpec((1, 1, seq), lambda h: (part * heads + h, 0, 0)),
            pl.BlockSpec((1, HEAD_DIM, seq), lambda h: (part * heads + h, 0, 0)),
        ]
        + [anywhere] * (len(earlier) + len(deps)),
        out_specs=block,
        out_shape=jax.ShapeDtypeStruct(qkv.shape, bf16),
        input_output_aliases={4 + i: i for i in range(len(earlier))},
        scratch_shapes=[
            pltpu.VMEM((seq, 512), f32),
            pltpu.VMEM((HEAD_DIM, seq), f32),
            pltpu.VMEM((HEAD_DIM, seq), f32),
        ],
        compiler_params=pltpu.CompilerParams(vmem_limit_bytes=VMEM_LIMIT),
        cost_estimate=cost(16.6),
        name="attend_back",
    )(mask, qkv, logsum, dmix, *earlier, *deps)


def move_kernel(plans, count, deps, where_ref, *refs):
    pieces = refs[:count]
    outs = refs[count + deps : count + deps + len(plans)]
    sem = refs[-1]
    zi, xi, yi = where_ref[0], where_ref[1], where_ref[2]

    def locate(ref, index):
        place = tuple(
            {"z": zi, "x": xi, "y": yi}[item[0]] ^ item[1] if isinstance(item, tuple) else item
            for item in index
        )
        return ref.at[place] if place else ref

    copies = []
    for out, plan in zip(outs, plans):
        for piece, source, target in plan:
            copies.append(
                pltpu.make_async_copy(
                    locate(pieces[piece], source), locate(out, target), sem.at[len(copies)]
                )
            )
    for copy in copies:
        copy.start()
    for copy in copies:
        copy.wait()


def move(where, pieces, shapes, plans, deps=(), name="move"):
    total = sum(len(plan) for plan in plans)
    anywhere = pl.BlockSpec(memory_space=pl.ANY)
    return pl.pallas_call(
        functools.partial(move_kernel, plans, len(pieces), len(deps)),
        in_specs=[pl.BlockSpec(memory_space=pltpu.SMEM)] + [anywhere] * (len(pieces) + len(deps)),
        out_specs=[pl.BlockSpec(memory_space=pltpu.VMEM)] * len(plans),
        out_shape=[jax.ShapeDtypeStruct(shape, pieces[0].dtype) for shape in shapes],
        scratch_shapes=[pltpu.SemaphoreType.DMA((total,))],
        compiler_params=pltpu.CompilerParams(vmem_limit_bytes=VMEM_LIMIT),
        cost_estimate=cost(4.0),
        name=name,
    )(where, *pieces, *deps)


def add_near_kernel(half, where_ref, grads, more, got_x, got_y, *refs):
    send_y, send_x, own, parts, gx, gy, sem = refs[-7:]
    zi, xi, yi = where_ref[0], where_ref[1], where_ref[2]
    lows, highs = pl.ds(0, half), pl.ds(half, half)
    sources = [
        ((lows, xi, 1 - yi), got_x.at[:, 1 - yi], gx.at[0]),
        ((highs, 1 - xi, yi), got_y.at[:, 1 - xi], gy.at[0]),
        ((lows, xi, yi), got_x.at[:, yi], gx.at[1]),
        ((highs, xi, yi), got_y.at[:, xi], gy.at[1]),
    ]
    copies = []
    for number, (place, got_from, got_to) in enumerate(sources):
        pairs = [
            (grads.at[place], parts.at[number, :, pl.ds(0, 3)]),
            (more.at[place], parts.at[number, :, 3]),
            (got_from, got_to),
        ]
        copies.append(
            [
                pltpu.make_async_copy(source, target, sem.at[3 * number + i])
                for i, (source, target) in enumerate(pairs)
            ]
        )
    for group in copies:
        for copy in group:
            copy.start()
    for number in range(4):
        for copy in copies[number]:
            copy.wait()
        got = (gx, gy, gx, gy)[number]
        for k in range(half):
            for i in range(4):
                total = parts[number, k, i].astype(f32) + got[number // 2, k, i].astype(f32)
                if number == 0:
                    send_y[k, i] = total.astype(bf16)
                elif number == 1:
                    send_x[k, i] = total.astype(bf16)
                else:
                    own[(number - 2) * half + k, i] = total


def add_near(where, grads, more, got_x, got_y, deps=()):
    nz, rows, columns = grads.shape[0], *grads.shape[-2:]
    half = nz // 2
    anywhere = pl.BlockSpec(memory_space=pl.ANY)
    inside = pl.BlockSpec(memory_space=pltpu.VMEM)
    return pl.pallas_call(
        functools.partial(add_near_kernel, half),
        in_specs=[pl.BlockSpec(memory_space=pltpu.SMEM)] + [anywhere] * (4 + len(deps)),
        out_specs=[inside] * 3,
        out_shape=[
            jax.ShapeDtypeStruct((half, 4, rows, columns), bf16),
            jax.ShapeDtypeStruct((half, 4, rows, columns), bf16),
            jax.ShapeDtypeStruct((nz, 4, rows, columns), f32),
        ],
        scratch_shapes=[
            pltpu.VMEM((4, half, 4, rows, columns), bf16),
            pltpu.VMEM((2, half, 4, rows, columns), bf16),
            pltpu.VMEM((2, half, 4, rows, columns), bf16),
            pltpu.SemaphoreType.DMA((12,)),
        ],
        compiler_params=pltpu.CompilerParams(vmem_limit_bytes=VMEM_LIMIT),
        cost_estimate=cost(5.4),
        name="add_near",
    )(where, grads, more, got_x, got_y, *deps)


def add_far_kernel(nz, where_ref, own_ref, got_y, got_x, *refs):
    sends, mine = refs[-2:]
    zi = where_ref[0]
    half = nz // 2
    for k in range(nz):
        got = got_y[k] if k < half else got_x[k - half]
        total = own_ref[k] + got.astype(f32)
        distance = zi ^ k

        @pl.when(distance == 0)
        def _():
            mine[...] = total

        @pl.when(distance > 0)
        def _():
            sends[jnp.maximum(distance - 1, 0)] = total.astype(bf16)


def add_far(where, own, got_y, got_x, deps=()):
    nz = own.shape[0]
    inside = pl.BlockSpec(memory_space=pltpu.VMEM)
    return pl.pallas_call(
        functools.partial(add_far_kernel, nz),
        in_specs=[pl.BlockSpec(memory_space=pltpu.SMEM)]
        + [inside] * 3
        + [pl.BlockSpec(memory_space=pl.ANY)] * len(deps),
        out_specs=[inside] * 2,
        out_shape=[
            jax.ShapeDtypeStruct((nz - 1, *own.shape[1:]), bf16),
            jax.ShapeDtypeStruct(own.shape[1:], f32),
        ],
        compiler_params=pltpu.CompilerParams(vmem_limit_bytes=VMEM_LIMIT),
        cost_estimate=cost(3.8),
        name="add_far",
    )(where, own, got_y, got_x, *deps)


def run(us, kernel, grid, ins, outs, args, name, scratch=(), deps=()):
    return pl.pallas_call(
        functools.partial(kernel, len(ins), len(deps)),
        grid=grid,
        in_specs=list(ins) + [pl.BlockSpec(memory_space=pl.ANY)] * len(deps),
        out_specs=[spec for spec, _ in outs],
        out_shape=[shape for _, shape in outs],
        scratch_shapes=list(scratch),
        compiler_params=pltpu.CompilerParams(vmem_limit_bytes=VMEM_LIMIT),
        cost_estimate=cost(us),
        name=name,
    )(*args, *deps)


def split_refs(count, deps, refs):
    return refs[:count], refs[count + deps :]


def fixed(*shape):
    return pl.BlockSpec(shape, lambda i: (0,) * len(shape))


def down(*shape):
    return pl.BlockSpec(shape, lambda i: (i,) + (0,) * (len(shape) - 1))


def across(*shape):
    return pl.BlockSpec(shape, lambda i: (0,) * (len(shape) - 1) + (i,))


def array(dtype, *shape):
    return jax.ShapeDtypeStruct(shape, dtype)


def qkv_kernel(count, deps, *refs):
    (w_ref, mine_ref, other_ref, bias_ref), (out_ref, turned_ref) = split_refs(count, deps, refs)
    step = pl.program_id(0)

    @pl.when(step == 0)
    def _():
        turned_ref[...] = w_ref[...].T

    @pl.when(step < 2)
    def _():
        total = dot(turned_ref[...], mine_ref[...], ((1,), (1,))) + bias_ref[...]
        out_ref[...] = total.astype(bf16)

    @pl.when(step >= 2)
    def _():
        total = dot(turned_ref[...], other_ref[...], ((1,), (1,))) + bias_ref[...]
        out_ref[...] = total.astype(bf16)


def project_qkv(weight, mine, other, bias, deps=()):
    rows, width = mine.shape
    columns = weight.shape[1]
    step = rows // 2
    return run(
        10.4,
        qkv_kernel,
        (4,),
        [
            fixed(width, columns),
            pl.BlockSpec((step, width), lambda i: (jnp.minimum(i, 1), 0)),
            pl.BlockSpec((step, width), lambda i: (jnp.maximum(i - 2, 0), 0)),
            fixed(columns, 1),
        ],
        [(across(columns, step), array(bf16, columns, 2 * rows))],
        (weight, mine, other, bias),
        "project_qkv",
        [pltpu.VMEM((columns, width), bf16)],
        deps,
    )[0]


def multiply_kernel(turn_left, over, count, deps, *refs):
    (left_ref, right_ref), (out_ref,) = split_refs(count, deps, refs)
    left = left_ref[...].T if turn_left else left_ref[...]
    out_ref[...] = dot(left, right_ref[...], ((1,), (over,)))


def multiply(left, right, part, turn_left=False, over=0, deps=()):
    tokens = left.shape[1] if turn_left else left.shape[0]
    inner = left.shape[0] if turn_left else left.shape[1]
    columns = right.shape[1 - over]
    step = tokens // 2
    if turn_left:
        left_spec = pl.BlockSpec((inner, step), lambda i: (0, i + part))
    else:
        left_spec = pl.BlockSpec((step, inner), lambda i: (i + part, 0))
    return run(
        inner * columns / 3.4e5,
        functools.partial(multiply_kernel, turn_left, over),
        (1,),
        [left_spec, fixed(*right.shape)],
        [(down(step, columns), array(f32, tokens // 2, columns))],
        (left, right),
        "multiply",
        (),
        deps,
    )[0]


def fc1_kernel(count, deps, *refs):
    (mine_ref, other_ref, w_ref, bias_ref), (slope_ref, hidden_ref) = split_refs(count, deps, refs)
    rows = mine_ref.shape[0]
    factor = math.sqrt(2.0 / math.pi)
    for part, ref in enumerate((mine_ref, other_ref)):
        pre = dot(ref[...], w_ref[...], ((1,), (0,))) + bias_ref[...]
        square = pre * pre
        bent = jnp.tanh(pre * (factor + (factor * 0.044715) * square))
        share = 0.5 + 0.5 * bent
        slope = share + (0.5 * pre) * (1.0 - bent * bent) * (
            factor + (3.0 * 0.044715 * factor) * square
        )
        slope_ref[part * rows : (part + 1) * rows] = slope
        hidden_ref[part * rows : (part + 1) * rows] = (pre * share).astype(bf16)


def fc1(mine, other, weight, bias, deps=()):
    rows, width = mine.shape
    columns = weight.shape[1]
    step = 384
    return run(
        16.0,
        fc1_kernel,
        (columns // step,),
        [fixed(rows, width)] * 2 + [across(width, step), across(1, step)],
        [
            (across(2 * rows, step), array(f32, 2 * rows, columns)),
            (across(2 * rows, step), array(bf16, 2 * rows, columns)),
        ],
        (mine, other, weight, bias),
        "fc1",
        (),
        deps,
    )


def fc2_back_kernel(count, deps, *refs):
    (mine_ref, other_ref, w_ref, slope_ref), (out_ref, sums_ref) = split_refs(count, deps, refs)
    rows = mine_ref.shape[0]
    total = 0.0
    for part, ref in enumerate((mine_ref, other_ref)):
        d_hidden = dot(ref[...], w_ref[...], ((1,), (1,)))
        d_pre = (d_hidden * slope_ref[part * rows : (part + 1) * rows]).astype(bf16)
        out_ref[part * rows : (part + 1) * rows] = d_pre
        total = total + jnp.sum(d_pre.astype(f32), 0, keepdims=True)
    sums_ref[...] = total


def fc2_back(mine, other, weight, slope, deps=()):
    rows, width = mine.shape
    columns = weight.shape[0]
    step = 384
    return run(
        13.9,
        fc2_back_kernel,
        (columns // step,),
        [fixed(rows, width)] * 2 + [down(step, width), across(2 * rows, step)],
        [
            (across(2 * rows, step), array(bf16, 2 * rows, columns)),
            (across(1, step), array(f32, 1, columns)),
        ],
        (mine, other, weight, slope),
        "fc2_back",
        (),
        deps,
    )


def fc2_grad_kernel(count, deps, *refs):
    (hidden_ref, mine_ref, other_ref), (out_ref,) = split_refs(count, deps, refs)
    rows = mine_ref.shape[0]
    turned = hidden_ref[...].T
    total = dot(turned[:, :rows], mine_ref[...], ((1,), (0,)))
    total = total + dot(turned[:, rows:], other_ref[...], ((1,), (0,)))
    out_ref[...] = total.astype(bf16)


def fc2_grad(hidden, mine, other, deps=()):
    tokens, columns = hidden.shape
    rows, width = mine.shape
    step = 384
    return run(
        10.7,
        fc2_grad_kernel,
        (columns // step,),
        [across(tokens, step)] + [fixed(rows, width)] * 2,
        [(down(step, width), array(bf16, columns, width))],
        (hidden, mine, other),
        "fc2_grad",
        (),
        deps,
    )[0]


def fc1_grad_kernel(count, deps, *refs):
    (mine_ref, other_ref, right_ref), (out_ref, turned_ref) = split_refs(count, deps, refs)
    z = pl.program_id(0)
    rows = out_ref.shape[2]
    half = mine_ref.shape[0]

    @pl.when(z == 0)
    def _():
        shape = (*turned_ref.shape[:2], half)
        turned_ref[:, :, :half] = mine_ref[...].T.reshape(shape)
        turned_ref[:, :, half:] = other_ref[...].T.reshape(shape)

    total = dot(turned_ref[z], right_ref[...], ((1,), (0,))).astype(bf16)
    for k in range(4):
        out_ref[k, 0] = total[k * rows : (k + 1) * rows]


def fc1_grad(mine, other, right, nz, deps=()):
    half, width = mine.shape
    tokens, columns = right.shape
    rows = width // (4 * nz)
    return run(
        11.4,
        fc1_grad_kernel,
        (nz,),
        [fixed(half, width)] * 2 + [fixed(tokens, columns)],
        [
            (
                pl.BlockSpec((4, 1, rows, columns), lambda z: (0, z, 0, 0)),
                array(bf16, 4, nz, rows, columns),
            )
        ],
        (mine, other, right),
        "fc1_grad",
        [pltpu.VMEM((nz, 4 * rows, tokens), bf16)],
        deps,
    )[0]


def qkv_grad_kernel(count, deps, *refs):
    (mine_ref, other_ref, right_ref), (out_ref,) = split_refs(count, deps, refs)
    half = mine_ref.shape[0]
    total = dot(mine_ref[...].T, right_ref[:, :half], ((1,), (1,)))
    total = total + dot(other_ref[...].T, right_ref[:, half:], ((1,), (1,)))
    out_ref[...] = total.astype(bf16)


def qkv_grad(mine, other, right, deps=()):
    half, width = mine.shape
    columns, tokens = right.shape
    step = 384
    return run(
        8.5,
        qkv_grad_kernel,
        (width // step,),
        [across(half, step)] * 2 + [fixed(columns, tokens)],
        [(down(step, columns), array(bf16, width, columns))],
        (mine, other, right),
        "qkv_grad",
        (),
        deps,
    )[0]


def proj_back_kernel(count, deps, *refs):
    (w_ref, mixed_ref, mine_ref, other_ref), (back_ref, grad_ref) = split_refs(count, deps, refs)
    half = mine_ref.shape[0]
    back_ref[:, :half] = dot(w_ref[...], mine_ref[...], ((1,), (1,))).astype(bf16)
    back_ref[:, half:] = dot(w_ref[...], other_ref[...], ((1,), (1,))).astype(bf16)
    total = dot(mixed_ref[:, :half], mine_ref[...], ((1,), (0,)))
    total = total + dot(mixed_ref[:, half:], other_ref[...], ((1,), (0,)))
    grad_ref[...] = total.astype(bf16)


def proj_back(weight, mixed, mine, other, deps=()):
    inner, tokens = mixed.shape
    half, width = mine.shape
    step = inner // 2
    return run(
        6.4,
        proj_back_kernel,
        (2,),
        [down(step, width), down(step, tokens)] + [fixed(half, width)] * 2,
        [
            (down(step, tokens), array(bf16, inner, tokens)),
            (down(step, width), array(bf16, inner, width)),
        ],
        (weight, mixed, mine, other),
        "proj_back",
        (),
        deps,
    )


def lane_sums_kernel(count, deps, *refs):
    (value_ref,), (out_ref,) = split_refs(count, deps, refs)
    out_ref[...] = jnp.sum(value_ref[...].astype(f32), 1, keepdims=True)


def lane_sums(value, deps=()):
    rows, width = value.shape
    return run(
        3.4,
        lane_sums_kernel,
        (1,),
        [fixed(rows, width)],
        [(fixed(rows, 1), array(f32, rows, 1))],
        (value,),
        "lane_sums",
        (),
        deps,
    )[0]


def sum_blocks_kernel(count, deps, *refs):
    ins, (out_ref,) = split_refs(count, deps, refs)
    out_ref[...] = sum((ref[...].astype(f32) for ref in ins[1:]), ins[0][...].astype(f32))


def sum_blocks(mine, got, deps=()):
    shape = mine.shape
    return run(
        3.0,
        sum_blocks_kernel,
        (1,),
        [fixed(*shape)] * (1 + len(got)),
        [(fixed(*shape), array(f32, *shape))],
        (mine, *got),
        "sum_blocks",
        (),
        deps,
    )[0]


ROWS = 128


def middle_kernel(count, deps, *refs):
    (vec_ref, mine_ref, got_ref, x_ref), (attn_ref, mid_ref, mlp_ref) = split_refs(
        count, deps, refs
    )
    attn = mine_ref[...] + got_ref[...] + vec_ref[6:7]
    mid = x_ref[...] + vec_ref[2:3] * attn
    normed, _ = normalize(mid)
    attn_ref[...] = attn
    mid_ref[...] = mid
    mlp_ref[...] = (normed * (1.0 + vec_ref[4:5]) + vec_ref[3:4]).astype(bf16)


def middle(vec, mine, got, x_in, deps=()):
    rows, width = mine.shape
    block = down(ROWS, width)
    return run(
        6.2,
        middle_kernel,
        (rows // ROWS,),
        [fixed(8, width)] + [block] * 3,
        [
            (block, array(f32, rows, width)),
            (block, array(f32, rows, width)),
            (block, array(bf16, rows, width)),
        ],
        (vec, mine, got, x_in),
        "middle",
        (),
        deps,
    )


def add_sums(sums_ref, values):
    @pl.when(pl.program_id(0) == 0)
    def _():
        sums_ref[...] = jnp.zeros_like(sums_ref)

    for number, value in enumerate(values):
        sums_ref[number : number + 1] += jnp.sum(value, 0, keepdims=True)


def valid_cotangent(valid_ref, cot_ref):
    row = pl.program_id(0) * ROWS + lax.broadcasted_iota(jnp.int32, (ROWS, 1), 0)
    return jnp.where(row < valid_ref[0], cot_ref[...].astype(f32), 0.0)


def middle_back_kernel(count, deps, *refs):
    (valid_ref, vec_ref, mine_ref, got_ref, cot_ref, mid_ref, attn_ref), (
        d_mid_ref,
        d_attn_ref,
        sums_ref,
    ) = split_refs(count, deps, refs)
    d_mlp = mine_ref[...] + got_ref[...]
    normed, spread = normalize(mid_ref[...])
    d_mid = valid_cotangent(valid_ref, cot_ref) + norm_back(
        normed, spread, d_mlp * (1.0 + vec_ref[4:5])
    )
    d_attn = (vec_ref[2:3] * d_mid).astype(bf16)
    d_mid_ref[...] = d_mid
    d_attn_ref[...] = d_attn
    add_sums(sums_ref, (d_mlp, d_mlp * normed, d_mid * attn_ref[...], d_attn.astype(f32)))


def middle_back(valid, vec, mine, got, cot, mid, attn, deps=()):
    rows, width = mine.shape
    block = down(ROWS, width)
    return run(
        7.5,
        middle_back_kernel,
        (rows // ROWS,),
        [pl.BlockSpec(memory_space=pltpu.SMEM), fixed(8, width)] + [block] * 5,
        [
            (block, array(f32, rows, width)),
            (block, array(bf16, rows, width)),
            (fixed(8, width), array(f32, 8, width)),
        ],
        (valid, vec, mine, got, cot, mid, attn),
        "middle_back",
        (),
        deps,
    )


def finish_first_kernel(count, deps, *refs):
    (vec_ref, mine_ref, got_ref, d_mid_ref, x_ref), (grad_ref, sums_ref) = split_refs(
        count, deps, refs
    )
    d_attn_in = mine_ref[...] + got_ref[...]
    normed, spread = normalize(x_ref[...])
    grad_ref[...] = (
        d_mid_ref[...] + norm_back(normed, spread, d_attn_in * (1.0 + vec_ref[1:2]))
    ).astype(bf16)
    add_sums(sums_ref, (d_attn_in, d_attn_in * normed))


def finish_first(vec, mine, got, d_mid, x_in, deps=()):
    rows, width = mine.shape
    block = down(ROWS, width)
    return run(
        6.2,
        finish_first_kernel,
        (rows // ROWS,),
        [fixed(8, width)] + [block] * 4,
        [
            (block, array(bf16, rows, width)),
            (fixed(8, width), array(f32, 8, width)),
        ],
        (vec, mine, got, d_mid, x_in),
        "finish_first",
        (),
        deps,
    )


def finish_last_kernel(count, deps, *refs):
    (valid_ref, vec_ref, mine_ref, got_ref, cot_ref, mid_ref), (out_ref, sums_ref) = split_refs(
        count, deps, refs
    )
    branch = mine_ref[...] + got_ref[...] + vec_ref[7:8]
    out_ref[...] = (mid_ref[...] + vec_ref[5:6] * branch).astype(bf16)
    add_sums(sums_ref, (valid_cotangent(valid_ref, cot_ref) * branch,))


def finish_last(valid, vec, mine, got, cot, mid, deps=()):
    rows, width = mine.shape
    block = down(ROWS, width)
    return run(
        5.3,
        finish_last_kernel,
        (rows // ROWS,),
        [pl.BlockSpec(memory_space=pltpu.SMEM), fixed(8, width)] + [block] * 4,
        [
            (block, array(bf16, rows, width)),
            (fixed(8, width), array(f32, 8, width)),
        ],
        (valid, vec, mine, got, cot, mid),
        "finish_last",
        (),
        deps,
    )


def adam_kernel(layout, rate, scalar_ref, *refs):
    grads, (w_ref, m_ref, v_ref), (new_w, new_m, new_v) = refs[:-6], refs[-6:-3], refs[-3:]
    factor = scalar_ref[0]
    column = 0
    if layout is None:
        pieces = [(0, 0, w_ref.shape[1])]
    else:
        pieces = layout
    swap = scalar_ref[1] > 0.5
    for part, first, width in pieces:
        if layout is None:
            grad = grads[0][...].astype(f32)
        else:
            here = slice(first, first + width)
            grad = jnp.where(
                swap, grads[1 - part][:, here].astype(f32), grads[part][:, here].astype(f32)
            )
        place = (slice(None), slice(column, column + width))
        weight, moment, second = adam_step(
            w_ref[place], m_ref[place], v_ref[place], grad, factor, rate
        )
        new_w[place], new_m[place], new_v[place] = weight, moment, second
        column += width


def adam(weight, first, second, grads, scalars, rate, layout=None):
    inside = pl.BlockSpec(memory_space=pltpu.VMEM)
    shape = jax.ShapeDtypeStruct(weight.shape, f32)
    return pl.pallas_call(
        functools.partial(adam_kernel, layout, rate),
        in_specs=[pl.BlockSpec(memory_space=pltpu.SMEM)] + [inside] * (len(grads) + 3),
        out_specs=[inside] * 3,
        out_shape=[shape] * 3,
        compiler_params=pltpu.CompilerParams(vmem_limit_bytes=VMEM_LIMIT),
        cost_estimate=cost(4.0),
        name="adam",
    )(scalars, *grads, weight, first, second)


def after_kernel(value_ref, *refs):
    refs[-1][...] = value_ref[...]


def after(value, *deps):
    flat = value.reshape(-1, value.shape[-1])
    return pl.pallas_call(
        after_kernel,
        in_specs=[pl.BlockSpec(memory_space=pltpu.VMEM)]
        + [pl.BlockSpec(memory_space=pl.ANY)] * len(deps),
        out_specs=pl.BlockSpec(memory_space=pltpu.VMEM),
        out_shape=jax.ShapeDtypeStruct(flat.shape, flat.dtype),
        compiler_params=pltpu.CompilerParams(vmem_limit_bytes=VMEM_LIMIT),
        cost_estimate=cost(1.5),
        name="after",
    )(flat, *deps).reshape(value.shape)


class Group:
    def __init__(self, n):
        self.n = n
        self.nz = n // 8
        self.me = lax.axis_index(AXES).astype(jnp.int32)
        self.y = self.me & 1
        self.c = (self.me >> 1) & 1
        self.x = (self.me >> 2) & 1
        self.z = self.me >> 3
        self.where = jnp.stack([self.z, self.x, self.y])

    def xor(self, value, mask):
        return lax.ppermute(value, AXES, [(i, i ^ mask) for i in range(self.n)])

    def core(self, value):
        return self.xor(value, 2)

    def turn(self, value):
        got = lax.ppermute(
            value,
            AXES,
            [(i, i ^ 3) for i in range(self.n) if (i & 3) in (1, 2)],
        )
        return jnp.where(self.c == self.y, value, got)

    def turn_other(self, value):
        return lax.ppermute(
            value,
            AXES,
            [(i, (i & ~3) | ((1 - (i & 1)) << 1) | ((i >> 1) & 1)) for i in range(self.n)],
        )

    def turn_other_back(self, value):
        return lax.ppermute(
            value,
            AXES,
            [(i, (i & ~3) | ((i & 1) << 1) | (1 - ((i >> 1) & 1))) for i in range(self.n)],
        )

    def to_block(self, parts):
        mine = lax.dynamic_index_in_dim(parts, self.y, 0, False)
        other = lax.dynamic_index_in_dim(parts, 1 - self.y, 0, False)
        got_a, got_b = self.turn(mine), self.turn_other(other)
        straight = self.c == 0
        return jnp.concatenate(
            [jnp.where(straight, got_a, got_b), jnp.where(straight, got_b, got_a)], 0
        )

    def from_block(self, block):
        rows = block.shape[0] // 2
        pieces = block.reshape(2, rows, block.shape[1])
        got_a = self.turn(lax.dynamic_index_in_dim(pieces, self.c, 0, False))
        got_b = self.turn_other_back(lax.dynamic_index_in_dim(pieces, 1 - self.c, 0, False))
        return got_a, got_b

    def gather_z(self, block):
        return [block] + [self.xor(block, d << 3) for d in range(1, self.nz)]

    def gather_near(self, pieces, deps=()):
        half = self.nz // 2
        plans = [
            [(k, (), (k,)) for k in range(half)],
            [(half + k, (), (k,)) for k in range(half)],
        ]
        shape = (half, *pieces[0].shape)
        low, high = move(self.where, pieces, [shape] * 2, plans, deps, "stack_z")
        return low, high, self.xor(low, 1), self.xor(high, 4)

    def gather_far(self, near, deps=()):
        half = self.nz // 2
        low, high, low_y, high_x = near
        plans = [[(0, (), (0,)), (2, (), (1,))], [(1, (), (0,)), (3, (), (1,))]]
        shape = (2, *low.shape)
        low_2, high_2 = move(self.where, near, [shape] * 2, plans, deps, "stack_near")
        return low_2, high_2, self.xor(low_2, 4), self.xor(high_2, 1)

    def gather_end(self, far, deps=(), cuts=((),), shapes=None, order="zxy"):
        nz, half = self.nz, self.nz // 2
        plans = []
        for cut in cuts:
            plan = []
            for k in range(half):
                for other in range(2):
                    for piece, target in (
                        (0, (("z", k), ("x", 0), ("y", other))),
                        (1, (("z", half + k), ("x", other), ("y", 0))),
                        (2, (("z", k), ("x", 1), ("y", other))),
                        (3, (("z", half + k), ("x", other), ("y", 1))),
                    ):
                        target = tuple(dict((t[0], t) for t in target)[axis] for axis in order)
                        plan.append((piece, (other, k, *cut), target))
            plans.append(plan)
        lead = tuple({"z": nz}.get(axis, 2) for axis in order)
        shapes = [(*lead, *shape) for shape in shapes or [far[0].shape[2:]]]
        return move(self.where, far, shapes, plans, deps, "place")

    def scatter_z(self, blocks, deps=()):
        nz = self.nz
        plans = [[(0, (("z", d),), ())] for d in range(nz)]
        parts = move(self.where, [blocks], [blocks.shape[1:]] * nz, plans, deps, "split_z")
        return parts, [self.xor(parts[d], d << 3) for d in range(1, nz)]

    def sum_z(self, state):
        parts, got = state
        return sum((item.astype(f32) for item in got), parts[0].astype(f32))

    def scatter_start(self, grads, deps=()):
        half = self.nz // 2
        plans = [[], []]
        for k in range(half):
            for other in range(2):
                for piece, cut in ((0, pl.ds(0, 3)), (1, 3)):
                    plans[0].append((piece, (k, ("x", 1), other), (k, other, cut)))
                    plans[1].append((piece, (half + k, other, ("y", 1)), (k, other, cut)))
        shape = (half, 2, 4, *grads[1].shape[3:])
        to_x, to_y = move(self.where, grads, [shape] * 2, plans, deps, "split")
        return grads, self.xor(to_x, 4), self.xor(to_y, 1), to_x

    def scatter_near(self, state, deps=()):
        grads, got_x, got_y = state[:3]
        send_y, send_x, own = add_near(self.where, *grads, got_x, got_y, deps)
        return own, self.xor(send_y, 1), self.xor(send_x, 4)

    def scatter_far(self, state, deps=()):
        sends, mine = add_far(self.where, *state, deps)
        return mine, [self.xor(sends[d - 1], d << 3) for d in range(1, self.nz)]

    def scatter_end(self, state):
        mine, got = state
        return sum((item.astype(f32) for item in got), mine)

    def all_sum(self, value):
        value = value + self.core(value)
        value = value + self.xor(value, 1)
        value = value + self.xor(value, 4)
        return sum((self.xor(value, d << 3) for d in range(1, self.nz)), value)


def per_device(
    tokens,
    embedding,
    heights,
    widths,
    cotangent,
    w_qkv,
    w_proj,
    w_fc1,
    w_fc2,
    w_ada,
    biases,
    m_qkv,
    m_proj,
    m_fc1,
    m_fc2,
    m_ada,
    m_bias,
    v_qkv,
    v_proj,
    v_fc1,
    v_fc2,
    v_ada,
    v_bias,
):
    rows = tokens.shape[1]
    n = math.prod(lax.axis_size(axis) for axis in AXES)
    own_rows = w_qkv.shape[0]
    g = Group(n)
    nz = g.nz
    groups = n // 4
    pair = 2 * own_rows
    ff_rows = w_fc2.shape[0]
    bias_rows = biases.shape[0]

    qkv_parts = (
        w_qkv.astype(bf16)
        .reshape(own_rows, 3, 2, HALF, 2, HEAD_DIM)
        .transpose(4, 0, 2, 1, 3, 5)
        .reshape(2, own_rows, QKV)
    )
    third = own_rows * D // QKV
    qp_block = jnp.concatenate(
        [g.to_block(qkv_parts), w_proj.astype(bf16).reshape(third, QKV)], 0
    ).reshape(4, third, QKV)
    qp_z = g.gather_z(qp_block)
    tokens_here = g.turn(after(tokens[0], qp_block))
    cotangent_here = g.turn(after(cotangent[0], tokens_here))
    cond_row = jax.nn.silu(embedding[0]).astype(bf16).reshape(groups * 2, 2, own_rows)
    cond_row = lax.dynamic_index_in_dim(cond_row, g.y, 1, False)
    small = jnp.concatenate([biases.astype(bf16), heights.astype(bf16), widths.astype(bf16)])
    small = jnp.concatenate(
        [cond_row, jnp.broadcast_to(small[None], (groups * 2, bias_rows + 2))], 1
    )
    small = jnp.pad(small, ((0, 0), (0, -small.shape[1] % 128)))
    small = lax.all_to_all(small, ("z", "x", "core"), 0, 0, tiled=True)
    conds_own = small[:, :own_rows]
    small_other = g.xor(small, 1)
    low = g.y == 0
    natural = jnp.stack(
        [jnp.where(low, small, small_other), jnp.where(low, small_other, small)], 1
    ).reshape(n, -1)[:, own_rows:].astype(f32)
    mod_part = dot(conds_own, w_ada.astype(bf16), ((1,), (0,)))
    mod_sum = jnp.sum(
        lax.all_to_all(mod_part, ("z", "x", "y"), 0, 0, tiled=True), 0, keepdims=True
    )
    mod_sum = mod_sum + g.core(mod_sum)
    qp_near = g.gather_near(qp_z, [tokens_here, mod_sum])
    fc1_parts = (
        w_fc1.astype(bf16)
        .reshape(own_rows, nz, 2, 2, 2, ff_rows)
        .transpose(3, 0, 2, 4, 1, 5)
        .reshape(2, own_rows, OWN_FF)
    )
    fc1_block = g.to_block(after(fc1_parts, qp_block))
    ff_block = jnp.concatenate(
        [
            fc1_block.reshape(2 * own_rows, 2, D).swapaxes(0, 1).reshape(-1, D),
            w_fc2.astype(bf16),
        ]
    )
    ff_all = lax.all_gather(after(ff_block, qp_near[0]), ("x", "y", "z"), axis=0, tiled=True)
    ff_all = ff_all.reshape(2, 2, nz, 4, 2 * own_rows, D)
    qp_far = g.gather_far(qp_near)
    bias_full = natural[:, :bias_rows].reshape(-1)
    bias_qkv = bias_full[: 3 * D]
    bias_proj = bias_full[3 * D : 4 * D]
    bias_fc1 = bias_full[4 * D : 4 * D + FF]
    bias_fc2 = bias_full[4 * D + FF : 5 * D + FF]
    bias_ada = bias_full[5 * D + FF :]
    image_row = lax.dynamic_index_in_dim(natural, (g.me & ~3) | (g.y << 1), 0, True)
    image_row = after(image_row, qp_far[0])[0]
    height = image_row[bias_rows].astype(jnp.int32)
    width = image_row[bias_rows + 1].astype(jnp.int32)
    modul = mod_sum + bias_ada
    shift1, scale1, gate1, shift2, scale2, gate2 = [
        modul[:, j * D : (j + 1) * D] for j in range(6)
    ]

    vec = jnp.concatenate([modul.reshape(6, D), bias_proj[None], bias_fc2[None]])

    slots = g.c * rows + jnp.arange(rows, dtype=jnp.int32)
    count = height * width
    valid_rows = (slots < count).astype(f32)[:, None]
    seq = 2 * rows
    cut = jnp.where(count < seq, -1e30, 0.0).astype(f32)
    mask = jnp.stack([jnp.where(g.c == 1, cut, 0.0), jnp.where(g.c == 0, cut, 0.0)])
    valid = jnp.clip(count - g.c * rows, 0, rows).astype(jnp.int32)[None]
    x_in = tokens_here.astype(f32) + position_rows(slots, width)
    normed1, spread1 = normalize(x_in)
    attn_in = (normed1 * (1.0 + scale1) + shift1).astype(bf16)
    d_out = cotangent_here.astype(f32) * valid_rows
    d_branch = (gate2 * d_out).astype(bf16)
    gb_fc2 = jnp.sum(d_branch.astype(f32), 0, keepdims=True)
    attn_sib = g.core(attn_in)
    qkv_w = g.gather_end(qp_far, [attn_in], ((pl.ds(0, 3),),), ((3, third, QKV),))[0]
    qkv_w = qkv_w.reshape(D, QKV)
    own_bias_qkv = lax.dynamic_index_in_dim(
        bias_qkv.reshape(3, 2, HALF, 2, HEAD_DIM), g.c, 3, False
    ).swapaxes(0, 1).reshape(-1, 1)
    qkv = project_qkv(qkv_w, attn_in, attn_sib, own_bias_qkv)
    qkv = qkv.reshape(2, 3, HALF, HEAD_DIM, seq)
    first = attend(0, qkv, mask)
    proj_own = g.gather_end(qp_far, first[1:], ((3,),), ((third, QKV),))[0].reshape(-1, D)
    heads_match = pair % HEAD_DIM == 0
    if heads_match:
        proj_w = proj_own
    else:
        mine = proj_own.reshape(groups, pair, D)
        theirs = g.core(mine)
        own_first = g.c == 0
        whole = jnp.stack(
            [jnp.where(own_first, mine, theirs), jnp.where(own_first, theirs, mine)], 1
        ).reshape(OWN_HEADS, 2, HEAD_DIM, D)
        proj_w = lax.dynamic_index_in_dim(whole, g.c, 1, False).reshape(OWN_HEADS * HEAD_DIM, D)
    mixed, logsum = attend(1, qkv, mask, first, [proj_w])
    mixed = mixed.reshape(OWN_HEADS * HEAD_DIM, seq)
    attn_got = g.core(dot(mixed[:, rows:], proj_w, ((0,), (0,))))
    attn_mine = dot(mixed[:, :rows], proj_w, ((0,), (0,)))
    attn, x_mid, mlp_in = middle(vec, attn_mine, attn_got, x_in)
    mlp_got = g.core(mlp_in)
    own_bias_fc1 = lax.dynamic_index_in_dim(
        bias_fc1.reshape(nz, 2, 2, 2, ff_rows), g.c, 2, False
    ).transpose(1, 2, 0, 3).reshape(-1)
    plan = [
        (0, (x, y, z, h), (z, x, y, slice(None), pl.ds(h * D, D)))
        for x in range(2)
        for y in range(2)
        for z in range(nz)
        for h in range(2)
    ]
    fc1_w = move(
        g.where, [ff_all], [(nz, 2, 2, 2 * own_rows, OWN_FF)], [plan], [mlp_in], "place_fc1"
    )[0].reshape(D, OWN_FF)
    slope, hidden = fc1(mlp_in, mlp_got, fc1_w, own_bias_fc1[None])
    branch_got = g.core(d_branch)
    g_fc2 = fc2_grad(hidden, d_branch, branch_got)
    red_fc2 = lax.psum_scatter(g_fc2, ("x", "y"), scatter_dimension=0, tiled=True)
    plan = [
        (0, (x, y, z, pl.ds(2, 2)), (x, y, z)) for x in range(2) for y in range(2) for z in range(nz)
    ]
    fc2_w = move(
        g.where, [ff_all], [(2, 2, nz, 2, 2 * own_rows, D)], [plan], [g_fc2], "place_fc2"
    )[0].reshape(OWN_FF, D)
    d_pre, gb_fc1 = fc2_back(d_branch, branch_got, fc2_w, slope, [g_fc2])
    d_mlp_got = g.core(dot(d_pre[rows:], fc1_w, ((1,), (1,))))
    d_mlp_mine = dot(d_pre[:rows], fc1_w, ((1,), (1,)))
    g_fc1 = fc1_grad(mlp_in, mlp_got, d_pre, nz, [d_mlp_mine]).reshape(D, OWN_FF)
    red_fc1 = lax.psum_scatter(g_fc1, ("x", "y"), scatter_dimension=0, tiled=True)
    d_mid, d_attn, middle_sums = middle_back(
        valid, vec, d_mlp_mine, d_mlp_got, cotangent_here, x_mid, attn
    )
    d_attn_got = g.core(d_attn)
    d_mixed, g_proj = proj_back(proj_w, mixed, d_attn, d_attn_got)
    if heads_match:
        g_proj = g_proj.reshape(nz, 2, 2, third, QKV)
    else:
        own = (jnp.arange(2) == g.c)[None, :, None, None]
        whole = jnp.where(own, g_proj.reshape(OWN_HEADS, 1, HEAD_DIM, D), 0).reshape(
            groups, 2, pair, D
        )
        theirs = g.core(lax.dynamic_index_in_dim(whole, 1 - g.c, 1, False))
        mine = lax.dynamic_index_in_dim(whole, g.c, 1, False)
        g_proj = (mine.astype(f32) + theirs.astype(f32)).astype(bf16).reshape(nz, 2, 2, third, QKV)
    d_mixed = d_mixed.reshape(OWN_HEADS, HEAD_DIM, seq)
    d_qkv = attend_back(0, qkv, logsum, d_mixed, mask, (), [g_proj])
    fc2_state = g.scatter_z(red_fc2.reshape(nz, -1, D), [d_qkv])
    d_qkv = attend_back(1, qkv, logsum, d_mixed, mask, [d_qkv], [fc2_state[0][0]])
    d_qkv = d_qkv.reshape(QKV, seq)
    g_qkv = qkv_grad(attn_in, attn_sib, d_qkv)
    red_fc2 = sum_blocks(fc2_state[0][0], fc2_state[1], [g_qkv])
    qkv_state = g.scatter_start([g_qkv.reshape(nz, 2, 2, 3, third, QKV), g_proj], [red_fc2])
    red_fc1 = lax.psum_scatter(
        after(red_fc1, qkv_state[3]), "z", scatter_dimension=0, tiled=True
    )
    d_attn_in = multiply(d_qkv, qkv_w, 1, True, 1, [qkv_state[3]])
    d_attn_in_got = g.core(d_attn_in)
    d_attn_in = multiply(d_qkv, qkv_w, 0, True, 1, [d_attn_in])
    gb_qkv = lane_sums(d_qkv, [d_attn_in])
    grad_tokens, first_sums = finish_first(
        vec, d_attn_in, d_attn_in_got, d_mid, x_in, [gb_qkv]
    )
    qkv_state = g.scatter_near(qkv_state, [first_sums, red_fc1])
    branch = multiply(hidden, fc2_w, 1, deps=[qkv_state[0]])
    branch_got = g.core(branch)
    branch = multiply(hidden, fc2_w, 0, deps=[branch])
    qkv_state = g.scatter_far(qkv_state, [branch])
    output, last_sums = finish_last(
        valid, vec, branch, branch_got, cotangent_here, x_mid, [qkv_state[0]]
    )
    grad_tokens = g.turn(after(grad_tokens, qkv_state[0]))[None]
    red_qp = sum_blocks(qkv_state[0], qkv_state[1], [last_sums, grad_tokens])
    fc1_parts = g.from_block(after(red_fc1, red_qp))

    own = (jnp.arange(2) == g.c)[None, :, None]
    gb_qkv = gb_qkv.reshape(2, 3, HALF, HEAD_DIM).swapaxes(0, 1)
    gb_qkv = jnp.where(own, gb_qkv.reshape(3 * OWN_HEADS, 1, HEAD_DIM), 0.0).reshape(3, D)
    gb_fc1 = gb_fc1.reshape(2, 2, nz, ff_rows).transpose(2, 0, 1, 3)
    gb_fc1 = jnp.where(own, gb_fc1.reshape(groups, 1, 2 * ff_rows), 0.0).reshape(-1, D)
    vector = jnp.concatenate(
        [
            gb_qkv,
            middle_sums[3:4],
            gb_fc1,
            gb_fc2,
            first_sums[:2],
            middle_sums[2:3],
            middle_sums[:2],
            last_sums[:1],
        ]
    )
    vector = after(vector, red_qp)
    vector = vector + g.core(vector)
    plain = vector.shape[0] - 6
    others = [g.xor(vector, d << 3) for d in range(1, nz)]
    sums = sum((item[:plain] for item in others), vector[:plain])
    mods = jnp.stack([vector[plain:]] + [item[plain:] for item in others])[:, None]
    for bit in (1, 4):
        packed = jnp.concatenate([sums, mods.reshape(-1, D)])
        packed = g.xor(packed, bit)
        sums = sums + packed[:plain]
        mods = jnp.stack([mods, packed[plain:].reshape(mods.shape)], 1)
    mods = mods.reshape(groups * 2, 6 * D)
    place_of = (g.z * 2 + g.x) * 2 + g.y
    order = jnp.arange(groups * 2)[None, :] == (jnp.arange(groups * 2)[:, None] ^ place_of)
    conds_own = dot(order.astype(bf16), conds_own, ((1,), (0,)))
    red_ada = lax.dot_general(
        conds_own.astype(f32),
        mods,
        (((0,), (0,)), ((), ())),
        precision=lax.Precision.HIGHEST,
        preferred_element_type=f32,
    )
    g_bias = jnp.concatenate([sums.reshape(-1), jnp.sum(mods, 0)])
    red_bias = lax.dynamic_slice_in_dim(g_bias, g.me * bias_rows, bias_rows)

    red_qkv = red_qp[:3].reshape(2 * own_rows, QKV)
    red_proj = red_qp[3].reshape(own_rows, D)
    output = g.turn(after(output, sums))[None]
    squares = sum(
        (
            jnp.sum(jnp.square(piece.astype(f32)))
            for piece in (red_qp, red_fc1, red_fc2, red_ada, red_bias)
        )
    )
    squares = g.all_sum(jnp.broadcast_to(squares, (1, 128)))[0, 0]
    red_qkv = g.from_block(red_qkv)
    grad_norm = jnp.sqrt(squares)
    factor = jnp.minimum(1.0, clip_limit / grad_norm)
    scalars = jnp.stack([factor, g.y.astype(f32)])
    piece = HALF * HEAD_DIM
    qkv_layout = [
        (c, (hh * 3 + kind) * piece + head * HEAD_DIM, HEAD_DIM)
        for kind in range(3)
        for hh in range(2)
        for head in range(HALF)
        for c in range(2)
    ]
    fc1_layout = [
        (c, ((x * 2 + y) * nz + z) * ff_rows, ff_rows)
        for z in range(nz)
        for x in range(2)
        for c in range(2)
        for y in range(2)
    ]
    results = [
        adam(w_qkv, m_qkv, v_qkv, red_qkv, scalars, learn_rate, qkv_layout),
        adam(w_proj, m_proj, v_proj, [red_proj], scalars, learn_rate),
        adam(w_fc1, m_fc1, v_fc1, fc1_parts, scalars, learn_rate, fc1_layout),
        adam(w_fc2, m_fc2, v_fc2, [red_fc2], scalars, learn_rate),
        adam(w_ada, m_ada, v_ada, [red_ada], scalars, learn_rate),
        adam_step(biases, m_bias, v_bias, red_bias, factor, bias_rate),
    ]
    return (
        output,
        grad_tokens,
        grad_norm,
        *[item[0] for item in results],
        *[item[1] for item in results],
        *[item[2] for item in results],
    )


def solution(mesh):
    count = mesh.devices.size
    fine = jax.sharding.Mesh(mesh.devices.reshape(count // 8, 2, 2, 2), AXES)
    image = ("z", "x", "core")
    patches = P(image, "y", None)
    state = (P(AXES, None),) * 5 + (P(AXES),)
    return jax.shard_map(
        per_device,
        mesh=fine,
        in_specs=(patches, P(image, None), P(image), P(image), patches, *state, *state, *state),
        out_specs=(patches, patches, P(), *state, *state, *state),
        check_vma=False,
    )
```

```python
import functools
import math

import jax
import jax.numpy as jnp
from jax import lax
from jax.experimental import pallas as pl
from jax.experimental.pallas import tpu as pltpu
from jax.sharding import PartitionSpec as P

D = 1152
HEADS = 16
HEAD_DIM = 72
FF = 4608
STEPS = 10
OWN_HEADS = HEADS // 2
OWN_FF = FF // 2
QKV = 3 * OWN_HEADS * HEAD_DIM
HALF = OWN_HEADS // 2
AXES = ("z", "x", "core", "y")

clip_limit = 1000.0
learn_rate = 0.04
bias_rate = 0.25
beta_one = 0.5
beta_two = 0.5
weight_decay = 0.01

bf16 = jnp.bfloat16
f32 = jnp.float32
VMEM_LIMIT = 56 * 1024 * 1024
PACE = 0.05 * 3.3e6


def cost(microseconds):
    return pl.CostEstimate(
        flops=1, bytes_accessed=int(microseconds * PACE), transcendentals=0
    )


SCALE = HEAD_DIM ** (-0.5)
SCALE2 = SCALE * math.log2(math.e)


def normalize(values):
    centre = jnp.mean(values, -1, keepdims=True)
    centered = values - centre
    spread = lax.rsqrt(jnp.mean(centered * centered, -1, keepdims=True) + 1e-06)
    return (centered * spread, spread)


def norm_back(normed, spread, grad):
    return spread * (
        grad
        - jnp.mean(grad, -1, keepdims=True)
        - normed * jnp.mean(grad * normed, -1, keepdims=True)
    )


def gelu_tanh(values):
    return jax.nn.gelu(values, approximate=True)


def position_rows(slots, width):
    quarter = D // 4
    omega = 1.0 / 10000.0 ** (jnp.arange(quarter, dtype=f32) / quarter)
    rowpos = (slots // width).astype(f32)[..., None] * omega
    colpos = (slots % width).astype(f32)[..., None] * omega
    return jnp.concatenate([jnp.sin(rowpos), jnp.cos(rowpos), jnp.sin(colpos), jnp.cos(colpos)], -1)


def adam_step(weight, first, second, grad, factor, rate):
    clipped = grad * factor
    first = beta_one * first + (1.0 - beta_one) * clipped
    second = beta_two * second + (1.0 - beta_two) * clipped * clipped
    first_hat = first / (1.0 - beta_one**STEPS)
    second_hat = second / (1.0 - beta_two**STEPS)
    update = first_hat / (jnp.sqrt(second_hat) + 1e-08) + weight_decay * weight
    return (weight - rate * update, first, second)


def dot(left, right, over):
    return lax.dot_general(left, right, (over, ((), ())), preferred_element_type=f32)


def attend_kernel(deps, mask_ref, qkv_ref, *refs):
    mixed_ref, logsum_ref, score_ref = refs[deps:]
    seq = qkv_ref.shape[-1]
    half = seq // 2
    step = 512
    keys = qkv_ref[0, 1, 0].T
    values = qkv_ref[0, 2, 0]
    for start in range(0, seq, step):
        query = qkv_ref[0, 0, 0, :, start : start + step]
        score_ref[...] = dot(keys, query, ((1,), (0,)))
        score_ref[half - 64 : half, :] += mask_ref[0]
        score_ref[seq - 64 :, :] += mask_ref[1]
        scores = score_ref[...]
        top = jnp.max(scores, 0, keepdims=True)
        expo = jnp.exp2((scores - top) * SCALE2)
        total = jnp.sum(expo, 0, keepdims=True)
        probs = (expo * (1.0 / total)).astype(bf16)
        mixed = dot(values, probs, ((1,), (0,)))
        mixed_ref[0, :, start : start + step] = mixed.astype(bf16)
        logsum_ref[0, :, start : start + step] = top * SCALE2 + jnp.log2(total)


def attend(part, qkv, mask, earlier=(), deps=()):
    heads, seq = qkv.shape[2], qkv.shape[4]
    pairs = heads * seq * seq
    anywhere = pl.BlockSpec(memory_space=pl.ANY)
    return pl.pallas_call(
        functools.partial(attend_kernel, len(earlier) + len(deps)),
        grid=(heads,),
        in_specs=[
            pl.BlockSpec(memory_space=pltpu.SMEM),
            pl.BlockSpec((1, 3, 1, HEAD_DIM, seq), lambda h: (part, 0, h, 0, 0)),
        ]
        + [anywhere] * (len(earlier) + len(deps)),
        out_specs=[
            pl.BlockSpec((1, HEAD_DIM, seq), lambda h: (part * heads + h, 0, 0)),
            pl.BlockSpec((1, 1, seq), lambda h: (part * heads + h, 0, 0)),
        ],
        out_shape=[
            jax.ShapeDtypeStruct((2 * heads, HEAD_DIM, seq), bf16),
            jax.ShapeDtypeStruct((2 * heads, 1, seq), f32),
        ],
        input_output_aliases={2 + i: i for i in range(len(earlier))},
        scratch_shapes=[pltpu.VMEM((seq, 512), f32)],
        compiler_params=pltpu.CompilerParams(vmem_limit_bytes=VMEM_LIMIT),
        cost_estimate=cost(9.8),
        name="attend",
    )(mask, qkv, *earlier, *deps)


def attend_back_kernel(deps, mask_ref, qkv_ref, logsum_ref, dmix_ref, *refs):
    out_ref, score_ref, dk_ref, dv_ref = refs[deps:]
    seq = qkv_ref.shape[-1]
    half = seq // 2
    step = 512
    keys_t = qkv_ref[0, 1, 0]
    keys = keys_t.T
    values = qkv_ref[0, 2, 0].T
    for start in range(0, seq, step):
        query = qkv_ref[0, 0, 0, :, start : start + step]
        dmix = dmix_ref[0, :, start : start + step]
        score_ref[...] = dot(keys, query, ((1,), (0,)))
        score_ref[half - 64 : half, :] += mask_ref[0]
        score_ref[seq - 64 :, :] += mask_ref[1]
        probs = jnp.exp2(score_ref[...] * SCALE2 - logsum_ref[0, :, start : start + step])
        dprobs = dot(values, dmix, ((1,), (0,)))
        prod = probs * dprobs
        delta = jnp.sum(prod, 0, keepdims=True)
        dscore = (prod - probs * delta).astype(bf16)
        probs_low = probs.astype(bf16)
        out_ref[0, 0, 0, :, start : start + step] = (
            dot(keys_t, dscore, ((1,), (0,))) * SCALE
        ).astype(bf16)
        dk = dot(query, dscore, ((1,), (1,)))
        dv = dot(dmix, probs_low, ((1,), (1,)))
        if start == 0:
            dk_ref[...] = dk
            dv_ref[...] = dv
        else:
            dk_ref[...] += dk
            dv_ref[...] += dv
    out_ref[0, 1, 0] = (dk_ref[...] * SCALE).astype(bf16)
    out_ref[0, 2, 0] = dv_ref[...].astype(bf16)


def attend_back(part, qkv, logsum, dmix, mask, earlier=(), deps=()):
    heads, seq = qkv.shape[2], qkv.shape[4]
    pairs = heads * seq * seq
    block = pl.BlockSpec((1, 3, 1, HEAD_DIM, seq), lambda h: (part, 0, h, 0, 0))
    anywhere = pl.BlockSpec(memory_space=pl.ANY)
    return pl.pallas_call(
        functools.partial(attend_back_kernel, len(earlier) + len(deps)),
        grid=(heads,),
        in_specs=[
            pl.BlockSpec(memory_space=pltpu.SMEM),
            block,
            pl.BlockSpec((1, 1, seq), lambda h: (part * heads + h, 0, 0)),
            pl.BlockSpec((1, HEAD_DIM, seq), lambda h: (part * heads + h, 0, 0)),
        ]
        + [anywhere] * (len(earlier) + len(deps)),
        out_specs=block,
        out_shape=jax.ShapeDtypeStruct(qkv.shape, bf16),
        input_output_aliases={4 + i: i for i in range(len(earlier))},
        scratch_shapes=[
            pltpu.VMEM((seq, 512), f32),
            pltpu.VMEM((HEAD_DIM, seq), f32),
            pltpu.VMEM((HEAD_DIM, seq), f32),
        ],
        compiler_params=pltpu.CompilerParams(vmem_limit_bytes=VMEM_LIMIT),
        cost_estimate=cost(16.6),
        name="attend_back",
    )(mask, qkv, logsum, dmix, *earlier, *deps)


def move_kernel(plans, count, deps, where_ref, *refs):
    pieces = refs[:count]
    outs = refs[count + deps : count + deps + len(plans)]
    sem = refs[-1]
    zi, xi, yi = where_ref[0], where_ref[1], where_ref[2]

    def locate(ref, index):
        place = tuple(
            {"z": zi, "x": xi, "y": yi}[item[0]] ^ item[1] if isinstance(item, tuple) else item
            for item in index
        )
        return ref.at[place] if place else ref

    copies = []
    for out, plan in zip(outs, plans):
        for piece, source, target in plan:
            copies.append(
                pltpu.make_async_copy(
                    locate(pieces[piece], source), locate(out, target), sem.at[len(copies)]
                )
            )
    for copy in copies:
        copy.start()
    for copy in copies:
        copy.wait()


def move(where, pieces, shapes, plans, deps=(), name="move"):
    total = sum(len(plan) for plan in plans)
    anywhere = pl.BlockSpec(memory_space=pl.ANY)
    return pl.pallas_call(
        functools.partial(move_kernel, plans, len(pieces), len(deps)),
        in_specs=[pl.BlockSpec(memory_space=pltpu.SMEM)] + [anywhere] * (len(pieces) + len(deps)),
        out_specs=[pl.BlockSpec(memory_space=pltpu.VMEM)] * len(plans),
        out_shape=[jax.ShapeDtypeStruct(shape, pieces[0].dtype) for shape in shapes],
        scratch_shapes=[pltpu.SemaphoreType.DMA((total,))],
        compiler_params=pltpu.CompilerParams(vmem_limit_bytes=VMEM_LIMIT),
        cost_estimate=cost(4.0),
        name=name,
    )(where, *pieces, *deps)


def add_near_kernel(half, where_ref, grads, more, got_x, got_y, *refs):
    send_y, send_x, own, parts, gx, gy, sem = refs[-7:]
    zi, xi, yi = where_ref[0], where_ref[1], where_ref[2]
    lows, highs = pl.ds(0, half), pl.ds(half, half)
    sources = [
        ((lows, xi, 1 - yi), got_x.at[:, 1 - yi], gx.at[0]),
        ((highs, 1 - xi, yi), got_y.at[:, 1 - xi], gy.at[0]),
        ((lows, xi, yi), got_x.at[:, yi], gx.at[1]),
        ((highs, xi, yi), got_y.at[:, xi], gy.at[1]),
    ]
    copies = []
    for number, (place, got_from, got_to) in enumerate(sources):
        pairs = [
            (grads.at[place], parts.at[number, :, pl.ds(0, 3)]),
            (more.at[place], parts.at[number, :, 3]),
            (got_from, got_to),
        ]
        copies.append(
            [
                pltpu.make_async_copy(source, target, sem.at[3 * number + i])
                for i, (source, target) in enumerate(pairs)
            ]
        )
    for group in copies:
        for copy in group:
            copy.start()
    for number in range(4):
        for copy in copies[number]:
            copy.wait()
        got = (gx, gy, gx, gy)[number]
        for k in range(half):
            for i in range(4):
                total = parts[number, k, i].astype(f32) + got[number // 2, k, i].astype(f32)
                if number == 0:
                    send_y[k, i] = total.astype(bf16)
                elif number == 1:
                    send_x[k, i] = total.astype(bf16)
                else:
                    own[(number - 2) * half + k, i] = total


def add_near(where, grads, more, got_x, got_y, deps=()):
    nz, rows, columns = grads.shape[0], *grads.shape[-2:]
    half = nz // 2
    anywhere = pl.BlockSpec(memory_space=pl.ANY)
    inside = pl.BlockSpec(memory_space=pltpu.VMEM)
    return pl.pallas_call(
        functools.partial(add_near_kernel, half),
        in_specs=[pl.BlockSpec(memory_space=pltpu.SMEM)] + [anywhere] * (4 + len(deps)),
        out_specs=[inside] * 3,
        out_shape=[
            jax.ShapeDtypeStruct((half, 4, rows, columns), bf16),
            jax.ShapeDtypeStruct((half, 4, rows, columns), bf16),
            jax.ShapeDtypeStruct((nz, 4, rows, columns), f32),
        ],
        scratch_shapes=[
            pltpu.VMEM((4, half, 4, rows, columns), bf16),
            pltpu.VMEM((2, half, 4, rows, columns), bf16),
            pltpu.VMEM((2, half, 4, rows, columns), bf16),
            pltpu.SemaphoreType.DMA((12,)),
        ],
        compiler_params=pltpu.CompilerParams(vmem_limit_bytes=VMEM_LIMIT),
        cost_estimate=cost(5.4),
        name="add_near",
    )(where, grads, more, got_x, got_y, *deps)


def add_far_kernel(nz, where_ref, own_ref, got_y, got_x, *refs):
    sends, mine = refs[-2:]
    zi = where_ref[0]
    half = nz // 2
    for k in range(nz):
        got = got_y[k] if k < half else got_x[k - half]
        total = own_ref[k] + got.astype(f32)
        distance = zi ^ k

        @pl.when(distance == 0)
        def _():
            mine[...] = total

        @pl.when(distance > 0)
        def _():
            sends[jnp.maximum(distance - 1, 0)] = total.astype(bf16)


def add_far(where, own, got_y, got_x, deps=()):
    nz = own.shape[0]
    inside = pl.BlockSpec(memory_space=pltpu.VMEM)
    return pl.pallas_call(
        functools.partial(add_far_kernel, nz),
        in_specs=[pl.BlockSpec(memory_space=pltpu.SMEM)]
        + [inside] * 3
        + [pl.BlockSpec(memory_space=pl.ANY)] * len(deps),
        out_specs=[inside] * 2,
        out_shape=[
            jax.ShapeDtypeStruct((nz - 1, *own.shape[1:]), bf16),
            jax.ShapeDtypeStruct(own.shape[1:], f32),
        ],
        compiler_params=pltpu.CompilerParams(vmem_limit_bytes=VMEM_LIMIT),
        cost_estimate=cost(3.8),
        name="add_far",
    )(where, own, got_y, got_x, *deps)


def run(us, kernel, grid, ins, outs, args, name, scratch=(), deps=()):
    return pl.pallas_call(
        functools.partial(kernel, len(ins), len(deps)),
        grid=grid,
        in_specs=list(ins) + [pl.BlockSpec(memory_space=pl.ANY)] * len(deps),
        out_specs=[spec for spec, _ in outs],
        out_shape=[shape for _, shape in outs],
        scratch_shapes=list(scratch),
        compiler_params=pltpu.CompilerParams(vmem_limit_bytes=VMEM_LIMIT),
        cost_estimate=cost(us),
        name=name,
    )(*args, *deps)


def split_refs(count, deps, refs):
    return refs[:count], refs[count + deps :]


def fixed(*shape):
    return pl.BlockSpec(shape, lambda i: (0,) * len(shape))


def down(*shape):
    return pl.BlockSpec(shape, lambda i: (i,) + (0,) * (len(shape) - 1))


def across(*shape):
    return pl.BlockSpec(shape, lambda i: (0,) * (len(shape) - 1) + (i,))


def array(dtype, *shape):
    return jax.ShapeDtypeStruct(shape, dtype)


def qkv_kernel(count, deps, *refs):
    (w_ref, mine_ref, other_ref, bias_ref), (out_ref, turned_ref) = split_refs(count, deps, refs)
    step = pl.program_id(0)

    @pl.when(step == 0)
    def _():
        turned_ref[...] = w_ref[...].T

    @pl.when(step < 2)
    def _():
        total = dot(turned_ref[...], mine_ref[...], ((1,), (1,))) + bias_ref[...]
        out_ref[...] = total.astype(bf16)

    @pl.when(step >= 2)
    def _():
        total = dot(turned_ref[...], other_ref[...], ((1,), (1,))) + bias_ref[...]
        out_ref[...] = total.astype(bf16)


def project_qkv(weight, mine, other, bias, deps=()):
    rows, width = mine.shape
    columns = weight.shape[1]
    step = rows // 2
    return run(
        10.4,
        qkv_kernel,
        (4,),
        [
            fixed(width, columns),
            pl.BlockSpec((step, width), lambda i: (jnp.minimum(i, 1), 0)),
            pl.BlockSpec((step, width), lambda i: (jnp.maximum(i - 2, 0), 0)),
            fixed(columns, 1),
        ],
        [(across(columns, step), array(bf16, columns, 2 * rows))],
        (weight, mine, other, bias),
        "project_qkv",
        [pltpu.VMEM((columns, width), bf16)],
        deps,
    )[0]


def multiply_kernel(turn_left, over, count, deps, *refs):
    (left_ref, right_ref), (out_ref,) = split_refs(count, deps, refs)
    left = left_ref[...].T if turn_left else left_ref[...]
    out_ref[...] = dot(left, right_ref[...], ((1,), (over,))).astype(out_ref.dtype)


def multiply(left, right, part, turn_left=False, over=0, deps=(), kind=f32):
    tokens = left.shape[1] if turn_left else left.shape[0]
    inner = left.shape[0] if turn_left else left.shape[1]
    columns = right.shape[1 - over]
    step = tokens // 2
    if turn_left:
        left_spec = pl.BlockSpec((inner, step), lambda i: (0, i + part))
    else:
        left_spec = pl.BlockSpec((step, inner), lambda i: (i + part, 0))
    return run(
        inner * columns / 3.4e5,
        functools.partial(multiply_kernel, turn_left, over),
        (1,),
        [left_spec, fixed(*right.shape)],
        [(down(step, columns), array(kind, tokens // 2, columns))],
        (left, right),
        "multiply",
        (),
        deps,
    )[0]


def fc1_kernel(count, deps, *refs):
    (mine_ref, other_ref, w_ref, bias_ref), (slope_ref, hidden_ref) = split_refs(count, deps, refs)
    rows = mine_ref.shape[0]
    factor = math.sqrt(2.0 / math.pi)
    for part, ref in enumerate((mine_ref, other_ref)):
        pre = dot(ref[...], w_ref[...], ((1,), (0,))) + bias_ref[...]
        square = pre * pre
        bent = jnp.tanh(pre * (factor + (factor * 0.044715) * square))
        share = 0.5 + 0.5 * bent
        slope = share + (0.5 * pre) * (1.0 - bent * bent) * (
            factor + (3.0 * 0.044715 * factor) * square
        )
        slope_ref[part * rows : (part + 1) * rows] = slope
        hidden_ref[part * rows : (part + 1) * rows] = (pre * share).astype(bf16)


def fc1(mine, other, weight, bias, deps=()):
    rows, width = mine.shape
    columns = weight.shape[1]
    step = 384
    return run(
        16.0,
        fc1_kernel,
        (columns // step,),
        [fixed(rows, width)] * 2 + [across(width, step), across(1, step)],
        [
            (across(2 * rows, step), array(f32, 2 * rows, columns)),
            (across(2 * rows, step), array(bf16, 2 * rows, columns)),
        ],
        (mine, other, weight, bias),
        "fc1",
        (),
        deps,
    )


def fc2_back_kernel(count, deps, *refs):
    (mine_ref, other_ref, w_ref, slope_ref), (out_ref, sums_ref) = split_refs(count, deps, refs)
    rows = mine_ref.shape[0]
    total = 0.0
    for part, ref in enumerate((mine_ref, other_ref)):
        d_hidden = dot(ref[...], w_ref[...], ((1,), (1,)))
        d_pre = (d_hidden * slope_ref[part * rows : (part + 1) * rows]).astype(bf16)
        out_ref[part * rows : (part + 1) * rows] = d_pre
        total = total + jnp.sum(d_pre.astype(f32), 0, keepdims=True)
    sums_ref[...] = total


def fc2_back(mine, other, weight, slope, deps=()):
    rows, width = mine.shape
    columns = weight.shape[0]
    step = 384
    return run(
        13.9,
        fc2_back_kernel,
        (columns // step,),
        [fixed(rows, width)] * 2 + [down(step, width), across(2 * rows, step)],
        [
            (across(2 * rows, step), array(bf16, 2 * rows, columns)),
            (across(1, step), array(f32, 1, columns)),
        ],
        (mine, other, weight, slope),
        "fc2_back",
        (),
        deps,
    )


def fc2_grad_kernel(count, deps, *refs):
    (hidden_ref, mine_ref, other_ref), (out_ref,) = split_refs(count, deps, refs)
    rows = mine_ref.shape[0]
    turned = hidden_ref[...].T
    total = dot(turned[:, :rows], mine_ref[...], ((1,), (0,)))
    total = total + dot(turned[:, rows:], other_ref[...], ((1,), (0,)))
    out_ref[...] = total.astype(bf16)


def fc2_grad(hidden, mine, other, deps=()):
    tokens, columns = hidden.shape
    rows, width = mine.shape
    step = 384
    return run(
        10.7,
        fc2_grad_kernel,
        (columns // step,),
        [across(tokens, step)] + [fixed(rows, width)] * 2,
        [(down(step, width), array(bf16, columns, width))],
        (hidden, mine, other),
        "fc2_grad",
        (),
        deps,
    )[0]


def fc1_grad_kernel(count, deps, *refs):
    (mine_ref, other_ref, right_ref), (out_ref, turned_ref) = split_refs(count, deps, refs)
    z = pl.program_id(0)
    rows = out_ref.shape[2]
    half = mine_ref.shape[0]

    @pl.when(z == 0)
    def _():
        shape = (*turned_ref.shape[:2], half)
        turned_ref[:, :, :half] = mine_ref[...].T.reshape(shape)
        turned_ref[:, :, half:] = other_ref[...].T.reshape(shape)

    total = dot(turned_ref[z], right_ref[...], ((1,), (0,))).astype(bf16)
    for k in range(4):
        out_ref[k, 0] = total[k * rows : (k + 1) * rows]


def fc1_grad(mine, other, right, nz, deps=()):
    half, width = mine.shape
    tokens, columns = right.shape
    rows = width // (4 * nz)
    return run(
        11.4,
        fc1_grad_kernel,
        (nz,),
        [fixed(half, width)] * 2 + [fixed(tokens, columns)],
        [
            (
                pl.BlockSpec((4, 1, rows, columns), lambda z: (0, z, 0, 0)),
                array(bf16, 4, nz, rows, columns),
            )
        ],
        (mine, other, right),
        "fc1_grad",
        [pltpu.VMEM((nz, 4 * rows, tokens), bf16)],
        deps,
    )[0]


def qkv_grad_kernel(count, deps, *refs):
    (mine_ref, other_ref, right_ref), (out_ref,) = split_refs(count, deps, refs)
    half = mine_ref.shape[0]
    total = dot(mine_ref[...].T, right_ref[:, :half], ((1,), (1,)))
    total = total + dot(other_ref[...].T, right_ref[:, half:], ((1,), (1,)))
    out_ref[...] = total.astype(bf16)


def qkv_grad(mine, other, right, deps=()):
    half, width = mine.shape
    columns, tokens = right.shape
    step = 384
    return run(
        8.5,
        qkv_grad_kernel,
        (width // step,),
        [across(half, step)] * 2 + [fixed(columns, tokens)],
        [(down(step, columns), array(bf16, width, columns))],
        (mine, other, right),
        "qkv_grad",
        (),
        deps,
    )[0]


def proj_back_kernel(count, deps, *refs):
    (w_ref, mixed_ref, mine_ref, other_ref), (back_ref, grad_ref) = split_refs(count, deps, refs)
    half = mine_ref.shape[0]
    back_ref[:, :half] = dot(w_ref[...], mine_ref[...], ((1,), (1,))).astype(bf16)
    back_ref[:, half:] = dot(w_ref[...], other_ref[...], ((1,), (1,))).astype(bf16)
    total = dot(mixed_ref[:, :half], mine_ref[...], ((1,), (0,)))
    total = total + dot(mixed_ref[:, half:], other_ref[...], ((1,), (0,)))
    grad_ref[...] = total.astype(bf16)


def proj_back(weight, mixed, mine, other, deps=()):
    inner, tokens = mixed.shape
    half, width = mine.shape
    step = inner // 2
    return run(
        6.4,
        proj_back_kernel,
        (2,),
        [down(step, width), down(step, tokens)] + [fixed(half, width)] * 2,
        [
            (down(step, tokens), array(bf16, inner, tokens)),
            (down(step, width), array(bf16, inner, width)),
        ],
        (weight, mixed, mine, other),
        "proj_back",
        (),
        deps,
    )


def lane_sums_kernel(count, deps, *refs):
    (value_ref,), (out_ref,) = split_refs(count, deps, refs)
    out_ref[...] = jnp.sum(value_ref[...].astype(f32), 1, keepdims=True)


def lane_sums(value, deps=()):
    rows, width = value.shape
    return run(
        3.4,
        lane_sums_kernel,
        (1,),
        [fixed(rows, width)],
        [(fixed(rows, 1), array(f32, rows, 1))],
        (value,),
        "lane_sums",
        (),
        deps,
    )[0]


def sum_blocks_kernel(count, deps, *refs):
    ins, (out_ref,) = split_refs(count, deps, refs)
    out_ref[...] = sum((ref[...].astype(f32) for ref in ins[1:]), ins[0][...].astype(f32))


def sum_blocks(mine, got, deps=()):
    shape = mine.shape
    return run(
        3.0,
        sum_blocks_kernel,
        (1,),
        [fixed(*shape)] * (1 + len(got)),
        [(fixed(*shape), array(f32, *shape))],
        (mine, *got),
        "sum_blocks",
        (),
        deps,
    )[0]


ROWS = 128


def middle_kernel(count, deps, *refs):
    (vec_ref, mine_ref, got_ref, x_ref), (attn_ref, mid_ref, mlp_ref) = split_refs(
        count, deps, refs
    )
    attn = mine_ref[...] + got_ref[...].astype(f32) + vec_ref[6:7]
    mid = x_ref[...] + vec_ref[2:3] * attn
    normed, _ = normalize(mid)
    attn_ref[...] = attn
    mid_ref[...] = mid
    mlp_ref[...] = (normed * (1.0 + vec_ref[4:5]) + vec_ref[3:4]).astype(bf16)


def middle(vec, mine, got, x_in, deps=()):
    rows, width = mine.shape
    block = down(ROWS, width)
    return run(
        6.2,
        middle_kernel,
        (rows // ROWS,),
        [fixed(8, width)] + [block] * 3,
        [
            (block, array(f32, rows, width)),
            (block, array(f32, rows, width)),
            (block, array(bf16, rows, width)),
        ],
        (vec, mine, got, x_in),
        "middle",
        (),
        deps,
    )


def add_sums(sums_ref, values):
    @pl.when(pl.program_id(0) == 0)
    def _():
        sums_ref[...] = jnp.zeros_like(sums_ref)

    for number, value in enumerate(values):
        sums_ref[number : number + 1] += jnp.sum(value, 0, keepdims=True)


def valid_cotangent(valid_ref, cot_ref):
    row = pl.program_id(0) * ROWS + lax.broadcasted_iota(jnp.int32, (ROWS, 1), 0)
    return jnp.where(row < valid_ref[0], cot_ref[...].astype(f32), 0.0)


def middle_back_kernel(count, deps, *refs):
    (valid_ref, vec_ref, mine_ref, got_ref, cot_ref, mid_ref, attn_ref), (
        d_mid_ref,
        d_attn_ref,
        sums_ref,
    ) = split_refs(count, deps, refs)
    d_mlp = mine_ref[...] + got_ref[...].astype(f32)
    normed, spread = normalize(mid_ref[...])
    d_mid = valid_cotangent(valid_ref, cot_ref) + norm_back(
        normed, spread, d_mlp * (1.0 + vec_ref[4:5])
    )
    d_attn = (vec_ref[2:3] * d_mid).astype(bf16)
    d_mid_ref[...] = d_mid
    d_attn_ref[...] = d_attn
    add_sums(sums_ref, (d_mlp, d_mlp * normed, d_mid * attn_ref[...], d_attn.astype(f32)))


def middle_back(valid, vec, mine, got, cot, mid, attn, deps=()):
    rows, width = mine.shape
    block = down(ROWS, width)
    return run(
        7.5,
        middle_back_kernel,
        (rows // ROWS,),
        [pl.BlockSpec(memory_space=pltpu.SMEM), fixed(8, width)] + [block] * 5,
        [
            (block, array(f32, rows, width)),
            (block, array(bf16, rows, width)),
            (fixed(8, width), array(f32, 8, width)),
        ],
        (valid, vec, mine, got, cot, mid, attn),
        "middle_back",
        (),
        deps,
    )


def finish_first_kernel(count, deps, *refs):
    (vec_ref, mine_ref, got_ref, d_mid_ref, x_ref), (grad_ref, sums_ref) = split_refs(
        count, deps, refs
    )
    d_attn_in = mine_ref[...] + got_ref[...].astype(f32)
    normed, spread = normalize(x_ref[...])
    grad_ref[...] = (
        d_mid_ref[...] + norm_back(normed, spread, d_attn_in * (1.0 + vec_ref[1:2]))
    ).astype(bf16)
    add_sums(sums_ref, (d_attn_in, d_attn_in * normed))


def finish_first(vec, mine, got, d_mid, x_in, deps=()):
    rows, width = mine.shape
    block = down(ROWS, width)
    return run(
        6.2,
        finish_first_kernel,
        (rows // ROWS,),
        [fixed(8, width)] + [block] * 4,
        [
            (block, array(bf16, rows, width)),
            (fixed(8, width), array(f32, 8, width)),
        ],
        (vec, mine, got, d_mid, x_in),
        "finish_first",
        (),
        deps,
    )


def finish_last_kernel(count, deps, *refs):
    (valid_ref, vec_ref, mine_ref, got_ref, cot_ref, mid_ref), (out_ref, sums_ref) = split_refs(
        count, deps, refs
    )
    branch = mine_ref[...] + got_ref[...].astype(f32) + vec_ref[7:8]
    out_ref[...] = (mid_ref[...] + vec_ref[5:6] * branch).astype(bf16)
    add_sums(sums_ref, (valid_cotangent(valid_ref, cot_ref) * branch,))


def finish_last(valid, vec, mine, got, cot, mid, deps=()):
    rows, width = mine.shape
    block = down(ROWS, width)
    return run(
        5.3,
        finish_last_kernel,
        (rows // ROWS,),
        [pl.BlockSpec(memory_space=pltpu.SMEM), fixed(8, width)] + [block] * 4,
        [
            (block, array(bf16, rows, width)),
            (fixed(8, width), array(f32, 8, width)),
        ],
        (valid, vec, mine, got, cot, mid),
        "finish_last",
        (),
        deps,
    )


def adam_kernel(layout, rate, scalar_ref, *refs):
    grads, (w_ref, m_ref, v_ref), (new_w, new_m, new_v) = refs[:-6], refs[-6:-3], refs[-3:]
    factor = scalar_ref[0]
    column = 0
    if layout is None:
        pieces = [(0, 0, w_ref.shape[1])]
    else:
        pieces = layout
    swap = scalar_ref[1] > 0.5
    for part, first, width in pieces:
        if layout is None:
            grad = grads[0][...].astype(f32)
        else:
            here = slice(first, first + width)
            grad = jnp.where(
                swap, grads[1 - part][:, here].astype(f32), grads[part][:, here].astype(f32)
            )
        place = (slice(None), slice(column, column + width))
        weight, moment, second = adam_step(
            w_ref[place], m_ref[place], v_ref[place], grad, factor, rate
        )
        new_w[place], new_m[place], new_v[place] = weight, moment, second
        column += width


def adam(weight, first, second, grads, scalars, rate, layout=None):
    inside = pl.BlockSpec(memory_space=pltpu.VMEM)
    shape = jax.ShapeDtypeStruct(weight.shape, f32)
    return pl.pallas_call(
        functools.partial(adam_kernel, layout, rate),
        in_specs=[pl.BlockSpec(memory_space=pltpu.SMEM)] + [inside] * (len(grads) + 3),
        out_specs=[inside] * 3,
        out_shape=[shape] * 3,
        compiler_params=pltpu.CompilerParams(vmem_limit_bytes=VMEM_LIMIT),
        cost_estimate=cost(4.0),
        name="adam",
    )(scalars, *grads, weight, first, second)


def after_kernel(value_ref, *refs):
    refs[-1][...] = value_ref[...]


def after(value, *deps):
    flat = value.reshape(-1, value.shape[-1])
    return pl.pallas_call(
        after_kernel,
        in_specs=[pl.BlockSpec(memory_space=pltpu.VMEM)]
        + [pl.BlockSpec(memory_space=pl.ANY)] * len(deps),
        out_specs=pl.BlockSpec(memory_space=pltpu.VMEM),
        out_shape=jax.ShapeDtypeStruct(flat.shape, flat.dtype),
        compiler_params=pltpu.CompilerParams(vmem_limit_bytes=VMEM_LIMIT),
        cost_estimate=cost(1.5),
        name="after",
    )(flat, *deps).reshape(value.shape)


class Group:
    def __init__(self, n):
        self.n = n
        self.nz = n // 8
        self.me = lax.axis_index(AXES).astype(jnp.int32)
        self.y = self.me & 1
        self.c = (self.me >> 1) & 1
        self.x = (self.me >> 2) & 1
        self.z = self.me >> 3
        self.where = jnp.stack([self.z, self.x, self.y])

    def xor(self, value, mask):
        return lax.ppermute(value, AXES, [(i, i ^ mask) for i in range(self.n)])

    def core(self, value):
        return self.xor(value, 2)

    def turn(self, value):
        got = lax.ppermute(
            value,
            AXES,
            [(i, i ^ 3) for i in range(self.n) if (i & 3) in (1, 2)],
        )
        return jnp.where(self.c == self.y, value, got)

    def turn_other(self, value):
        return lax.ppermute(
            value,
            AXES,
            [(i, (i & ~3) | ((1 - (i & 1)) << 1) | ((i >> 1) & 1)) for i in range(self.n)],
        )

    def turn_other_back(self, value):
        return lax.ppermute(
            value,
            AXES,
            [(i, (i & ~3) | ((i & 1) << 1) | (1 - ((i >> 1) & 1))) for i in range(self.n)],
        )

    def to_block(self, parts):
        mine = lax.dynamic_index_in_dim(parts, self.y, 0, False)
        other = lax.dynamic_index_in_dim(parts, 1 - self.y, 0, False)
        got_a, got_b = self.turn(mine), self.turn_other(other)
        straight = self.c == 0
        return jnp.concatenate(
            [jnp.where(straight, got_a, got_b), jnp.where(straight, got_b, got_a)], 0
        )

    def from_block(self, block):
        rows = block.shape[0] // 2
        pieces = block.reshape(2, rows, block.shape[1])
        got_a = self.turn(lax.dynamic_index_in_dim(pieces, self.c, 0, False))
        got_b = self.turn_other_back(lax.dynamic_index_in_dim(pieces, 1 - self.c, 0, False))
        return got_a, got_b

    def gather_z(self, block):
        return [block] + [self.xor(block, d << 3) for d in range(1, self.nz)]

    def gather_near(self, pieces, deps=()):
        half = self.nz // 2
        plans = [
            [(k, (), (k,)) for k in range(half)],
            [(half + k, (), (k,)) for k in range(half)],
        ]
        shape = (half, *pieces[0].shape)
        low, high = move(self.where, pieces, [shape] * 2, plans, deps, "stack_z")
        return low, high, self.xor(low, 1), self.xor(high, 4)

    def gather_far(self, near, deps=()):
        half = self.nz // 2
        low, high, low_y, high_x = near
        plans = [[(0, (), (0,)), (2, (), (1,))], [(1, (), (0,)), (3, (), (1,))]]
        shape = (2, *low.shape)
        low_2, high_2 = move(self.where, near, [shape] * 2, plans, deps, "stack_near")
        return low_2, high_2, self.xor(low_2, 4), self.xor(high_2, 1)

    def gather_end(self, far, deps=(), cuts=((),), shapes=None, order="zxy"):
        nz, half = self.nz, self.nz // 2
        plans = []
        for cut in cuts:
            plan = []
            for k in range(half):
                for other in range(2):
                    for piece, target in (
                        (0, (("z", k), ("x", 0), ("y", other))),
                        (1, (("z", half + k), ("x", other), ("y", 0))),
                        (2, (("z", k), ("x", 1), ("y", other))),
                        (3, (("z", half + k), ("x", other), ("y", 1))),
                    ):
                        target = tuple(dict((t[0], t) for t in target)[axis] for axis in order)
                        plan.append((piece, (other, k, *cut), target))
            plans.append(plan)
        lead = tuple({"z": nz}.get(axis, 2) for axis in order)
        shapes = [(*lead, *shape) for shape in shapes or [far[0].shape[2:]]]
        return move(self.where, far, shapes, plans, deps, "place")

    def scatter_z(self, blocks, deps=()):
        nz = self.nz
        plans = [[(0, (("z", d),), ())] for d in range(nz)]
        parts = move(self.where, [blocks], [blocks.shape[1:]] * nz, plans, deps, "split_z")
        return parts, [self.xor(parts[d], d << 3) for d in range(1, nz)]

    def sum_z(self, state):
        parts, got = state
        return sum((item.astype(f32) for item in got), parts[0].astype(f32))

    def scatter_start(self, grads, deps=()):
        half = self.nz // 2
        plans = [[], []]
        for k in range(half):
            for other in range(2):
                for piece, cut in ((0, pl.ds(0, 3)), (1, 3)):
                    plans[0].append((piece, (k, ("x", 1), other), (k, other, cut)))
                    plans[1].append((piece, (half + k, other, ("y", 1)), (k, other, cut)))
        shape = (half, 2, 4, *grads[1].shape[3:])
        to_x, to_y = move(self.where, grads, [shape] * 2, plans, deps, "split")
        return grads, self.xor(to_x, 4), self.xor(to_y, 1), to_x

    def scatter_near(self, state, deps=()):
        grads, got_x, got_y = state[:3]
        send_y, send_x, own = add_near(self.where, *grads, got_x, got_y, deps)
        return own, self.xor(send_y, 1), self.xor(send_x, 4)

    def scatter_far(self, state, deps=()):
        sends, mine = add_far(self.where, *state, deps)
        return mine, [self.xor(sends[d - 1], d << 3) for d in range(1, self.nz)]

    def scatter_end(self, state):
        mine, got = state
        return sum((item.astype(f32) for item in got), mine)

    def all_sum(self, value):
        value = value + self.core(value)
        value = value + self.xor(value, 1)
        value = value + self.xor(value, 4)
        return sum((self.xor(value, d << 3) for d in range(1, self.nz)), value)


def per_device(
    tokens,
    embedding,
    heights,
    widths,
    cotangent,
    w_qkv,
    w_proj,
    w_fc1,
    w_fc2,
    w_ada,
    biases,
    m_qkv,
    m_proj,
    m_fc1,
    m_fc2,
    m_ada,
    m_bias,
    v_qkv,
    v_proj,
    v_fc1,
    v_fc2,
    v_ada,
    v_bias,
):
    rows = tokens.shape[1]
    n = math.prod(lax.axis_size(axis) for axis in AXES)
    own_rows = w_qkv.shape[0]
    g = Group(n)
    nz = g.nz
    groups = n // 4
    pair = 2 * own_rows
    ff_rows = w_fc2.shape[0]
    bias_rows = biases.shape[0]

    qkv_parts = (
        w_qkv.astype(bf16)
        .reshape(own_rows, 3, 2, HALF, 2, HEAD_DIM)
        .transpose(4, 0, 2, 1, 3, 5)
        .reshape(2, own_rows, QKV)
    )
    third = own_rows * D // QKV
    qp_block = jnp.concatenate(
        [g.to_block(qkv_parts), w_proj.astype(bf16).reshape(third, QKV)], 0
    ).reshape(4, third, QKV)
    qp_z = g.gather_z(qp_block)
    tokens_here = g.turn(after(tokens[0], qp_block))
    cotangent_here = g.turn(after(cotangent[0], tokens_here))
    cond_row = jax.nn.silu(embedding[0]).astype(bf16).reshape(groups * 2, 2, own_rows)
    cond_row = lax.dynamic_index_in_dim(cond_row, g.y, 1, False)
    small = jnp.concatenate([biases.astype(bf16), heights.astype(bf16), widths.astype(bf16)])
    small = jnp.concatenate(
        [cond_row, jnp.broadcast_to(small[None], (groups * 2, bias_rows + 2))], 1
    )
    small = jnp.pad(small, ((0, 0), (0, -small.shape[1] % 128)))
    small = lax.all_to_all(small, ("z", "x", "core"), 0, 0, tiled=True)
    conds_own = small[:, :own_rows]
    small_other = g.xor(small, 1)
    low = g.y == 0
    natural = jnp.stack(
        [jnp.where(low, small, small_other), jnp.where(low, small_other, small)], 1
    ).reshape(n, -1)[:, own_rows:].astype(f32)
    mod_part = dot(conds_own, w_ada.astype(bf16), ((1,), (0,)))
    mod_sum = jnp.sum(
        lax.all_to_all(mod_part, ("z", "x", "y"), 0, 0, tiled=True), 0, keepdims=True
    )
    mod_sum = mod_sum + g.core(mod_sum)
    qp_near = g.gather_near(qp_z, [tokens_here, mod_sum])
    fc1_parts = (
        w_fc1.astype(bf16)
        .reshape(own_rows, nz, 2, 2, 2, ff_rows)
        .transpose(3, 0, 2, 4, 1, 5)
        .reshape(2, own_rows, OWN_FF)
    )
    fc1_block = g.to_block(after(fc1_parts, qp_block))
    ff_block = jnp.concatenate(
        [
            fc1_block.reshape(2 * own_rows, 2, D).swapaxes(0, 1).reshape(-1, D),
            w_fc2.astype(bf16),
        ]
    )
    ff_all = lax.all_gather(after(ff_block, qp_near[0]), ("x", "y", "z"), axis=0, tiled=True)
    ff_all = ff_all.reshape(2, 2, nz, 4, 2 * own_rows, D)
    qp_far = g.gather_far(qp_near)
    bias_full = natural[:, :bias_rows].reshape(-1)
    bias_qkv = bias_full[: 3 * D]
    bias_proj = bias_full[3 * D : 4 * D]
    bias_fc1 = bias_full[4 * D : 4 * D + FF]
    bias_fc2 = bias_full[4 * D + FF : 5 * D + FF]
    bias_ada = bias_full[5 * D + FF :]
    image_row = lax.dynamic_index_in_dim(natural, (g.me & ~3) | (g.y << 1), 0, True)
    image_row = after(image_row, qp_far[0])[0]
    height = image_row[bias_rows].astype(jnp.int32)
    width = image_row[bias_rows + 1].astype(jnp.int32)
    modul = mod_sum + bias_ada
    shift1, scale1, gate1, shift2, scale2, gate2 = [
        modul[:, j * D : (j + 1) * D] for j in range(6)
    ]

    vec = jnp.concatenate([modul.reshape(6, D), bias_proj[None], bias_fc2[None]])

    slots = g.c * rows + jnp.arange(rows, dtype=jnp.int32)
    count = height * width
    valid_rows = (slots < count).astype(f32)[:, None]
    seq = 2 * rows
    cut = jnp.where(count < seq, -1e30, 0.0).astype(f32)
    mask = jnp.stack([jnp.where(g.c == 1, cut, 0.0), jnp.where(g.c == 0, cut, 0.0)])
    valid = jnp.clip(count - g.c * rows, 0, rows).astype(jnp.int32)[None]
    x_in = tokens_here.astype(f32) + position_rows(slots, width)
    normed1, spread1 = normalize(x_in)
    attn_in = (normed1 * (1.0 + scale1) + shift1).astype(bf16)
    d_out = cotangent_here.astype(f32) * valid_rows
    d_branch = (gate2 * d_out).astype(bf16)
    gb_fc2 = jnp.sum(d_branch.astype(f32), 0, keepdims=True)
    attn_sib = g.core(attn_in)
    qkv_w = g.gather_end(qp_far, [attn_in], ((pl.ds(0, 3),),), ((3, third, QKV),))[0]
    qkv_w = qkv_w.reshape(D, QKV)
    own_bias_qkv = lax.dynamic_index_in_dim(
        bias_qkv.reshape(3, 2, HALF, 2, HEAD_DIM), g.c, 3, False
    ).swapaxes(0, 1).reshape(-1, 1)
    qkv = project_qkv(qkv_w, attn_in, attn_sib, own_bias_qkv)
    qkv = qkv.reshape(2, 3, HALF, HEAD_DIM, seq)
    first = attend(0, qkv, mask)
    proj_own = g.gather_end(qp_far, first[1:], ((3,),), ((third, QKV),))[0].reshape(-1, D)
    heads_match = pair % HEAD_DIM == 0
    if heads_match:
        proj_w = proj_own
    else:
        mine = proj_own.reshape(groups, pair, D)
        theirs = g.core(mine)
        own_first = g.c == 0
        whole = jnp.stack(
            [jnp.where(own_first, mine, theirs), jnp.where(own_first, theirs, mine)], 1
        ).reshape(OWN_HEADS, 2, HEAD_DIM, D)
        proj_w = lax.dynamic_index_in_dim(whole, g.c, 1, False).reshape(OWN_HEADS * HEAD_DIM, D)
    mixed, logsum = attend(1, qkv, mask, first, [proj_w])
    mixed = mixed.reshape(OWN_HEADS * HEAD_DIM, seq)
    attn_got = g.core(dot(mixed[:, rows:], proj_w, ((0,), (0,))).astype(bf16))
    attn_mine = dot(mixed[:, :rows], proj_w, ((0,), (0,)))
    attn, x_mid, mlp_in = middle(vec, attn_mine, attn_got, x_in)
    mlp_got = g.core(mlp_in)
    own_bias_fc1 = lax.dynamic_index_in_dim(
        bias_fc1.reshape(nz, 2, 2, 2, ff_rows), g.c, 2, False
    ).transpose(1, 2, 0, 3).reshape(-1)
    plan = [
        (0, (x, y, z, h), (z, x, y, slice(None), pl.ds(h * D, D)))
        for x in range(2)
        for y in range(2)
        for z in range(nz)
        for h in range(2)
    ]
    fc1_w = move(
        g.where, [ff_all], [(nz, 2, 2, 2 * own_rows, OWN_FF)], [plan], [mlp_in], "place_fc1"
    )[0].reshape(D, OWN_FF)
    slope, hidden = fc1(mlp_in, mlp_got, fc1_w, own_bias_fc1[None])
    branch_got = g.core(d_branch)
    g_fc2 = fc2_grad(hidden, d_branch, branch_got)
    red_fc2 = lax.psum_scatter(g_fc2, ("x", "y"), scatter_dimension=0, tiled=True)
    plan = [
        (0, (x, y, z, pl.ds(2, 2)), (x, y, z)) for x in range(2) for y in range(2) for z in range(nz)
    ]
    fc2_w = move(
        g.where, [ff_all], [(2, 2, nz, 2, 2 * own_rows, D)], [plan], [g_fc2], "place_fc2"
    )[0].reshape(OWN_FF, D)
    d_pre, gb_fc1 = fc2_back(d_branch, branch_got, fc2_w, slope, [g_fc2])
    d_mlp_got = g.core(dot(d_pre[rows:], fc1_w, ((1,), (1,))).astype(bf16))
    d_mlp_mine = dot(d_pre[:rows], fc1_w, ((1,), (1,)))
    g_fc1 = fc1_grad(mlp_in, mlp_got, d_pre, nz, [d_mlp_mine]).reshape(D, OWN_FF)
    red_fc1 = lax.psum_scatter(g_fc1, ("x", "y"), scatter_dimension=0, tiled=True)
    d_mid, d_attn, middle_sums = middle_back(
        valid, vec, d_mlp_mine, d_mlp_got, cotangent_here, x_mid, attn
    )
    d_attn_got = g.core(d_attn)
    d_mixed, g_proj = proj_back(proj_w, mixed, d_attn, d_attn_got)
    if heads_match:
        g_proj = g_proj.reshape(nz, 2, 2, third, QKV)
    else:
        own = (jnp.arange(2) == g.c)[None, :, None, None]
        whole = jnp.where(own, g_proj.reshape(OWN_HEADS, 1, HEAD_DIM, D), 0).reshape(
            groups, 2, pair, D
        )
        theirs = g.core(lax.dynamic_index_in_dim(whole, 1 - g.c, 1, False))
        mine = lax.dynamic_index_in_dim(whole, g.c, 1, False)
        g_proj = (mine.astype(f32) + theirs.astype(f32)).astype(bf16).reshape(nz, 2, 2, third, QKV)
    d_mixed = d_mixed.reshape(OWN_HEADS, HEAD_DIM, seq)
    d_qkv = attend_back(0, qkv, logsum, d_mixed, mask, (), [g_proj])
    fc2_state = g.scatter_z(red_fc2.reshape(nz, -1, D), [d_qkv])
    d_qkv = attend_back(1, qkv, logsum, d_mixed, mask, [d_qkv], [fc2_state[0][0]])
    d_qkv = d_qkv.reshape(QKV, seq)
    g_qkv = qkv_grad(attn_in, attn_sib, d_qkv)
    red_fc2 = sum_blocks(fc2_state[0][0], fc2_state[1], [g_qkv])
    qkv_state = g.scatter_start([g_qkv.reshape(nz, 2, 2, 3, third, QKV), g_proj], [red_fc2])
    red_fc1 = lax.psum_scatter(
        after(red_fc1, qkv_state[3]), "z", scatter_dimension=0, tiled=True
    )
    d_attn_in = multiply(d_qkv, qkv_w, 1, True, 1, [qkv_state[3]], bf16)
    d_attn_in_got = g.core(d_attn_in)
    d_attn_in = multiply(d_qkv, qkv_w, 0, True, 1, [d_attn_in])
    gb_qkv = lane_sums(d_qkv, [d_attn_in])
    grad_tokens, first_sums = finish_first(
        vec, d_attn_in, d_attn_in_got, d_mid, x_in, [gb_qkv]
    )
    qkv_state = g.scatter_near(qkv_state, [first_sums, red_fc1])
    branch = multiply(hidden, fc2_w, 1, deps=[qkv_state[0]], kind=bf16)
    branch_got = g.core(branch)
    branch = multiply(hidden, fc2_w, 0, deps=[branch])
    qkv_state = g.scatter_far(qkv_state, [branch])
    output, last_sums = finish_last(
        valid, vec, branch, branch_got, cotangent_here, x_mid, [qkv_state[0]]
    )
    grad_tokens = g.turn(after(grad_tokens, qkv_state[0]))[None]
    red_qp = sum_blocks(qkv_state[0], qkv_state[1], [last_sums, grad_tokens])
    fc1_parts = g.from_block(after(red_fc1, red_qp))

    own = (jnp.arange(2) == g.c)[None, :, None]
    gb_qkv = gb_qkv.reshape(2, 3, HALF, HEAD_DIM).swapaxes(0, 1)
    gb_qkv = jnp.where(own, gb_qkv.reshape(3 * OWN_HEADS, 1, HEAD_DIM), 0.0).reshape(3, D)
    gb_fc1 = gb_fc1.reshape(2, 2, nz, ff_rows).transpose(2, 0, 1, 3)
    gb_fc1 = jnp.where(own, gb_fc1.reshape(groups, 1, 2 * ff_rows), 0.0).reshape(-1, D)
    vector = jnp.concatenate(
        [
            gb_qkv,
            middle_sums[3:4],
            gb_fc1,
            gb_fc2,
            first_sums[:2],
            middle_sums[2:3],
            middle_sums[:2],
            last_sums[:1],
        ]
    )
    vector = after(vector, red_qp)
    vector = vector + g.core(vector)
    plain = vector.shape[0] - 6
    others = [g.xor(vector, d << 3) for d in range(1, nz)]
    sums = sum((item[:plain] for item in others), vector[:plain])
    mods = jnp.stack([vector[plain:]] + [item[plain:] for item in others])[:, None]
    for bit in (1, 4):
        packed = jnp.concatenate([sums, mods.reshape(-1, D)])
        packed = g.xor(packed, bit)
        sums = sums + packed[:plain]
        mods = jnp.stack([mods, packed[plain:].reshape(mods.shape)], 1)
    mods = mods.reshape(groups * 2, 6 * D)
    place_of = (g.z * 2 + g.x) * 2 + g.y
    order = jnp.arange(groups * 2)[None, :] == (jnp.arange(groups * 2)[:, None] ^ place_of)
    conds_own = dot(order.astype(bf16), conds_own, ((1,), (0,)))
    red_ada = lax.dot_general(
        conds_own.astype(f32),
        mods,
        (((0,), (0,)), ((), ())),
        precision=lax.Precision.HIGHEST,
        preferred_element_type=f32,
    )
    g_bias = jnp.concatenate([sums.reshape(-1), jnp.sum(mods, 0)])
    red_bias = lax.dynamic_slice_in_dim(g_bias, g.me * bias_rows, bias_rows)

    red_qkv = red_qp[:3].reshape(2 * own_rows, QKV)
    red_proj = red_qp[3].reshape(own_rows, D)
    output = g.turn(after(output, sums))[None]
    squares = sum(
        (
            jnp.sum(jnp.square(piece.astype(f32)))
            for piece in (red_qp, red_fc1, red_fc2, red_ada, red_bias)
        )
    )
    squares = g.all_sum(jnp.broadcast_to(squares, (1, 128)))[0, 0]
    red_qkv = g.from_block(red_qkv)
    grad_norm = jnp.sqrt(squares)
    factor = jnp.minimum(1.0, clip_limit / grad_norm)
    scalars = jnp.stack([factor, g.y.astype(f32)])
    piece = HALF * HEAD_DIM
    qkv_layout = [
        (c, (hh * 3 + kind) * piece + head * HEAD_DIM, HEAD_DIM)
        for kind in range(3)
        for hh in range(2)
        for head in range(HALF)
        for c in range(2)
    ]
    fc1_layout = [
        (c, ((x * 2 + y) * nz + z) * ff_rows, ff_rows)
        for z in range(nz)
        for x in range(2)
        for c in range(2)
        for y in range(2)
    ]
    results = [
        adam(w_qkv, m_qkv, v_qkv, red_qkv, scalars, learn_rate, qkv_layout),
        adam(w_proj, m_proj, v_proj, [red_proj], scalars, learn_rate),
        adam(w_fc1, m_fc1, v_fc1, fc1_parts, scalars, learn_rate, fc1_layout),
        adam(w_fc2, m_fc2, v_fc2, [red_fc2], scalars, learn_rate),
        adam(w_ada, m_ada, v_ada, [red_ada], scalars, learn_rate),
        adam_step(biases, m_bias, v_bias, red_bias, factor, bias_rate),
    ]
    return (
        output,
        grad_tokens,
        grad_norm,
        *[item[0] for item in results],
        *[item[1] for item in results],
        *[item[2] for item in results],
    )


def solution(mesh):
    count = mesh.devices.size
    fine = jax.sharding.Mesh(mesh.devices.reshape(count // 8, 2, 2, 2), AXES)
    image = ("z", "x", "core")
    patches = P(image, "y", None)
    state = (P(AXES, None),) * 5 + (P(AXES),)
    return jax.shard_map(
        per_device,
        mesh=fine,
        in_specs=(patches, P(image, None), P(image), P(image), patches, *state, *state, *state),
        out_specs=(patches, patches, P(), *state, *state, *state),
        check_vma=False,
    )
```
